32 devices in a mesh: dp: 8 (over y, x, core), sp: 4 (over z).
Axes of the slice: x: 2, y: 2, z: 4, core: 2. Of those that a mesh axis runs over, the one named last changes fastest.
Arguments:
- features: bfloat16 [8, 512, 1024], P('dp', 'sp'), may hold values from -6 to 6
- logit_grad: bfloat16 [8, 512, 32], P('dp', 'sp'), may hold values from -6 to 6
- segment_ids: int32 [8, 512], P('dp'), may hold values from 0 to 2, as said below
- conv_weight: bfloat16 [1024, 64, 128], P('sp'), may hold values from -0.0625 to 0.0625
- conv_bias: float32 [1024], P('sp'), may hold values from -3 to 3
- w_qkv: bfloat16 [1024, 3, 1024], P(None, None, 'sp'), may hold values from -0.1875 to 0.1875
- qv_bias: float32 [2, 1024], P(None, 'sp'), may hold values from -3 to 3
- w_out: bfloat16 [1024, 1024], P('sp'), may hold values from -0.75 to 0.75
- w_up: bfloat16 [1024, 4096], P(None, 'sp'), may hold values from -0.1875 to 0.1875
- ffn_bias: float32 [4096], P('sp'), may hold values from -3 to 3
- w_down: bfloat16 [4096, 1024], P('sp'), may hold values from -0.09375 to 0.09375
- out_biases: float32 [2, 1024], replicated, may hold values from -2 to 2
- gains: float32 [3, 1024], replicated, may hold values from 0.5 to 1.5
- shifts: float32 [3, 1024], replicated, may hold values from -2 to 2
- ctc_weight: bfloat16 [1024, 32], replicated, may hold values from -0.1875 to 0.1875
- ctc_bias: float32 [32], replicated, may hold values from -3 to 3
Outputs:
- logits: float32 [8, 512, 32], P('dp', 'sp')
- feature_grad: float32 [8, 512, 1024], P('dp', 'sp')
- conv_weight_grad: float32 [1024, 64, 128], P('sp')
- conv_bias_grad: float32 [1024], P('sp')
- qkv_grad: float32 [1024, 3, 1024], P(None, None, 'sp')
- qv_bias_grad: float32 [2, 1024], P(None, 'sp')
- out_grad: float32 [1024, 1024], P('sp')
- up_grad: float32 [1024, 4096], P(None, 'sp')
- ffn_bias_grad: float32 [4096], P('sp')
- down_grad: float32 [4096, 1024], P('sp')
- out_biases_grad: float32 [2, 1024], replicated
- gains_grad: float32 [3, 1024], P(None, 'sp')
- shifts_grad: float32 [3, 1024], P(None, 'sp')
- ctc_weight_grad: float32 [1024, 32], P('sp')
- ctc_bias_grad: float32 [32], P('sp')
The draws below stay inside these ranges and needn't reach their ends.
Inputs may be any that keep to these rules, and one draw needn't show every extreme that they name: `segment_ids`: each row holds three utterances numbered 0, 1, 2 in frame order; the first and the last have 1 to 64 frames each, so the middle one starts among the frames of the first index of sp and ends among those of the last.
All inputs are finite; a program needn't handle non-finite values.
Results may differ from the reference program's by a relative error of at most 0.02.
Values may be sent and summed in bfloat16 or wider, within the bound.
No kernel may reach another device: no remote copies, remote signals or barrier semaphores. Data moves between devices by JAX's collectives and lax.ppermute only.
A program may use at most 192 MiB of HBM per device.

```python
import jax
import jax.numpy as jnp
from jax import lax

D = 1024
H = 16
HD = 64
FF = 4096
G = 16
CG = 64
KW = 128
V = 32
F = 128
LENGTH = 512
ROWS = 8


def draw_segment_ids(key, part):
    key = jax.random.fold_in(key, 11)
    lead_key, tail_key = jax.random.split(key)
    upper_end = F - KW // 2 + 1
    leading = jax.random.randint(lead_key, (ROWS, 1), 1, upper_end)
    trailing = jax.random.randint(tail_key, (ROWS, 1), 1, upper_end)
    position = jnp.arange(LENGTH, dtype=jnp.int32)[None, :]
    return (position >= leading).astype(jnp.int32) + (position >= LENGTH - trailing).astype(jnp.int32)


def block_scale(own_key, extent, cuts, low, largest):
    loudness = 1.0
    for axis_at, blocks in cuts:
        heights = jax.random.uniform(jax.random.fold_in(jax.random.fold_in(own_key, 6), axis_at), (blocks,), jnp.float32, low / len(cuts), largest / len(cuts))
        loudness = loudness * jnp.repeat(jnp.exp(heights), extent[axis_at] // blocks).reshape((-1,) + (1,) * (len(extent) - 1 - axis_at))
    return loudness


def bell_draw(rng, dims, deviation, most, cuts=(), kind=jnp.bfloat16):
    array = deviation * jax.random.normal(rng, dims, jnp.float32)
    if cuts:
        array = array * block_scale(rng, dims, cuts, -0.22, 0.18)
    return jnp.clip(array, -most, most).astype(kind)


def setup_inputs(seed: int = 0) -> dict:
    key_list = jax.random.split(jax.random.key(seed), 17)
    features = bell_draw(key_list[0], (ROWS, LENGTH, D), 1.0, 6.0, ((0, 8), (1, 4)))
    logit_grad = bell_draw(key_list[1], (ROWS, LENGTH, V), 1.0, 6.0, ((0, 8), (1, 4)))
    segment_ids = draw_segment_ids(jax.random.fold_in(key_list[16], 71), 0)
    conv_weight = bell_draw(key_list[3], (D, CG, KW), (CG * KW) ** -0.5, 0.0625, ((0, 4),))
    conv_bias = bell_draw(key_list[4], (D,), 0.5, 3.0, ((0, 4),), jnp.float32)
    w_qkv = bell_draw(key_list[5], (D, 3, D), D ** -0.5, 0.1875, ((2, 4),))
    qv_bias = bell_draw(key_list[6], (2, D), 0.5, 3.0, ((1, 4),), jnp.float32)
    w_out = bell_draw(key_list[7], (D, D), (D // 16) ** -0.5, 0.75, ((0, 4),))
    w_up = bell_draw(key_list[8], (D, FF), D ** -0.5, 0.1875, ((1, 4),))
    ffn_bias = bell_draw(key_list[9], (FF,), 0.5, 3.0, ((0, 4),), jnp.float32)
    w_down = bell_draw(key_list[10], (FF, D), FF ** -0.5, 0.09375, ((0, 4),))
    out_biases = bell_draw(key_list[11], (2, D), 0.3, 2.0, (), jnp.float32)
    gains = jnp.clip(1.0 + 0.1 * jax.random.normal(key_list[12], (3, D), jnp.float32), 0.5, 1.5)
    shifts = bell_draw(key_list[13], (3, D), 0.3, 2.0, (), jnp.float32)
    ctc_weight = bell_draw(key_list[14], (D, V), D ** -0.5, 0.1875)
    ctc_bias = bell_draw(key_list[15], (V,), 0.5, 3.0, (), jnp.float32)
    return {"features": features, "logit_grad": logit_grad, "segment_ids": segment_ids, "conv_weight": conv_weight, "conv_bias": conv_bias, "w_qkv": w_qkv, "qv_bias": qv_bias, "w_out": w_out, "w_up": w_up, "ffn_bias": ffn_bias, "w_down": w_down, "out_biases": out_biases, "gains": gains, "shifts": shifts, "ctc_weight": ctc_weight, "ctc_bias": ctc_bias}


HIGH = lax.Precision.HIGHEST
EPS = 1e-05
NEG = -1e+30

@jax.custom_vjp
def low(v):
    return lax.optimization_barrier(v.astype(jnp.bfloat16)).astype(jnp.float32)

@jax.custom_vjp
def low_back(v):
    return v

def low_keep(v):
    return (low(v), None)

def low_pass(kept, grad):
    return (grad,)

def back_keep(v):
    return (v, None)

def back_low(kept, grad):
    return (low(grad),)
low.defvjp(low_keep, low_pass)
low_back.defvjp(back_keep, back_low)

def norm_rows(values, gain, shift):
    center = values - lax.optimization_barrier(jnp.mean(values, axis=-1, keepdims=True))
    spread = lax.optimization_barrier(jnp.mean(center * center, axis=-1, keepdims=True))
    return center * lax.rsqrt(spread + EPS) * gain + shift

def masked_conv(signal, kernel, parity_masks):
    running = jnp.zeros(signal.shape, jnp.float32)
    for parity in range(2):
        chosen = parity_masks[parity]
        result = lax.conv_general_dilated((signal * chosen)[None], kernel, (1,), [(KW // 2, KW // 2 - 1)], dimension_numbers=('NWC', 'OIW', 'NWC'), feature_group_count=G, precision=HIGH)[0]
        running = running + result * chosen
    return running

def attention(queries, key_rows, value_rows, segments):
    length = queries.shape[0]
    block_rows = 512 if length % 512 == 0 else length
    block_count = length // block_rows
    score_scale = HD ** (-0.5)
    key_heads = key_rows.reshape(length, H, HD)
    value_heads = value_rows.reshape(length, H, HD)

    def one_block(inputs):
        query_block, segment_block = inputs
        scores = jnp.einsum('qhd,khd->hqk', query_block, key_heads, precision=HIGH) * score_scale
        scores = low_back(scores)
        same_utter = segment_block[:, None] == segments[None, :]
        scores = jnp.where(same_utter[None], scores, NEG)
        row_top = lax.optimization_barrier(jnp.max(scores, axis=-1, keepdims=True))
        weights = jnp.exp(scores - row_top)
        weights = low(weights / lax.optimization_barrier(jnp.sum(weights, axis=-1, keepdims=True)))
        return jnp.einsum('hqk,khd->qhd', weights, value_heads, precision=HIGH)
    blocks = lax.map(jax.checkpoint(one_block), (queries.reshape(block_count, block_rows, H, HD), segments.reshape(block_count, block_rows)))
    return blocks.reshape(length, H * HD)

def row_forward(weights, features, segments):
    conv_weight, conv_bias, w_qkv, qv_bias, w_out, w_up, ffn_bias, w_down, out_biases, gains, shifts, ctc_weight, ctc_bias = weights
    parity = segments % 2
    parity_masks = jnp.stack([parity == 0, parity == 1]).astype(jnp.float32)[:, :, None]
    conv_sum = low_back(masked_conv(features, conv_weight, parity_masks) + conv_bias)
    branch = low_back(low(jax.nn.gelu(conv_sum, approximate=False)))
    first_sum = features + branch
    normed = low(norm_rows(first_sum, gains[0], shifts[0]))
    joined = jnp.dot(normed, w_qkv.reshape(D, 3 * D), precision=HIGH)
    queries = low_back(low(joined[:, :D] + qv_bias[0]))
    key_rows = low_back(low(joined[:, D:2 * D]))
    value_rows = low_back(low(joined[:, 2 * D:] + qv_bias[1]))
    mixed_heads = low_back(low(attention(queries, key_rows, value_rows, segments)))
    second = first_sum + low_back(jnp.dot(mixed_heads, w_out, precision=HIGH) + out_biases[0])
    normed_two = low(norm_rows(second, gains[1], shifts[1]))
    hidden = low_back(jnp.dot(normed_two, w_up, precision=HIGH) + ffn_bias)
    active = low(jax.nn.gelu(hidden, approximate=False))
    third_sum = second + low_back(jnp.dot(active, w_down, precision=HIGH) + out_biases[1])
    final_norm = low(norm_rows(third_sum, gains[2], shifts[2]))
    return jnp.dot(final_norm, ctc_weight, precision=HIGH) + ctc_bias

def reference(features, logit_grad, segment_ids, conv_weight, conv_bias, w_qkv, qv_bias, w_out, w_up, ffn_bias, w_down, out_biases, gains, shifts, ctc_weight, ctc_bias):
    weights = tuple((member.astype(jnp.float32) for member in (conv_weight, conv_bias, w_qkv, qv_bias, w_out, w_up, ffn_bias, w_down, out_biases, gains, shifts, ctc_weight, ctc_bias)))

    def one_row(running, row_inputs):
        row_features, row_cotangent, row_segments = row_inputs

        def forward(params, signal):
            return row_forward(params, signal, row_segments)
        logits, pullback = jax.vjp(forward, weights, row_features.astype(jnp.float32))
        param_grads, feature_grad = pullback(row_cotangent.astype(jnp.float32))
        running = jax.tree.map(jnp.add, running, param_grads)
        return (running, (logits, feature_grad))
    zero_grads = jax.tree.map(jnp.zeros_like, weights)
    totals, (logits, feature_grad) = lax.scan(one_row, zero_grads, (features, logit_grad, segment_ids))
    return (logits, feature_grad, totals[0], totals[1], totals[2], totals[3], totals[4], totals[5], totals[6], totals[7], totals[8], totals[9], totals[10], totals[11], totals[12])
```

```python
import jax
import jax.numpy as jnp
from jax import lax
from jax.experimental import pallas as pl
from jax.experimental.pallas import tpu as pltpu
from jax.sharding import PartitionSpec as P

HD = 64


EPS = 1e-05
NEG = -1e30


def norm_rows(values, gain, shift):
    center = values - jnp.mean(values, axis=-1, keepdims=True)
    spread = jnp.mean(center * center, axis=-1, keepdims=True)
    return center * lax.rsqrt(spread + EPS) * gain + shift


def gelu_exact(values):
    return jax.nn.gelu(values, approximate=False)


PH = 4
RB = 16


def swap_halves(even, odd):
    half = even.shape[1] // 2
    left = lax.broadcasted_iota(jnp.int32, even.shape, 1) < half
    return (
        jnp.where(left, even, pltpu.roll(odd, half, 1)),
        jnp.where(left, pltpu.roll(even, half, 1), odd),
    )


def split_segments(rows_ref, seg_ref, main_ref, side_ref):
    length, channels = rows_ref.shape
    pad = side_ref.shape[2] // 3
    seg = seg_ref[...]
    rows = rows_ref[...].astype(jnp.float32)
    middle = jnp.where(seg == 1, rows, 0.0)
    first = jnp.where(seg[:pad] == 0, rows[:pad], 0.0)
    last = jnp.where(seg[length - pad :] == 2, rows[length - pad :], 0.0)
    blank = jnp.zeros((pad, 128), jnp.float32)
    for tile in range(channels // 128):
        lanes = slice(128 * tile, 128 * tile + 128)
        main_ref[tile, 0:pad, :] = blank
        main_ref[tile, pad : pad + length, :] = middle[:, lanes]
        main_ref[tile, pad + length :, :] = blank
        for at, part in ((0, first), (1, last)):
            side_ref[at, tile, 0:pad, :] = blank
            side_ref[at, tile, pad : 2 * pad, :] = part[:, lanes]
            side_ref[at, tile, 2 * pad :, :] = blank


def phase_layout(main_ref, side_ref, main_out, side_out):
    tiles = main_ref.shape[0]
    pad = side_ref.shape[2] // 3
    stride = (main_ref.shape[1] - 2 * pad) // RB
    main_blocks = main_out.shape[1] // RB
    side_blocks = side_out.shape[1] // (2 * RB)

    def pack(load, store):
        for pair in range(PH // 2):
            for tile in range(tiles):
                both = swap_halves(load(tile, 2 * pair), load(tile, 2 * pair + 1))
                for at in range(2):
                    store(2 * tile + at, pair, both[at].astype(jnp.bfloat16))

    @pl.loop(0, main_blocks)
    def _(block):
        def load(tile, phase):
            return main_ref.at[tile][pl.ds(PH * block + phase, RB, stride=stride), :]

        def store(group, pair, value):
            main_out[group, pl.ds(pl.multiple_of(RB * block, RB), RB), 128 * pair : 128 * pair + 128] = value

        pack(load, store)

    @pl.loop(0, side_blocks)
    def _(block):
        for end in range(2):
            def load(tile, phase):
                return side_ref.at[end, tile][pl.ds(PH * block + phase, RB, stride=PH), :]

            def store(group, pair, value):
                at = pl.multiple_of(2 * RB * block + RB * end, RB)
                side_out[group, pl.ds(at, RB), 128 * pair : 128 * pair + 128] = value

            pack(load, store)


def frame_layout(sums_ref, main_ref, side_ref):
    tiles = main_ref.shape[0]
    length = main_ref.shape[1]
    blocks = length // (PH * RB)
    stride = length // RB
    for tile in range(tiles):
        for pair in range(PH // 2):
            lanes = slice(128 * pair, 128 * pair + 128)
            for block in range(blocks + 2):
                rows = slice(RB * block, RB * block + RB)
                both = swap_halves(sums_ref[2 * tile, rows, lanes], sums_ref[2 * tile + 1, rows, lanes])
                for at in range(2):
                    phase = 2 * pair + at
                    if block < blocks:
                        main_ref.at[tile][pl.ds(PH * block + phase, RB, stride=stride), :] = both[at]
                    else:
                        side_ref.at[block - blocks, tile][pl.ds(phase, RB, stride=PH), :] = both[at]


def join_segments(main_ref, side_ref, seg_ref):
    length = main_ref.shape[1]
    pad = side_ref.shape[2]
    seg = seg_ref[...]
    pieces = []
    for tile in range(main_ref.shape[0]):
        main = main_ref[tile]
        top = jnp.where(seg[:pad] == 0, side_ref[0, tile], main[:pad])
        low = jnp.where(seg[length - pad :] == 2, side_ref[1, tile], main[length - pad :])
        pieces.append(jnp.concatenate([top, main[pad : length - pad], low], axis=0))
    return jnp.concatenate(pieces, axis=1)


def tap_chunks(count):
    step = 11 if count % 11 == 0 else 1
    return [(at, step) for at in range(0, count, step)]


def phase_dot(main_in, side_in, taps_ref, sums_ref, turned):
    rows = sums_ref.shape[1] - 2 * RB
    width = main_in.shape[2]
    count = side_in.shape[1] // (2 * RB)

    @pl.loop(0, sums_ref.shape[0])
    def _(group):
        total = jnp.zeros(sums_ref.shape[1:], jnp.float32)
        for first, step in tap_chunks(count):
            if turned:
                for d in range(first, first + step):
                    back = count - 1 - d
                    left = jnp.concatenate(
                        [main_in[group, RB * back : RB * back + rows, :], side_in[group, 2 * RB * back : 2 * RB * back + 2 * RB, :]], axis=0
                    )
                    right = jnp.concatenate(
                        [taps_ref[group, width * d + 128 : width * d + 128 + width, :], taps_ref[group, width * d : width * d + width, :]], axis=1
                    )
                    total += lax.dot_general(left, right, (((1,), (1,)), ((), ())), preferred_element_type=jnp.float32)
            else:
                left = jnp.concatenate(
                    [
                        jnp.concatenate(
                            [main_in[group, RB * d : RB * d + rows, :], side_in[group, 2 * RB * d : 2 * RB * d + 2 * RB, :]], axis=0
                        )
                        for d in range(first, first + step)
                    ],
                    axis=1,
                )
                low, high = width * first, width * (first + step)
                right = jnp.concatenate([taps_ref[group, low + 128 : high + 128, :], taps_ref[group, low:high, :]], axis=1)
                total += jnp.dot(left, right, preferred_element_type=jnp.float32)
        sums_ref[group] = total


def gelu_parts(values):
    share = 0.5 * (1.0 + lax.erf(values * (0.5**0.5)))
    slope = jnp.exp(-0.5 * values * values) * 0.3989422804014327
    return values * share, share + values * slope


def conv_forward_kernel(
    rows_ref, seg_ref, taps_ref, bias_ref, branch_ref, slope_ref,
    main_seq, side_seq, main_in, side_in, sums, main_out, side_out,
):
    split_segments(rows_ref, seg_ref, main_seq, side_seq)
    phase_layout(main_seq, side_seq, main_in, side_in)
    phase_dot(main_in, side_in, taps_ref, sums, False)
    frame_layout(sums, main_out, side_out)
    conv_sum = join_segments(main_out, side_out, seg_ref) + bias_ref[...]
    value, slope = gelu_parts(conv_sum)
    branch_ref[...] = value.astype(branch_ref.dtype)
    slope_ref[...] = slope.astype(slope_ref.dtype)


def conv_input_grad_kernel(
    rows_ref, seg_ref, taps_ref, grad_ref,
    main_seq, side_seq, main_in, side_in, sums, main_out, side_out,
):
    split_segments(rows_ref, seg_ref, main_seq, side_seq)
    phase_layout(main_seq, side_seq, main_in, side_in)
    phase_dot(main_in, side_in, taps_ref, sums, True)
    frame_layout(sums, main_out, side_out)
    grad_ref[...] = join_segments(main_out, side_out, seg_ref).astype(grad_ref.dtype)


def scratch_of(length, channels, group, taps):
    pad = taps // 2
    groups = channels // group
    tiles = channels // 128
    count = taps // PH + 1
    main_rows = RB * (length // (PH * RB) + count - 1)
    return dict(
        main_seq=pltpu.VMEM((tiles, length + 2 * pad, 128), jnp.float32),
        side_seq=pltpu.VMEM((2, tiles, 3 * pad, 128), jnp.float32),
        main_in=pltpu.VMEM((groups, main_rows, PH * group), jnp.bfloat16),
        side_in=pltpu.VMEM((groups, 2 * RB * count, PH * group), jnp.bfloat16),
        sums=pltpu.VMEM((groups, length // PH + 2 * RB, PH * group), jnp.float32),
        main_out=pltpu.VMEM((tiles, length, 128), jnp.float32),
        side_out=pltpu.VMEM((2, tiles, pad, 128), jnp.float32),
    )


PARAMS = pltpu.CompilerParams(vmem_limit_bytes=50 * 1024 * 1024)
WHOLE = pl.BlockSpec(memory_space=pltpu.VMEM)


def conv_forward(rows, seg_col, taps, bias, group, width):
    length, channels = rows.shape
    flops = 2 * (length + 128) * channels * group * (width + 4)
    return pl.pallas_call(
        conv_forward_kernel,
        out_shape=(
            jax.ShapeDtypeStruct((length, channels), jnp.bfloat16),
            jax.ShapeDtypeStruct((length, channels), jnp.float32),
        ),
        in_specs=[WHOLE] * 4,
        out_specs=(WHOLE, WHOLE),
        scratch_shapes=list(scratch_of(length, channels, group, width).values()),
        compiler_params=PARAMS,
        cost_estimate=pl.CostEstimate(flops=flops, bytes_accessed=taps.size * 2, transcendentals=0),
    )(rows, seg_col, taps, bias)


def conv_input_grad(rows, seg_col, taps, group, width):
    length, channels = rows.shape
    flops = 2 * (length + 128) * channels * group * (width + 4)
    return pl.pallas_call(
        conv_input_grad_kernel,
        out_shape=jax.ShapeDtypeStruct((length, channels), jnp.float32),
        in_specs=[WHOLE] * 3,
        out_specs=WHOLE,
        scratch_shapes=list(scratch_of(length, channels, group, width).values()),
        compiler_params=PARAMS,
        cost_estimate=pl.CostEstimate(flops=flops, bytes_accessed=taps.size * 2, transcendentals=0),
    )(rows, seg_col, taps)


def conv_weight_grad_kernel(
    rows_ref, low_ref, seg_ref, grad_ref,
    main_seq, side_seq, main_in, side_in, main_low, side_low, folded, turned,
):
    groups, _, width = main_in.shape
    count = side_in.shape[1] // (2 * RB)
    low_rows = low_ref.shape[0] // PH
    middle = (count - 1) // 2
    group_size = width // PH
    taps = PH * (count - 1)
    split_segments(low_ref, seg_ref, main_seq, side_seq)
    phase_layout(main_seq, side_seq, main_low, side_low)
    split_segments(rows_ref, seg_ref, main_seq, side_seq)
    phase_layout(main_seq, side_seq, main_in, side_in)
    left_lanes = lax.broadcasted_iota(jnp.int32, (taps, 128), 1) < group_size

    @pl.loop(0, groups)
    def _(group):
        right = jnp.concatenate(
            [
                main_low[group, RB * middle : RB * middle + low_rows, :],
                side_low[group, 2 * RB * middle : 2 * RB * middle + 2 * RB, :],
            ],
            axis=0,
        )
        folded[0:128, :] = jnp.zeros((128, 128), jnp.float32)
        for d in range(count):
            left = jnp.concatenate(
                [main_in[group, RB * d : RB * d + low_rows, :], side_in[group, 2 * RB * d : 2 * RB * d + 2 * RB, :]], axis=0
            )
            part = lax.dot_general(left, right, (((0,), (0,)), ((), ())), preferred_element_type=jnp.float32)
            folded[width * d + 128 : width * d + 128 + width, :] = part[:, 0:128]
            folded[width * d : width * d + width, :] += part[:, 128:256]

        @pl.loop(0, group_size // 8)
        def _(chunk):
            for at in range(8):
                channel = 8 * chunk + at
                now = folded[pl.ds(128 + channel, taps, stride=group_size), :]
                later = folded[pl.ds(128 + group_size + channel, taps, stride=group_size), :]
                both = jnp.where(left_lanes, now, later).T
                turned[pl.ds(channel, group_size, stride=group_size), :] = both[0:group_size] + both[group_size:]

        grad_ref[pl.ds(pl.multiple_of(group * group_size * group_size, 128), group_size * group_size), :] = turned[...].astype(grad_ref.dtype)


def kernel_weight_grad(rows, low, seg_col, group, width):
    length, channels = rows.shape
    flops = 2 * (length + 128) * channels * group * (width + 4)
    shapes = scratch_of(length, channels, group, width)
    count = width // PH + 1
    names = ["main_seq", "side_seq", "main_in", "side_in", "main_in", "side_in"]
    out = pl.pallas_call(
        conv_weight_grad_kernel,
        out_shape=jax.ShapeDtypeStruct((channels * group, width), jnp.bfloat16),
        in_specs=[WHOLE] * 3,
        out_specs=WHOLE,
        scratch_shapes=[shapes[n] for n in names]
        + [
            pltpu.VMEM((PH * group * count + 128, 128), jnp.float32),
            pltpu.VMEM((group * group, width), jnp.float32),
        ],
        compiler_params=PARAMS,
        cost_estimate=pl.CostEstimate(flops=flops, bytes_accessed=channels * group * width * 2, transcendentals=0),
    )(rows, low, seg_col)
    return out.reshape(channels, group, width)


def tap_matrix(kernel):
    channels, group, width = kernel.shape
    groups = channels // group
    flat = kernel.reshape(groups, group, group, width).transpose(0, 3, 2, 1).reshape(groups, width * group, group)
    now = jnp.pad(flat, ((0, 0), (128, 2 * 128), (0, 0)))
    before = jnp.pad(flat, ((0, 0), (128 + group, 128 + group), (0, 0)))
    return jnp.concatenate([now, before], axis=2)


def contract_first(left_rows, right_rows):
    return lax.dot_general(
        left_rows, right_rows, (((0,), (0,)), ((), ())), preferred_element_type=jnp.float32
    )


def contract_last(left_rows, right_rows):
    return lax.dot_general(
        left_rows, right_rows, (((1,), (1,)), ((), ())), preferred_element_type=jnp.float32
    )


def shards(
    features,
    logit_grad,
    segment_ids,
    conv_weight,
    conv_bias,
    w_qkv,
    qv_bias,
    w_out,
    w_up,
    ffn_bias,
    w_down,
    out_biases,
    gains,
    shifts,
    ctc_weight,
    ctc_bias,
):
    rank_count = lax.axis_size("sp")
    signal = features[0]
    frames, model_width = signal.shape
    segments = segment_ids[0]
    length = segments.shape[0]
    local_width = model_width // rank_count
    kernel_width = conv_weight.shape[2]
    heads_here = local_width // HD
    score_scale = HD ** (-0.5)
    block_rows = 512
    block_count = length // block_rows
    group_size = conv_weight.shape[1]
    seg_col = segments[:, None]
    taps = tap_matrix(conv_weight)
    grouped = lax.all_to_all(signal, "sp", split_axis=1, concat_axis=0, tiled=True)
    activated, conv_slope = conv_forward(grouped, seg_col, taps, conv_bias[None], group_size, kernel_width)
    back_frames = lax.all_to_all(
        activated, "sp", split_axis=0, concat_axis=1, tiled=True
    )
    first_sum = signal.astype(jnp.float32) + back_frames.astype(jnp.float32)
    normed, norm_one_pull = jax.vjp(norm_rows, first_sum, gains[0], shifts[0])
    normed_full = lax.all_gather(normed.astype(jnp.bfloat16), "sp", axis=0, tiled=True)
    joined = jnp.dot(
        normed_full, w_qkv.reshape(model_width, 3 * local_width), preferred_element_type=jnp.float32
    )
    queries = (
        (joined[:, :local_width] + qv_bias[0]).astype(jnp.bfloat16).reshape(length, heads_here, HD)
    )
    key_rows = (
        joined[:, local_width : 2 * local_width]
        .astype(jnp.bfloat16)
        .reshape(length, heads_here, HD)
    )
    value_rows = (
        (joined[:, 2 * local_width :] + qv_bias[1])
        .astype(jnp.bfloat16)
        .reshape(length, heads_here, HD)
    )
    query_blocks = queries.reshape(block_count, block_rows, heads_here, HD)
    segment_blocks = segments.reshape(block_count, block_rows)

    def block_scores(query_block, segment_block):
        scores = (
            jnp.einsum("qhd,khd->hqk", query_block, key_rows, preferred_element_type=jnp.float32)
            * score_scale
        )
        same_utter = segment_block[:, None] == segments[None, :]
        return jnp.where(same_utter[None], scores, NEG)

    def attend_block(inputs):
        query_block, segment_block = inputs
        scores = block_scores(query_block, segment_block)
        row_top = jnp.max(scores, axis=-1, keepdims=True)
        weights = jnp.exp(scores - row_top)
        row_total = jnp.sum(weights, axis=-1, keepdims=True)
        probs_low = (weights / row_total).astype(jnp.bfloat16)
        result = jnp.einsum(
            "hqk,khd->qhd", probs_low, value_rows, preferred_element_type=jnp.float32
        )
        return (result.astype(jnp.bfloat16), (row_top + jnp.log(row_total))[..., 0])

    mixed_blocks, log_totals = lax.map(attend_block, (query_blocks, segment_blocks))
    mixed_heads = mixed_blocks.reshape(length, local_width)
    attn_part = lax.psum_scatter(
        jnp.dot(mixed_heads, w_out, preferred_element_type=jnp.float32).astype(jnp.bfloat16),
        "sp",
        scatter_dimension=0,
        tiled=True,
    ).astype(jnp.float32)
    second_sum = first_sum + attn_part + out_biases[0]
    normed_two, norm_two_pull = jax.vjp(norm_rows, second_sum, gains[1], shifts[1])
    normed_two_low = normed_two.astype(jnp.bfloat16)
    ffn_rows = lax.all_gather(normed_two_low, "sp", axis=0, tiled=True)
    hidden = jnp.dot(ffn_rows, w_up, preferred_element_type=jnp.float32) + ffn_bias
    active, gelu_ffn_pull = jax.vjp(gelu_exact, hidden)
    active_low = active.astype(jnp.bfloat16)
    third_sum = (
        second_sum
        + lax.psum_scatter(
            jnp.dot(
                lax.slice_in_dim(active_low, 0, frames * lax.axis_size("sp"), axis=0),
                w_down,
                preferred_element_type=jnp.float32,
            ).astype(jnp.bfloat16),
            "sp",
            scatter_dimension=0,
            tiled=True,
        ).astype(jnp.float32)
        + out_biases[1]
    )
    final_norm, norm_final_pull = jax.vjp(norm_rows, third_sum, gains[2], shifts[2])
    final_low = final_norm.astype(jnp.bfloat16)
    logits = jnp.dot(final_low, ctc_weight, preferred_element_type=jnp.float32) + ctc_bias
    cotangent = logit_grad[0]
    ctc_weight_grad = contract_first(final_low, cotangent)
    ctc_bias_grad = jnp.sum(cotangent.astype(jnp.float32), axis=0)
    final_grad = contract_last(cotangent, ctc_weight)
    third_grad, final_gain_grad, final_shift_grad = norm_final_pull(final_grad)
    down_full = lax.all_gather(third_grad.astype(jnp.bfloat16), "sp", axis=0, tiled=True)
    down_bias_grad = jnp.sum(down_full.astype(jnp.float32), axis=0)
    down_grad = contract_first(active_low, down_full)
    active_grad = contract_last(down_full, w_down)
    (hidden_grad,) = gelu_ffn_pull(active_grad)
    hidden_low = hidden_grad.astype(jnp.bfloat16)
    ffn_bias_grad = jnp.sum(hidden_low.astype(jnp.float32), axis=0)
    up_grad = contract_first(ffn_rows, hidden_low)
    normed_two_grad = lax.psum_scatter(
        contract_last(
            lax.slice_in_dim(hidden_low, 0, frames * lax.axis_size("sp"), axis=0), w_up
        ).astype(jnp.bfloat16),
        "sp",
        scatter_dimension=0,
        tiled=True,
    ).astype(jnp.float32)
    second_part, gain_two_grad, shift_two_grad = norm_two_pull(normed_two_grad)
    second_grad = third_grad + second_part
    out_full = lax.all_gather(second_grad.astype(jnp.bfloat16), "sp", axis=0, tiled=True)
    out_bias_grad = jnp.sum(out_full.astype(jnp.float32), axis=0)
    out_grad = contract_first(mixed_heads, out_full)
    mixed_grad = contract_last(out_full, w_out).astype(jnp.bfloat16)
    grad_blocks = mixed_grad.reshape(block_count, block_rows, heads_here, HD)

    def attend_back(carry, inputs):
        key_acc, value_acc = carry
        query_block, segment_block, grad_block, total_block = inputs
        scores = block_scores(query_block, segment_block)
        probs = jnp.exp(scores - total_block[..., None])
        probs_low = probs.astype(jnp.bfloat16)
        prob_grad = jnp.einsum(
            "qhd,khd->hqk", grad_block, value_rows, preferred_element_type=jnp.float32
        )
        row_delta = jnp.sum(probs * prob_grad, axis=-1, keepdims=True)
        score_grad = (probs * (prob_grad - row_delta)).astype(jnp.bfloat16)
        query_part = (
            jnp.einsum("hqk,khd->qhd", score_grad, key_rows, preferred_element_type=jnp.float32)
            * score_scale
        )
        key_acc = (
            key_acc
            + jnp.einsum(
                "hqk,qhd->khd", score_grad, query_block, preferred_element_type=jnp.float32
            )
            * score_scale
        )
        value_acc = value_acc + jnp.einsum(
            "hqk,qhd->khd", probs_low, grad_block, preferred_element_type=jnp.float32
        )
        return ((key_acc, value_acc), query_part)

    zero_heads = jnp.zeros((length, heads_here, HD), jnp.float32)
    (key_grad, value_grad), query_grad = lax.scan(
        attend_back,
        (zero_heads, zero_heads),
        (query_blocks, segment_blocks, grad_blocks, log_totals),
    )
    query_low = query_grad.reshape(length, local_width).astype(jnp.bfloat16)
    key_low = key_grad.reshape(length, local_width).astype(jnp.bfloat16)
    value_low = value_grad.reshape(length, local_width).astype(jnp.bfloat16)
    joined_grad = jnp.concatenate([query_low, key_low, value_low], axis=1)
    qkv_grad = contract_first(normed_full, joined_grad).reshape(model_width, 3, local_width)
    qv_bias_grad = jnp.stack(
        [
            jnp.sum(query_low.astype(jnp.float32), axis=0),
            jnp.sum(value_low.astype(jnp.float32), axis=0),
        ]
    )
    normed_part = contract_last(joined_grad, w_qkv.reshape(model_width, 3 * local_width))
    norm_parts = jnp.stack([gain_two_grad, final_gain_grad, shift_two_grad, final_shift_grad])
    normed_grad, ctc_weight_part, ctc_bias_part, norm_part_sum = (
        lax.psum_scatter(
            normed_part.astype(jnp.bfloat16), "sp", scatter_dimension=0, tiled=True
        ).astype(jnp.float32),
        lax.psum_scatter(
            ctc_weight_grad.astype(jnp.bfloat16), "sp", scatter_dimension=0, tiled=True
        ).astype(jnp.float32),
        lax.psum_scatter(
            ctc_bias_grad.astype(jnp.bfloat16), "sp", scatter_dimension=0, tiled=True
        ).astype(jnp.float32),
        lax.psum_scatter(
            norm_parts.astype(jnp.bfloat16), "sp", scatter_dimension=1, tiled=True
        ).astype(jnp.float32),
    )
    first_part, gain_one_grad, shift_one_grad = norm_one_pull(normed_grad)
    first_grad = second_grad + first_part
    branch_groups = lax.all_to_all(
        first_grad.astype(jnp.bfloat16), "sp", split_axis=1, concat_axis=0, tiled=True
    )
    conv_low = (branch_groups.astype(jnp.float32) * conv_slope).astype(jnp.bfloat16)
    conv_bias_grad = jnp.sum(conv_low.astype(jnp.float32), axis=0)
    conv_weight_grad = kernel_weight_grad(grouped, conv_low, seg_col, group_size, kernel_width)
    signal_groups = conv_input_grad(conv_low, seg_col, taps, group_size, kernel_width)
    one_parts = (
        jnp.stack([gain_one_grad, shift_one_grad])
        .reshape(2, rank_count, local_width)
        .transpose(1, 0, 2)
        .reshape(2 * rank_count, local_width)
    )
    signal_back, one_received = (
        lax.all_to_all(
            signal_groups.astype(jnp.bfloat16), "sp", split_axis=0, concat_axis=1, tiled=True
        ).astype(signal_groups.dtype),
        lax.all_to_all(
            one_parts.astype(jnp.bfloat16), "sp", split_axis=0, concat_axis=1, tiled=True
        ).astype(one_parts.dtype),
    )
    one_sum = jnp.sum(one_received.reshape(2, rank_count, local_width), axis=1)
    feature_grad = first_grad + signal_back
    gains_grad = jnp.stack([one_sum[0], norm_part_sum[0], norm_part_sum[1]])
    shifts_grad = jnp.stack([one_sum[1], norm_part_sum[2], norm_part_sum[3]])
    out_biases_grad = jnp.stack([out_bias_grad, down_bias_grad])
    summed = (
        lax.psum(conv_weight_grad.astype(jnp.bfloat16), "dp").astype(jnp.float32),
        lax.psum(conv_bias_grad.astype(jnp.bfloat16), "dp").astype(jnp.float32),
        lax.psum(qkv_grad.astype(jnp.bfloat16), "dp").astype(jnp.float32),
        lax.psum(qv_bias_grad.astype(jnp.bfloat16), "dp").astype(jnp.float32),
        lax.psum(out_grad.astype(jnp.bfloat16), "dp").astype(jnp.float32),
        lax.psum(up_grad.astype(jnp.bfloat16), "dp").astype(jnp.float32),
        lax.psum(ffn_bias_grad.astype(jnp.bfloat16), "dp").astype(jnp.float32),
        lax.psum(down_grad.astype(jnp.bfloat16), "dp").astype(jnp.float32),
        lax.psum(out_biases_grad.astype(jnp.bfloat16), "dp").astype(jnp.float32),
        lax.psum(gains_grad.astype(jnp.bfloat16), "dp").astype(jnp.float32),
        lax.psum(shifts_grad.astype(jnp.bfloat16), "dp").astype(jnp.float32),
        lax.psum(ctc_weight_part.astype(jnp.bfloat16), "dp").astype(jnp.float32),
        lax.psum(ctc_bias_part.astype(jnp.bfloat16), "dp").astype(jnp.float32),
    )
    return (
        logits[None],
        feature_grad[None],
        summed[0],
        summed[1],
        summed[2],
        summed[3],
        summed[4],
        summed[5],
        summed[6],
        summed[7],
        summed[8],
        summed[9],
        summed[10],
        summed[11],
        summed[12],
    )


def solution(mesh):
    in_specs = (
        P("dp", "sp", None),
        P("dp", "sp", None),
        P("dp", None),
        P("sp", None, None),
        P("sp"),
        P(None, None, "sp"),
        P(None, "sp"),
        P("sp", None),
        P(None, "sp"),
        P("sp"),
        P("sp", None),
        P(),
        P(),
        P(),
        P(),
        P(),
    )
    out_specs = (
        P("dp", "sp", None),
        P("dp", "sp", None),
        P("sp", None, None),
        P("sp"),
        P(None, None, "sp"),
        P(None, "sp"),
        P("sp", None),
        P(None, "sp"),
        P("sp"),
        P("sp", None),
        P(),
        P(None, "sp"),
        P(None, "sp"),
        P("sp", None),
        P("sp"),
    )
    return jax.shard_map(shards, mesh=mesh, in_specs=in_specs, out_specs=out_specs, check_vma=False)
```

```python
import jax
import jax.numpy as jnp
from jax import lax
from jax.experimental import pallas as pl
from jax.experimental.pallas import tpu as pltpu
from jax.sharding import PartitionSpec as P

HD = 64


EPS = 1e-05
NEG = -1e30


def norm_rows(values, gain, shift):
    center = values - jnp.mean(values, axis=-1, keepdims=True)
    spread = jnp.mean(center * center, axis=-1, keepdims=True)
    return center * lax.rsqrt(spread + EPS) * gain + shift


def gelu_exact(values):
    return jax.nn.gelu(values, approximate=False)


PH = 4
RB = 16


def swap_halves(even, odd):
    half = even.shape[1] // 2
    left = lax.broadcasted_iota(jnp.int32, even.shape, 1) < half
    return (
        jnp.where(left, even, pltpu.roll(odd, half, 1)),
        jnp.where(left, pltpu.roll(even, half, 1), odd),
    )


def split_segments(rows_ref, seg_ref, main_ref, side_ref):
    length, channels = rows_ref.shape
    pad = side_ref.shape[2] // 3
    seg = seg_ref[...]
    rows = rows_ref[...].astype(jnp.float32)
    middle = jnp.where(seg == 1, rows, 0.0)
    first = jnp.where(seg[:pad] == 0, rows[:pad], 0.0)
    last = jnp.where(seg[length - pad :] == 2, rows[length - pad :], 0.0)
    blank = jnp.zeros((pad, 128), jnp.float32)
    for tile in range(channels // 128):
        lanes = slice(128 * tile, 128 * tile + 128)
        main_ref[tile, 0:pad, :] = blank
        main_ref[tile, pad : pad + length, :] = middle[:, lanes]
        main_ref[tile, pad + length :, :] = blank
        for at, part in ((0, first), (1, last)):
            side_ref[at, tile, 0:pad, :] = blank
            side_ref[at, tile, pad : 2 * pad, :] = part[:, lanes]
            side_ref[at, tile, 2 * pad :, :] = blank


def phase_layout(main_ref, side_ref, main_out, side_out):
    tiles = main_ref.shape[0]
    pad = side_ref.shape[2] // 3
    stride = (main_ref.shape[1] - 2 * pad) // RB
    main_blocks = main_out.shape[1] // RB
    side_blocks = side_out.shape[1] // (2 * RB)

    def pack(load, store):
        for pair in range(PH // 2):
            for tile in range(tiles):
                both = swap_halves(load(tile, 2 * pair), load(tile, 2 * pair + 1))
                for at in range(2):
                    store(2 * tile + at, pair, both[at].astype(jnp.bfloat16))

    @pl.loop(0, main_blocks)
    def _(block):
        def load(tile, phase):
            return main_ref.at[tile][pl.ds(PH * block + phase, RB, stride=stride), :]

        def store(group, pair, value):
            main_out[group, pl.ds(pl.multiple_of(RB * block, RB), RB), 128 * pair : 128 * pair + 128] = value

        pack(load, store)

    @pl.loop(0, side_blocks)
    def _(block):
        for end in range(2):
            def load(tile, phase):
                return side_ref.at[end, tile][pl.ds(PH * block + phase, RB, stride=PH), :]

            def store(group, pair, value):
                at = pl.multiple_of(2 * RB * block + RB * end, RB)
                side_out[group, pl.ds(at, RB), 128 * pair : 128 * pair + 128] = value

            pack(load, store)


def frame_layout(sums_ref, main_ref, side_ref):
    tiles = main_ref.shape[0]
    length = main_ref.shape[1]
    blocks = length // (PH * RB)
    stride = length // RB
    for tile in range(tiles):
        for pair in range(PH // 2):
            lanes = slice(128 * pair, 128 * pair + 128)
            for block in range(blocks + 2):
                rows = slice(RB * block, RB * block + RB)
                both = swap_halves(sums_ref[2 * tile, rows, lanes], sums_ref[2 * tile + 1, rows, lanes])
                for at in range(2):
                    phase = 2 * pair + at
                    if block < blocks:
                        main_ref.at[tile][pl.ds(PH * block + phase, RB, stride=stride), :] = both[at]
                    else:
                        side_ref.at[block - blocks, tile][pl.ds(phase, RB, stride=PH), :] = both[at]


def join_segments(main_ref, side_ref, seg_ref):
    length = main_ref.shape[1]
    pad = side_ref.shape[2]
    seg = seg_ref[...]
    pieces = []
    for tile in range(main_ref.shape[0]):
        main = main_ref[tile]
        top = jnp.where(seg[:pad] == 0, side_ref[0, tile], main[:pad])
        low = jnp.where(seg[length - pad :] == 2, side_ref[1, tile], main[length - pad :])
        pieces.append(jnp.concatenate([top, main[pad : length - pad], low], axis=0))
    return jnp.concatenate(pieces, axis=1)


def tap_chunks(count):
    step = 11 if count % 11 == 0 else 1
    return [(at, step) for at in range(0, count, step)]


def fill_taps(rows_ref, group, taps_ref):
    count, size = rows_ref.shape[1:]
    step = min(1024, count)
    taps_ref[0:128, :] = jnp.zeros((128, 128), taps_ref.dtype)
    for at in range(0, count, step):
        now = rows_ref[group, at : at + step, :]
        if at:
            before = rows_ref[group, at - size : at - size + step, :]
        else:
            before = jnp.concatenate([jnp.zeros((size, size), now.dtype), rows_ref[group, 0 : step - size, :]], axis=0)
        taps_ref[128 + at : 128 + at + step, :] = jnp.concatenate([now, before], axis=1)
    last = rows_ref[group, count - size : count, :]
    taps_ref[128 + count : 128 + count + size, :] = jnp.concatenate([jnp.zeros_like(last), last], axis=1)
    taps_ref[128 + count + size :, :] = jnp.zeros((taps_ref.shape[0] - 128 - count - size, 128), taps_ref.dtype)


def phase_dot(main_in, side_in, rows_ref, taps_ref, sums_ref, turned):
    rows = sums_ref.shape[1] - 2 * RB
    width = main_in.shape[2]
    count = side_in.shape[1] // (2 * RB)

    @pl.loop(0, sums_ref.shape[0])
    def _(group):
        fill_taps(rows_ref, group, taps_ref)
        total = jnp.zeros(sums_ref.shape[1:], jnp.float32)
        for first, step in tap_chunks(count):
            if turned:
                for d in range(first, first + step):
                    back = count - 1 - d
                    left = jnp.concatenate(
                        [main_in[group, RB * back : RB * back + rows, :], side_in[group, 2 * RB * back : 2 * RB * back + 2 * RB, :]], axis=0
                    )
                    right = jnp.concatenate(
                        [taps_ref[width * d + 128 : width * d + 128 + width, :], taps_ref[width * d : width * d + width, :]], axis=1
                    )
                    total += lax.dot_general(left, right, (((1,), (1,)), ((), ())), preferred_element_type=jnp.float32)
            else:
                left = jnp.concatenate(
                    [
                        jnp.concatenate(
                            [main_in[group, RB * d : RB * d + rows, :], side_in[group, 2 * RB * d : 2 * RB * d + 2 * RB, :]], axis=0
                        )
                        for d in range(first, first + step)
                    ],
                    axis=1,
                )
                low, high = width * first, width * (first + step)
                right = jnp.concatenate([taps_ref[low + 128 : high + 128, :], taps_ref[low:high, :]], axis=1)
                total += jnp.dot(left, right, preferred_element_type=jnp.float32)
        sums_ref[group] = total


def gelu_parts(values):
    share = 0.5 * (1.0 + lax.erf(values * (0.5**0.5)))
    slope = jnp.exp(-0.5 * values * values) * 0.3989422804014327
    return values * share, share + values * slope


def conv_forward_kernel(
    rows_ref, seg_ref, taps_ref, bias_ref, branch_ref, slope_ref, parts_ref,
    main_seq, side_seq, main_in, side_in, sums, taps_in, main_out, side_out,
):
    split_segments(rows_ref, seg_ref, main_seq, side_seq)

    def store(part, tile, value):
        parts_ref[part, :, 128 * tile : 128 * tile + 128] = value

    pack_wide(main_seq, side_seq, parts_ref.shape[2] // WP, store)
    phase_layout(main_seq, side_seq, main_in, side_in)
    phase_dot(main_in, side_in, taps_ref, taps_in, sums, False)
    frame_layout(sums, main_out, side_out)
    conv_sum = join_segments(main_out, side_out, seg_ref) + bias_ref[...]
    value, slope = gelu_parts(conv_sum)
    branch_ref[...] = value.astype(branch_ref.dtype)
    slope_ref[...] = slope.astype(slope_ref.dtype)


def conv_input_grad_kernel(
    rows_ref, seg_ref, taps_ref, grad_ref,
    main_seq, side_seq, main_in, side_in, sums, taps_in, main_out, side_out,
):
    split_segments(rows_ref, seg_ref, main_seq, side_seq)
    phase_layout(main_seq, side_seq, main_in, side_in)
    phase_dot(main_in, side_in, taps_ref, taps_in, sums, True)
    frame_layout(sums, main_out, side_out)
    grad_ref[...] = join_segments(main_out, side_out, seg_ref).astype(grad_ref.dtype)


def scratch_of(length, channels, group, taps):
    pad = taps // 2
    groups = channels // group
    tiles = channels // 128
    count = taps // PH + 1
    main_rows = RB * (length // (PH * RB) + count - 1)
    return dict(
        main_seq=pltpu.VMEM((tiles, length + 2 * pad, 128), jnp.float32),
        side_seq=pltpu.VMEM((2, tiles, 3 * pad, 128), jnp.float32),
        main_in=pltpu.VMEM((groups, main_rows, PH * group), jnp.bfloat16),
        side_in=pltpu.VMEM((groups, 2 * RB * count, PH * group), jnp.bfloat16),
        sums=pltpu.VMEM((groups, length // PH + 2 * RB, PH * group), jnp.float32),
        taps=pltpu.VMEM((PH * group * (count + 1), 128), jnp.bfloat16),
        main_out=pltpu.VMEM((tiles, length, 128), jnp.float32),
        side_out=pltpu.VMEM((2, tiles, pad, 128), jnp.float32),
    )


PARAMS = pltpu.CompilerParams(vmem_limit_bytes=50 * 1024 * 1024)
WHOLE = pl.BlockSpec(memory_space=pltpu.VMEM)


def conv_forward(rows, seg_col, taps, bias, group, width):
    length, channels = rows.shape
    flops = 2 * (length + 128) * channels * group * (width + 4)
    return pl.pallas_call(
        conv_forward_kernel,
        out_shape=(
            jax.ShapeDtypeStruct((length, channels), jnp.bfloat16),
            jax.ShapeDtypeStruct((length, channels), jnp.float32),
            jax.ShapeDtypeStruct((channels // group, (length + width) // WP, WP * group), jnp.bfloat16),
        ),
        in_specs=[WHOLE] * 4,
        out_specs=(WHOLE, WHOLE, WHOLE),
        scratch_shapes=list(scratch_of(length, channels, group, width).values()),
        compiler_params=PARAMS,
        cost_estimate=pl.CostEstimate(flops=flops, bytes_accessed=taps.size * 2, transcendentals=0),
    )(rows, seg_col, taps, bias)


def conv_input_grad(rows, seg_col, taps, group, width):
    length, channels = rows.shape
    flops = 2 * (length + 128) * channels * group * (width + 4)
    return pl.pallas_call(
        conv_input_grad_kernel,
        out_shape=jax.ShapeDtypeStruct((length, channels), jnp.float32),
        in_specs=[WHOLE] * 3,
        out_specs=WHOLE,
        scratch_shapes=list(scratch_of(length, channels, group, width).values()),
        compiler_params=PARAMS,
        cost_estimate=pl.CostEstimate(flops=flops, bytes_accessed=taps.size * 2, transcendentals=0),
    )(rows, seg_col, taps)


def conv_weight_grad_kernel(
    rows_ref, low_ref, seg_ref, grad_ref,
    main_seq, side_seq, main_in, side_in, main_low, side_low, folded, turned,
):
    groups, _, width = main_in.shape
    count = side_in.shape[1] // (2 * RB)
    low_rows = low_ref.shape[0] // PH
    middle = (count - 1) // 2
    group_size = width // PH
    taps = PH * (count - 1)
    split_segments(low_ref, seg_ref, main_seq, side_seq)
    phase_layout(main_seq, side_seq, main_low, side_low)
    split_segments(rows_ref, seg_ref, main_seq, side_seq)
    phase_layout(main_seq, side_seq, main_in, side_in)
    left_lanes = lax.broadcasted_iota(jnp.int32, (taps, 128), 1) < group_size

    @pl.loop(0, groups)
    def _(group):
        right = jnp.concatenate(
            [
                main_low[group, RB * middle : RB * middle + low_rows, :],
                side_low[group, 2 * RB * middle : 2 * RB * middle + 2 * RB, :],
            ],
            axis=0,
        )
        folded[0:128, :] = jnp.zeros((128, 128), jnp.float32)
        for d in range(count):
            left = jnp.concatenate(
                [main_in[group, RB * d : RB * d + low_rows, :], side_in[group, 2 * RB * d : 2 * RB * d + 2 * RB, :]], axis=0
            )
            part = lax.dot_general(left, right, (((0,), (0,)), ((), ())), preferred_element_type=jnp.float32)
            folded[width * d + 128 : width * d + 128 + width, :] = part[:, 0:128]
            folded[width * d : width * d + width, :] += part[:, 128:256]

        @pl.loop(0, group_size // 8)
        def _(chunk):
            for at in range(8):
                channel = 8 * chunk + at
                now = folded[pl.ds(128 + channel, taps, stride=group_size), :]
                later = folded[pl.ds(128 + group_size + channel, taps, stride=group_size), :]
                both = jnp.where(left_lanes, now, later).T
                turned[pl.ds(channel, group_size, stride=group_size), :] = both[0:group_size] + both[group_size:]

        grad_ref[pl.ds(pl.multiple_of(group * group_size * group_size, 128), group_size * group_size), :] = turned[...].astype(grad_ref.dtype)


def kernel_weight_grad(rows, low, seg_col, group, width):
    length, channels = rows.shape
    flops = 2 * (length + 128) * channels * group * (width + 4)
    shapes = scratch_of(length, channels, group, width)
    count = width // PH + 1
    names = ["main_seq", "side_seq", "main_in", "side_in", "main_in", "side_in"]
    out = pl.pallas_call(
        conv_weight_grad_kernel,
        out_shape=jax.ShapeDtypeStruct((channels * group, width), jnp.bfloat16),
        in_specs=[WHOLE] * 3,
        out_specs=WHOLE,
        scratch_shapes=[shapes[n] for n in names]
        + [
            pltpu.VMEM((PH * group * count + 128, 128), jnp.float32),
            pltpu.VMEM((group * group, width), jnp.float32),
        ],
        compiler_params=PARAMS,
        cost_estimate=pl.CostEstimate(flops=flops, bytes_accessed=channels * group * width * 2, transcendentals=0),
    )(rows, low, seg_col)
    return out.reshape(channels, group, width)


def tap_rows(kernel):
    channels, group, width = kernel.shape
    groups = channels // group
    return kernel.reshape(groups, group, group, width).transpose(0, 3, 2, 1).reshape(groups, width * group, group)


WP = 8


def pack_wide(main_ref, side_ref, channels_each, store):
    tiles = main_ref.shape[0]
    pad = side_ref.shape[2] // 3
    rows = (main_ref.shape[1] - 2 * pad) // WP
    ends = pad // WP
    per = 128 // channels_each
    lane = lax.broadcasted_iota(jnp.int32, (rows + 2 * ends, 128), 1) // channels_each
    for tile in range(tiles):
        for group in range(WP // per):
            loads = []
            for at in range(per):
                phase = per * group + at
                loads.append(
                    jnp.concatenate(
                        [main_ref.at[tile][pl.ds(pad + phase, rows, stride=WP), :]]
                        + [side_ref.at[end, tile][pl.ds(pad + phase, ends, stride=WP), :] for end in range(2)],
                        axis=0,
                    )
                )
            for part in range(per):
                value = loads[0] if part == 0 else pltpu.roll(loads[0], (128 - channels_each * part) % 128, 1)
                for at in range(1, per):
                    turn = (channels_each * (at - part)) % 128
                    moved = loads[at] if turn == 0 else pltpu.roll(loads[at], turn, 1)
                    value = jnp.where(lane == at, moved, value)
                store(per * tile + part, group, value.astype(jnp.bfloat16))


def conv_low_kernel(
    cot_ref, slope_ref, seg_ref, low_ref, parts_ref, bias_ref, main_seq, side_seq,
):
    low = (cot_ref[...].astype(jnp.float32) * slope_ref[...]).astype(jnp.bfloat16)
    low_ref[...] = low
    bias_ref[...] = jnp.sum(low.astype(jnp.float32), axis=0, keepdims=True)
    split_segments(low_ref, seg_ref, main_seq, side_seq)

    def store(part, tile, value):
        parts_ref[part, :, 128 * tile : 128 * tile + 128] = value

    pack_wide(main_seq, side_seq, parts_ref.shape[2] // WP, store)


def conv_low_parts(cotangent, slope, seg_col, group, width, parts):
    length, channels = cotangent.shape
    each = channels // parts
    shapes = scratch_of(length, channels, group, width)
    return pl.pallas_call(
        conv_low_kernel,
        out_shape=(
            jax.ShapeDtypeStruct((length, channels), jnp.bfloat16),
            jax.ShapeDtypeStruct((parts, (length + width) // WP, WP * each), jnp.bfloat16),
            jax.ShapeDtypeStruct((1, channels), jnp.float32),
        ),
        in_specs=[WHOLE] * 3,
        out_specs=(WHOLE, WHOLE, WHOLE),
        scratch_shapes=[shapes["main_seq"], shapes["side_seq"]],
        compiler_params=PARAMS,
        cost_estimate=pl.CostEstimate(flops=8 * length * channels, bytes_accessed=8 * length * channels, transcendentals=0),
    )(cotangent, slope, seg_col)


def split_weight_grad_kernel(
    rows_ref, low_ref, grad_ref, seq, side_seq, main_in, side_in, low_seq, low_all, even, odd, turned, final,
):
    batch, packed, wide = rows_ref.shape
    low_width = low_ref.shape[2]
    each = low_width // WP
    group = wide // WP
    count = side_in.shape[1] // RB
    ends = (count - 1) // 2
    main_rows = packed - 2 * ends
    blocks = main_rows // RB
    taps = WP * (count - 1)

    @pl.loop(0, batch)
    def _(row):
        for tile in range(wide // 128):
            lanes = slice(128 * tile, 128 * tile + 128)
            values = rows_ref[row, :, lanes].astype(jnp.float32)
            blank = jnp.zeros((ends, 128), jnp.float32)
            seq[tile] = jnp.concatenate([blank, values[:main_rows], blank], axis=0)
            for end in range(2):
                side_seq[tile, end] = jnp.concatenate(
                    [blank, values[main_rows + ends * end : main_rows + ends * (end + 1)], blank], axis=0
                )
            for block in range(blocks + count - 1):
                main_in[row, RB * block : RB * block + RB, lanes] = seq.at[tile][pl.ds(block, RB, stride=blocks), :].astype(jnp.bfloat16)
            for d in range(count):
                side_in[row, RB * d : RB * d + RB, lanes] = jnp.concatenate(
                    [side_seq[tile, 0, d : d + ends, :], side_seq[tile, 1, d : d + ends, :]], axis=0
                ).astype(jnp.bfloat16)
        for tile in range(low_width // 128):
            lanes = slice(128 * tile, 128 * tile + 128)
            low_seq[tile] = low_ref[row, :, lanes].astype(jnp.float32)
            for block in range(blocks):
                low_all[row, RB * block : RB * block + RB, lanes] = low_seq.at[tile][pl.ds(block, RB, stride=blocks), :].astype(jnp.bfloat16)
            low_all[row, main_rows:packed, lanes] = low_ref[row, main_rows:packed, lanes]

    left = jnp.concatenate([low_all[row] for row in range(batch)], axis=0).T
    even[...] = jnp.zeros(even.shape, jnp.float32)
    odd[...] = jnp.zeros(odd.shape, jnp.float32)

    @pl.loop(0, count)
    def _(d):
        at = pl.multiple_of(RB * d, RB)
        right = jnp.concatenate(
            [
                part
                for row in range(batch)
                for part in (main_in[row, pl.ds(at, main_rows), :], side_in[row, pl.ds(at, RB), :])
            ],
            axis=0,
        )
        part = jnp.dot(left, right, preferred_element_type=jnp.float32)
        for phase in range(WP):
            held = even if phase % 2 == 0 else odd
            lanes = pl.ds(pl.multiple_of(wide * d + wide - group * (phase - phase % 2), 128), wide)
            held[:, lanes] += part[each * phase : each * (phase + 1), :]

    left_lanes = lax.broadcasted_iota(jnp.int32, (each, 128), 1) < group
    for tile in range(taps * group // 128):
        at = wide + 128 * tile
        near, far = odd[:, at : at + 128], odd[:, at + 128 : at + 256]
        value = even[:, at : at + 128] + jnp.where(left_lanes, pltpu.roll(near, group, 1), pltpu.roll(far, group, 1))
        turned[128 * tile : 128 * tile + 128, 0:each] = value.T

    @pl.loop(0, group // 8)
    def _(chunk):
        for at in range(8):
            channel = 8 * chunk + at
            final[pl.ds(channel, each, stride=group), :] = turned[pl.ds(channel, taps, stride=group), :].T[0:each, :]

    grad_ref[...] = final[...].astype(grad_ref.dtype)


def split_weight_grad(rows, low, group, width):
    batch, packed, wide = rows.shape
    each = low.shape[2] // WP
    count = width // WP + 1
    ends = (count - 1) // 2
    main_rows = packed - 2 * ends
    blocks = main_rows // RB
    flops = 2 * batch * packed * low.shape[2] * wide * count
    out = pl.pallas_call(
        split_weight_grad_kernel,
        out_shape=jax.ShapeDtypeStruct((each * group, width), jnp.bfloat16),
        in_specs=[WHOLE] * 2,
        out_specs=WHOLE,
        scratch_shapes=[
            pltpu.VMEM((wide // 128, main_rows + 2 * ends, 128), jnp.float32),
            pltpu.VMEM((wide // 128, 2, 3 * ends, 128), jnp.float32),
            pltpu.VMEM((batch, RB * (blocks + count - 1), wide), jnp.bfloat16),
            pltpu.VMEM((batch, RB * count, wide), jnp.bfloat16),
            pltpu.VMEM((low.shape[2] // 128, packed, 128), jnp.float32),
            pltpu.VMEM((batch, packed, low.shape[2]), jnp.bfloat16),
            pltpu.VMEM((each, wide * (count + 1)), jnp.float32),
            pltpu.VMEM((each, wide * (count + 1)), jnp.float32),
            pltpu.VMEM((width * group, 128), jnp.float32),
            pltpu.VMEM((each * group, width), jnp.float32),
        ],
        compiler_params=PARAMS,
        cost_estimate=pl.CostEstimate(flops=flops, bytes_accessed=2 * (rows.size + low.size), transcendentals=0),
    )(rows, low)
    return out


def unite_kernel(turn_ref, *refs):
    blocks, out_ref = refs[:-1], refs[-1]
    for at, block in enumerate(blocks):

        @pl.when(pl.program_id(0) == at)
        def _():
            out_ref[...] = block[...].astype(jnp.float32)


def unite_blocks(blocks, me):
    rows, columns = blocks[0].shape
    return pl.pallas_call(
        unite_kernel,
        out_shape=jax.ShapeDtypeStruct((len(blocks) * rows, columns), jnp.float32),
        grid_spec=pltpu.PrefetchScalarGridSpec(
            num_scalar_prefetch=1,
            grid=(len(blocks),),
            in_specs=[pl.BlockSpec((rows, columns), lambda at, turn: (0, 0)) for _ in blocks],
            out_specs=pl.BlockSpec((rows, columns), lambda at, turn: (at ^ turn[0], 0)),
        ),
        compiler_params=PARAMS,
    )(me[None], *blocks)


def paired(block, step):
    return lax.ppermute(block, "dp", [(at, at ^ step) for at in range(lax.axis_size("dp"))])


def gather_eight(block):
    half = block.shape[0] // 2
    two, four = paired(block, 2), paired(block, 4)
    one = paired(block, 1)
    six = jnp.concatenate([paired(four[:half], 2), paired(two[half:], 4)])
    return [block, one, two, paired(two, 1), four, paired(four, 1), six, paired(six, 1)]


def contract_first(left_rows, right_rows):
    return lax.dot_general(
        left_rows, right_rows, (((0,), (0,)), ((), ())), preferred_element_type=jnp.float32
    )


def contract_last(left_rows, right_rows):
    return lax.dot_general(
        left_rows, right_rows, (((1,), (1,)), ((), ())), preferred_element_type=jnp.float32
    )


def low(values):
    return values.astype(jnp.bfloat16)


def wide(values):
    return values.astype(jnp.float32)


def shifted(block, step):
    count = lax.axis_size("sp")
    return lax.ppermute(block, "sp", [(at, (at + step) % count) for at in range(count)])


def gather_pieces(block):
    return [block] + [shifted(block, step) for step in range(1, lax.axis_size("sp"))]


def sum_pieces(pieces):
    total = wide(pieces[0])
    for step in range(1, lax.axis_size("sp")):
        total = total + wide(shifted(low(pieces[step]), -step))
    return total


def sum_rows_dp(values):
    count = lax.axis_size("dp")
    step = 1
    while step < count:
        values = values + lax.ppermute(values, "dp", [(at, at ^ step) for at in range(count)])
        step *= 2
    return values


def shards(
    features,
    logit_grad,
    segment_ids,
    conv_weight,
    conv_bias,
    w_qkv,
    qv_bias,
    w_out,
    w_up,
    ffn_bias,
    w_down,
    out_biases,
    gains,
    shifts,
    ctc_weight,
    ctc_bias,
):
    ranks = lax.axis_size("sp")
    me = lax.axis_index("sp")
    signal = features[0]
    frames, model_width = signal.shape
    segments = segment_ids[0]
    length = segments.shape[0]
    local_width = model_width // ranks
    kernel_width = conv_weight.shape[2]
    group_size = conv_weight.shape[1]
    heads_here = local_width // HD
    score_scale = HD ** (-0.5)
    seg_col = segments[:, None]
    taps = tap_rows(conv_weight)
    rows_count = lax.axis_size("dp")
    part_width = local_width // rows_count
    split_rows = rows_count == 8 and part_width % 16 == 0 and group_size % part_width == 0
    owners = [(me - step) % ranks for step in range(ranks)]
    seg_here = jnp.concatenate([lax.dynamic_slice_in_dim(segments, owner * frames, frames) for owner in owners])

    grouped = lax.all_to_all(signal, "sp", split_axis=1, concat_axis=0, tiled=True)
    activated, conv_slope, wide_rows = conv_forward(grouped, seg_col, taps, conv_bias[None], group_size, kernel_width)
    if split_rows:
        wide_all = lax.all_to_all(jnp.repeat(wide_rows, group_size // part_width, axis=0), "dp", 0, 0)
    back_frames = lax.all_to_all(activated, "sp", split_axis=0, concat_axis=1, tiled=True)
    first_sum = wide(signal) + wide(back_frames)
    normed, norm_one_pull = jax.vjp(norm_rows, first_sum, gains[0], shifts[0])
    normed_pieces = gather_pieces(low(normed))
    qkv_flat = w_qkv.reshape(model_width, 3 * local_width)
    joined = jnp.concatenate(
        [jnp.dot(piece, qkv_flat, preferred_element_type=jnp.float32) for piece in normed_pieces]
    )
    queries = low(joined[:, :local_width] + qv_bias[0]).reshape(length, heads_here, HD)
    key_rows = low(joined[:, local_width : 2 * local_width]).reshape(length, heads_here, HD)
    value_rows = low(joined[:, 2 * local_width :] + qv_bias[1]).reshape(length, heads_here, HD)
    same = seg_here[:, None] == seg_here[None, :]

    scores = jnp.einsum("qhd,khd->hqk", queries, key_rows, preferred_element_type=jnp.float32) * score_scale
    scores = jnp.where(same[None], scores, NEG)
    weights = jnp.exp(scores - jnp.max(scores, axis=-1, keepdims=True))
    probs_low = low(weights / jnp.sum(weights, axis=-1, keepdims=True))
    mixed_heads = low(
        jnp.einsum("hqk,khd->qhd", probs_low, value_rows, preferred_element_type=jnp.float32)
    ).reshape(length, local_width)
    attn_part = sum_pieces(
        [
            jnp.dot(mixed_heads[frames * step : frames * (step + 1)], w_out, preferred_element_type=jnp.float32)
            for step in range(ranks)
        ]
    )
    second_sum = first_sum + attn_part + out_biases[0]
    normed_two, norm_two_pull = jax.vjp(norm_rows, second_sum, gains[1], shifts[1])
    ffn_pieces = gather_pieces(low(normed_two))
    active_pieces, gelu_slopes, down_parts = [], [], []
    for piece in ffn_pieces:
        hidden = jnp.dot(piece, w_up, preferred_element_type=jnp.float32) + ffn_bias
        share = 0.5 * (1.0 + lax.erf(hidden * (0.5**0.5)))
        gelu_slopes.append(share + hidden * jnp.exp(-0.5 * hidden * hidden) * 0.3989422804014327)
        active_pieces.append(low(hidden * share))
        down_parts.append(jnp.dot(active_pieces[-1], w_down, preferred_element_type=jnp.float32))
    third_sum = second_sum + sum_pieces(down_parts) + out_biases[1]
    final_norm, norm_final_pull = jax.vjp(norm_rows, third_sum, gains[2], shifts[2])
    final_low = low(final_norm)
    cotangent = logit_grad[0]
    final_grad = contract_last(cotangent, ctc_weight)
    third_grad, final_gain_grad, final_shift_grad = norm_final_pull(final_grad)
    down_pieces = gather_pieces(low(third_grad))
    hidden_pieces, up_parts = [], []
    for piece, slope in zip(down_pieces, gelu_slopes):
        hidden_pieces.append(low(contract_last(piece, w_down) * slope))
        up_parts.append(contract_last(hidden_pieces[-1], w_up))
    normed_two_grad = sum_pieces(up_parts)
    logits = jnp.dot(final_low, ctc_weight, preferred_element_type=jnp.float32) + ctc_bias
    ctc_weight_grad = contract_first(final_low, cotangent)
    ctc_bias_grad = jnp.sum(wide(cotangent), axis=0)
    down_full = jnp.concatenate(down_pieces)
    hidden_full = jnp.concatenate(hidden_pieces)
    down_grad = contract_first(jnp.concatenate(active_pieces), down_full)
    up_grad = contract_first(jnp.concatenate(ffn_pieces), hidden_full)
    down_bias_grad = jnp.sum(wide(down_full), axis=0)
    ffn_bias_grad = jnp.sum(wide(hidden_full), axis=0)
    up_sum, down_sum = lax.psum((low(up_grad), low(down_grad)), "dp")

    second_part, gain_two_grad, shift_two_grad = norm_two_pull(normed_two_grad)
    second_grad = third_grad + second_part
    out_pieces = gather_pieces(low(second_grad))
    mixed_grad = jnp.concatenate([low(contract_last(piece, w_out)) for piece in out_pieces])
    mixed_grad = mixed_grad.reshape(length, heads_here, HD)
    out_full = jnp.concatenate(out_pieces)
    out_grad = contract_first(mixed_heads, out_full)
    out_bias_grad = jnp.sum(wide(out_full), axis=0)

    probs = wide(probs_low)
    prob_grad = jnp.einsum("qhd,khd->hqk", mixed_grad, value_rows, preferred_element_type=jnp.float32)
    row_delta = jnp.sum(probs * prob_grad, axis=-1, keepdims=True)
    score_grad = low(probs * (prob_grad - row_delta))
    query_low = low(
        jnp.einsum("hqk,khd->qhd", score_grad, key_rows, preferred_element_type=jnp.float32) * score_scale
    ).reshape(length, local_width)
    key_low = low(
        jnp.einsum("hqk,qhd->khd", score_grad, queries, preferred_element_type=jnp.float32) * score_scale
    ).reshape(length, local_width)
    value_low = low(
        jnp.einsum("hqk,qhd->khd", probs_low, mixed_grad, preferred_element_type=jnp.float32)
    ).reshape(length, local_width)
    joined_grad = jnp.concatenate([query_low, key_low, value_low], axis=1)
    normed_grad = sum_pieces(
        [
            contract_last(joined_grad[frames * step : frames * (step + 1)], qkv_flat)
            for step in range(ranks)
        ]
    )
    qkv_grad = contract_first(jnp.concatenate(normed_pieces), joined_grad).reshape(model_width, 3, local_width)
    qv_bias_grad = jnp.stack([jnp.sum(wide(query_low), axis=0), jnp.sum(wide(value_low), axis=0)])

    first_part, gain_one_grad, shift_one_grad = norm_one_pull(normed_grad)
    first_grad = second_grad + first_part
    branch_groups = lax.all_to_all(low(first_grad), "sp", split_axis=1, concat_axis=0, tiled=True)
    qkv_sum, out_sum, up_sum, down_sum = lax.optimization_barrier(
        (low(qkv_grad), low(out_grad), up_sum, down_sum)
    )
    qkv_sum, out_sum = lax.psum((qkv_sum, out_sum), "dp")
    if split_rows:
        conv_low, low_parts, conv_bias_grad = conv_low_parts(
            branch_groups, conv_slope, seg_col, group_size, kernel_width, rows_count
        )
        conv_bias_grad = conv_bias_grad[0]
        low_rows = lax.all_to_all(low_parts, "dp", 0, 0)
        conv_part = split_weight_grad(wide_all, low_rows, group_size, kernel_width)
        conv_sum = unite_blocks(gather_eight(conv_part), lax.axis_index("dp"))
        conv_sum = conv_sum.reshape(local_width, group_size, kernel_width)
    else:
        conv_low = low(wide(branch_groups) * conv_slope)
        conv_bias_grad = jnp.sum(wide(conv_low), axis=0)
        conv_weight_grad = kernel_weight_grad(grouped, conv_low, seg_col, group_size, kernel_width)
        conv_sum = wide(lax.psum(conv_weight_grad, "dp"))
    signal_groups = conv_input_grad(conv_low, seg_col, taps, group_size, kernel_width)
    signal_back = lax.all_to_all(low(signal_groups), "sp", split_axis=0, concat_axis=1, tiled=True)
    feature_grad = first_grad + wide(signal_back)

    norm_parts = jnp.stack(
        [gain_one_grad, gain_two_grad, final_gain_grad, shift_one_grad, shift_two_grad, final_shift_grad]
    )
    letters = ctc_weight.shape[1]
    few = letters // ranks
    rank_rows = jnp.concatenate(
        [
            norm_parts.reshape(6, ranks, local_width).transpose(1, 0, 2).reshape(ranks, -1),
            ctc_weight_grad.reshape(ranks, -1),
            ctc_bias_grad.reshape(ranks, few),
        ],
        axis=1,
    )
    rank_pieces = [lax.dynamic_index_in_dim(rank_rows, owner, 0, keepdims=False) for owner in owners]
    rank_sum = sum_pieces(rank_pieces)
    small = jnp.concatenate(
        [rank_sum, conv_bias_grad, qv_bias_grad.reshape(-1), ffn_bias_grad, out_bias_grad, down_bias_grad]
    )
    spare = -small.shape[0] % 1024
    small = sum_rows_dp(jnp.pad(small, (0, spare)).reshape(-1, 1024)).reshape(-1)
    cuts, at = [], 0
    for size in (
        6 * local_width, local_width * letters, few, local_width, 2 * local_width, ffn_bias.shape[0], model_width, model_width,
    ):
        cuts.append(small[at : at + size])
        at += size
    norm_sums = cuts[0].reshape(2, 3, local_width)
    return (
        logits[None],
        feature_grad[None],
        conv_sum,
        cuts[3],
        wide(qkv_sum),
        cuts[4].reshape(2, local_width),
        wide(out_sum),
        wide(up_sum),
        cuts[5],
        wide(down_sum),
        jnp.stack([cuts[6], cuts[7]]),
        norm_sums[0],
        norm_sums[1],
        cuts[1].reshape(local_width, letters),
        cuts[2],
    )


def solution(mesh):
    in_specs = (
        P("dp", "sp", None),
        P("dp", "sp", None),
        P("dp", None),
        P("sp", None, None),
        P("sp"),
        P(None, None, "sp"),
        P(None, "sp"),
        P("sp", None),
        P(None, "sp"),
        P("sp"),
        P("sp", None),
        P(),
        P(),
        P(),
        P(),
        P(),
    )
    out_specs = (
        P("dp", "sp", None),
        P("dp", "sp", None),
        P("sp", None, None),
        P("sp"),
        P(None, None, "sp"),
        P(None, "sp"),
        P("sp", None),
        P(None, "sp"),
        P("sp"),
        P("sp", None),
        P(),
        P(None, "sp"),
        P(None, "sp"),
        P("sp", None),
        P("sp"),
    )
    return jax.shard_map(shards, mesh=mesh, in_specs=in_specs, out_specs=out_specs, check_vma=False)
```

```python
import functools

import jax
import jax.numpy as jnp
from jax import lax
from jax.experimental import pallas as pl
from jax.experimental.pallas import tpu as pltpu
from jax.sharding import PartitionSpec as P

HD = 64


EPS = 1e-05
NEG = -1e30


def norm_rows(values, gain, shift):
    center = values - jnp.mean(values, axis=-1, keepdims=True)
    spread = jnp.mean(center * center, axis=-1, keepdims=True)
    return center * lax.rsqrt(spread + EPS) * gain + shift


def gelu_exact(values):
    return jax.nn.gelu(values, approximate=False)


def contract_first(left_rows, right_rows):
    return lax.dot_general(
        left_rows, right_rows, (((0,), (0,)), ((), ())), preferred_element_type=jnp.float32
    )


def contract_last(left_rows, right_rows):
    return lax.dot_general(
        left_rows, right_rows, (((1,), (1,)), ((), ())), preferred_element_type=jnp.float32
    )


PH = 4
RB = 16


class Held:
    def __init__(self, far, near, semaphore, outward):
        self.near, self.waited, self.outward = near, False, outward
        self.copy = pltpu.make_async_copy(near, far, semaphore) if outward else pltpu.make_async_copy(far, near, semaphore)
        self.started = False

    def start(self):
        if not self.started:
            self.copy.start()
            self.started = True

    def ready(self):
        if not self.outward and not self.waited:
            self.copy.wait()
            self.waited = True
        return self.near

    def finish(self):
        self.start()
        if not self.waited:
            self.copy.wait()
            self.waited = True

    def __getitem__(self, index):
        return self.ready()[index]

    def __setitem__(self, index, value):
        self.near[index] = value

    @property
    def shape(self):
        return self.near.shape

    @property
    def dtype(self):
        return self.near.dtype

    @property
    def at(self):
        return self.ready().at


class Near:
    def __init__(self, ref):
        self.near, self.shape, self.dtype = ref, ref.shape, ref.dtype

    def start(self):
        pass

    def ready(self):
        return self.near

    def __getitem__(self, index):
        return self.near[index]

    def __setitem__(self, index, value):
        self.near[index] = value

    @property
    def at(self):
        return self.near.at


class HeldParts:
    def __init__(self, far, near, semaphores):
        self.near = near
        self.copies = lambda at: pltpu.make_async_copy(far.at[at], near.at[at], semaphores.at[at])
        for at in range(near.shape[0]):
            self.copies(at).start()

    def ready(self, at):
        self.copies(at).wait()
        return self.near

    @property
    def shape(self):
        return self.near.shape


def held_call(body, outs, arrays, scratch, params, cost, scalars=0, parts=(), far=True):
    kinds = []
    for at, array in enumerate(arrays):
        kinds.append("scalar" if at < scalars else "parts" if at in parts else "far" if far else "near")
    out_kinds = ["far" if far else "near" for _ in outs]
    specs = {
        "scalar": pl.BlockSpec(memory_space=pltpu.SMEM),
        "parts": pl.BlockSpec(memory_space=pltpu.HBM),
        "far": pl.BlockSpec(memory_space=pltpu.HBM),
        "near": pl.BlockSpec(memory_space=pltpu.VMEM),
    }
    shapes = list(arrays) + list(outs)
    moved = [at for at, kind in enumerate(kinds + out_kinds) if kind in ("far", "parts")]
    buffers = [pltpu.VMEM(shapes[at].shape, shapes[at].dtype) for at in moved]
    semaphores = [
        pltpu.SemaphoreType.DMA((shapes[at].shape[0],)) if at in parts else pltpu.SemaphoreType.DMA for at in moved
    ]
    count = len(shapes)

    def kernel(*refs):
        given, rest = list(refs[:count]), refs[count:]
        near, sems, own = rest[: len(moved)], rest[len(moved) : 2 * len(moved)], rest[2 * len(moved) :]
        held = []
        given = [Near(ref) if kind == "near" else ref for ref, kind in zip(given, kinds + out_kinds)]
        for at, buffer, semaphore in zip(moved, near, sems):
            if at in parts:
                given[at] = HeldParts(given[at], buffer, semaphore)
                continue
            given[at] = Held(given[at], buffer, semaphore, at >= len(arrays))
            held.append(given[at])
            if not given[at].outward:
                given[at].start()
        body(*given, *own)
        for item in held:
            item.finish()

    return pl.pallas_call(
        kernel,
        out_shape=tuple(outs),
        in_specs=[specs[kind] for kind in kinds],
        out_specs=tuple(specs[kind] for kind in out_kinds),
        scratch_shapes=buffers + semaphores + list(scratch),
        compiler_params=params,
        cost_estimate=cost,
    )(*arrays)


def swap_halves(even, odd):
    half = even.shape[1] // 2
    left = lax.broadcasted_iota(jnp.int32, even.shape, 1) < half
    return (
        jnp.where(left, even, pltpu.roll(odd, half, 1)),
        jnp.where(left, pltpu.roll(even, half, 1), odd),
    )


def split_segments(rows_ref, seg_ref, main_ref, side_ref):
    length, channels = rows_ref.shape
    pad = side_ref.shape[2] // 3
    seg = seg_ref[...]
    rows = rows_ref[...].astype(jnp.float32)
    middle = jnp.where(seg == 1, rows, 0.0)
    first = jnp.where(seg[:pad] == 0, rows[:pad], 0.0)
    last = jnp.where(seg[length - pad :] == 2, rows[length - pad :], 0.0)
    blank = jnp.zeros((pad, 128), jnp.float32)
    for tile in range(channels // 128):
        lanes = slice(128 * tile, 128 * tile + 128)
        main_ref[tile, 0:pad, :] = blank
        main_ref[tile, pad : pad + length, :] = middle[:, lanes]
        main_ref[tile, pad + length :, :] = blank
        for at, part in ((0, first), (1, last)):
            side_ref[at, tile, 0:pad, :] = blank
            side_ref[at, tile, pad : 2 * pad, :] = part[:, lanes]
            side_ref[at, tile, 2 * pad :, :] = blank


def phase_layout(main_ref, side_ref, main_out, side_out):
    tiles = main_ref.shape[0]
    pad = side_ref.shape[2] // 3
    stride = (main_ref.shape[1] - 2 * pad) // RB
    main_blocks = main_out.shape[1] // RB
    side_blocks = side_out.shape[1] // (2 * RB)

    def pack(load, store):
        for pair in range(PH // 2):
            for tile in range(tiles):
                both = swap_halves(load(tile, 2 * pair), load(tile, 2 * pair + 1))
                for at in range(2):
                    store(2 * tile + at, pair, both[at].astype(jnp.bfloat16))

    @pl.loop(0, main_blocks)
    def _(block):
        def load(tile, phase):
            return main_ref.at[tile][pl.ds(PH * block + phase, RB, stride=stride), :]

        def store(group, pair, value):
            main_out[group, pl.ds(pl.multiple_of(RB * block, RB), RB), 128 * pair : 128 * pair + 128] = value

        pack(load, store)

    @pl.loop(0, side_blocks)
    def _(block):
        for end in range(2):
            def load(tile, phase):
                return side_ref.at[end, tile][pl.ds(PH * block + phase, RB, stride=PH), :]

            def store(group, pair, value):
                at = pl.multiple_of(2 * RB * block + RB * end, RB)
                side_out[group, pl.ds(at, RB), 128 * pair : 128 * pair + 128] = value

            pack(load, store)


def frame_layout(sums_ref, main_ref, side_ref):
    tiles = main_ref.shape[0]
    length = main_ref.shape[1]
    blocks = length // (PH * RB)
    stride = length // RB
    for tile in range(tiles):
        for pair in range(PH // 2):
            lanes = slice(128 * pair, 128 * pair + 128)
            for block in range(blocks + 2):
                rows = slice(RB * block, RB * block + RB)
                both = swap_halves(sums_ref[2 * tile, rows, lanes], sums_ref[2 * tile + 1, rows, lanes])
                for at in range(2):
                    phase = 2 * pair + at
                    if block < blocks:
                        main_ref.at[tile][pl.ds(PH * block + phase, RB, stride=stride), :] = both[at]
                    else:
                        side_ref.at[block - blocks, tile][pl.ds(phase, RB, stride=PH), :] = both[at]


def join_segments(main_ref, side_ref, seg_ref):
    length = main_ref.shape[1]
    pad = side_ref.shape[2]
    seg = seg_ref[...]
    pieces = []
    for tile in range(main_ref.shape[0]):
        main = main_ref[tile]
        top = jnp.where(seg[:pad] == 0, side_ref[0, tile], main[:pad])
        low = jnp.where(seg[length - pad :] == 2, side_ref[1, tile], main[length - pad :])
        pieces.append(jnp.concatenate([top, main[pad : length - pad], low], axis=0))
    return jnp.concatenate(pieces, axis=1)


def tap_chunks(count):
    step = 11 if count % 11 == 0 else 1
    return [(at, step) for at in range(0, count, step)]


def fill_taps(rows_ref, group, taps_ref):
    count, size = rows_ref.shape[1:]
    step = min(1024, count)
    taps_ref[0:128, :] = jnp.zeros((128, 128), taps_ref.dtype)
    for at in range(0, count, step):
        now = rows_ref[group, at : at + step, :]
        if at:
            before = rows_ref[group, at - size : at - size + step, :]
        else:
            before = jnp.concatenate([jnp.zeros((size, size), now.dtype), rows_ref[group, 0 : step - size, :]], axis=0)
        taps_ref[128 + at : 128 + at + step, :] = jnp.concatenate([now, before], axis=1)
    last = rows_ref[group, count - size : count, :]
    taps_ref[128 + count : 128 + count + size, :] = jnp.concatenate([jnp.zeros_like(last), last], axis=1)
    taps_ref[128 + count + size :, :] = jnp.zeros((taps_ref.shape[0] - 128 - count - size, 128), taps_ref.dtype)


def phase_dot(main_in, side_in, rows_ref, taps_ref, sums_ref, turned):
    rows = sums_ref.shape[1] - 2 * RB
    width = main_in.shape[2]
    count = side_in.shape[1] // (2 * RB)

    @pl.loop(0, sums_ref.shape[0])
    def _(group):
        fill_taps(rows_ref.ready(group), group, taps_ref)
        total = jnp.zeros(sums_ref.shape[1:], jnp.float32)
        for first, step in tap_chunks(count):
            if turned:
                for d in range(first, first + step):
                    back = count - 1 - d
                    left = jnp.concatenate(
                        [main_in[group, RB * back : RB * back + rows, :], side_in[group, 2 * RB * back : 2 * RB * back + 2 * RB, :]], axis=0
                    )
                    right = jnp.concatenate(
                        [taps_ref[width * d + 128 : width * d + 128 + width, :], taps_ref[width * d : width * d + width, :]], axis=1
                    )
                    total += lax.dot_general(left, right, (((1,), (1,)), ((), ())), preferred_element_type=jnp.float32)
            else:
                left = jnp.concatenate(
                    [
                        jnp.concatenate(
                            [main_in[group, RB * d : RB * d + rows, :], side_in[group, 2 * RB * d : 2 * RB * d + 2 * RB, :]], axis=0
                        )
                        for d in range(first, first + step)
                    ],
                    axis=1,
                )
                low, high = width * first, width * (first + step)
                right = jnp.concatenate([taps_ref[low + 128 : high + 128, :], taps_ref[low:high, :]], axis=1)
                total += jnp.dot(left, right, preferred_element_type=jnp.float32)
        sums_ref[group] = total


def gelu_parts(values):
    share = 0.5 * (1.0 + lax.erf(values * (0.5**0.5)))
    slope = jnp.exp(-0.5 * values * values) * 0.3989422804014327
    return values * share, share + values * slope


def conv_forward_kernel(
    rows_ref, seg_ref, taps_ref, bias_ref, sum_ref, slope_ref, parts_ref,
    main_seq, side_seq, main_in, side_in, sums, taps_in, main_out, side_out,
):
    split_segments(rows_ref, seg_ref, main_seq, side_seq)

    copies = parts_ref.shape[0] * parts_ref.shape[2] // (WP * rows_ref.shape[1])

    def store(part, tile, value):
        for copy in range(copies):
            parts_ref[copies * part + copy, :, 128 * tile : 128 * tile + 128] = value

    phase_layout(main_seq, side_seq, main_in, side_in)
    pack_wide(main_seq, side_seq, parts_ref.shape[2] // WP, store)
    parts_ref.start()
    phase_dot(main_in, side_in, taps_ref, taps_in, sums, False)
    frame_layout(sums, main_out, side_out)
    conv_sum = join_segments(main_out, side_out, seg_ref) + bias_ref[...]
    value, slope = gelu_parts(conv_sum)
    branch = value.astype(jnp.bfloat16).astype(jnp.float32)
    sum_ref[...] = (rows_ref[...].astype(jnp.float32) + branch).astype(sum_ref.dtype)
    slope_ref[...] = slope.astype(slope_ref.dtype)


def conv_input_grad_kernel(
    rows_ref, seg_ref, taps_ref, first_ref, grad_ref,
    main_seq, side_seq, main_in, side_in, sums, taps_in, main_out, side_out,
):
    split_segments(rows_ref, seg_ref, main_seq, side_seq)
    phase_layout(main_seq, side_seq, main_in, side_in)
    phase_dot(main_in, side_in, taps_ref, taps_in, sums, True)
    frame_layout(sums, main_out, side_out)
    grad_ref[...] = (first_ref[...] + join_segments(main_out, side_out, seg_ref)).astype(grad_ref.dtype)


def scratch_of(length, channels, group, taps):
    pad = taps // 2
    groups = channels // group
    tiles = channels // 128
    count = taps // PH + 1
    main_rows = RB * (length // (PH * RB) + count - 1)
    return dict(
        main_seq=pltpu.VMEM((tiles, length + 2 * pad, 128), jnp.float32),
        side_seq=pltpu.VMEM((2, tiles, 3 * pad, 128), jnp.float32),
        main_in=pltpu.VMEM((groups, main_rows, PH * group), jnp.bfloat16),
        side_in=pltpu.VMEM((groups, 2 * RB * count, PH * group), jnp.bfloat16),
        sums=pltpu.VMEM((groups, length // PH + 2 * RB, PH * group), jnp.float32),
        taps=pltpu.VMEM((PH * group * (count + 1), 128), jnp.bfloat16),
        main_out=pltpu.VMEM((tiles, length, 128), jnp.float32),
        side_out=pltpu.VMEM((2, tiles, pad, 128), jnp.float32),
    )


PARAMS = pltpu.CompilerParams(vmem_limit_bytes=60 * 1024 * 1024)
SOME = pltpu.CompilerParams(vmem_limit_bytes=28 * 1024 * 1024)
FEW = pltpu.CompilerParams(vmem_limit_bytes=14 * 1024 * 1024)
WHOLE = pl.BlockSpec(memory_space=pltpu.VMEM)


def conv_forward(rows, seg_col, taps, bias, group, width, parts):
    length, channels = rows.shape
    flops = 2 * (length + 128) * channels * group * (width + 4)
    return held_call(
        conv_forward_kernel,
        (
            jax.ShapeDtypeStruct((length, channels), jnp.bfloat16),
            jax.ShapeDtypeStruct((length, channels), jnp.float32),
            jax.ShapeDtypeStruct((parts, (length + width) // WP, WP * group), jnp.bfloat16),
        ),
        (rows, seg_col, taps, bias),
        scratch_of(length, channels, group, width).values(),
        PARAMS,
        pl.CostEstimate(flops=flops, bytes_accessed=taps.size * 2, transcendentals=0),
        parts=(2,),
    )


def conv_input_grad(rows, seg_col, taps, first, group, width):
    length, channels = rows.shape
    flops = 2 * (length + 128) * channels * group * (width + 4)
    return held_call(
        conv_input_grad_kernel,
        (jax.ShapeDtypeStruct((length, channels), jnp.bfloat16),),
        (rows, seg_col, taps, first),
        scratch_of(length, channels, group, width).values(),
        PARAMS,
        pl.CostEstimate(flops=flops, bytes_accessed=taps.size * 2, transcendentals=0),
        parts=(2,),
    )[0]


def conv_weight_grad_kernel(
    rows_ref, low_ref, seg_ref, grad_ref,
    main_seq, side_seq, main_in, side_in, main_low, side_low, folded, turned,
):
    groups, _, width = main_in.shape
    count = side_in.shape[1] // (2 * RB)
    low_rows = low_ref.shape[0] // PH
    middle = (count - 1) // 2
    group_size = width // PH
    taps = PH * (count - 1)
    split_segments(low_ref, seg_ref, main_seq, side_seq)
    phase_layout(main_seq, side_seq, main_low, side_low)
    split_segments(rows_ref, seg_ref, main_seq, side_seq)
    phase_layout(main_seq, side_seq, main_in, side_in)
    left_lanes = lax.broadcasted_iota(jnp.int32, (taps, 128), 1) < group_size

    @pl.loop(0, groups)
    def _(group):
        right = jnp.concatenate(
            [
                main_low[group, RB * middle : RB * middle + low_rows, :],
                side_low[group, 2 * RB * middle : 2 * RB * middle + 2 * RB, :],
            ],
            axis=0,
        )
        folded[0:128, :] = jnp.zeros((128, 128), jnp.float32)
        for d in range(count):
            left = jnp.concatenate(
                [main_in[group, RB * d : RB * d + low_rows, :], side_in[group, 2 * RB * d : 2 * RB * d + 2 * RB, :]], axis=0
            )
            part = lax.dot_general(left, right, (((0,), (0,)), ((), ())), preferred_element_type=jnp.float32)
            folded[width * d + 128 : width * d + 128 + width, :] = part[:, 0:128]
            folded[width * d : width * d + width, :] += part[:, 128:256]

        @pl.loop(0, group_size // 8)
        def _(chunk):
            for at in range(8):
                channel = 8 * chunk + at
                now = folded[pl.ds(128 + channel, taps, stride=group_size), :]
                later = folded[pl.ds(128 + group_size + channel, taps, stride=group_size), :]
                both = jnp.where(left_lanes, now, later).T
                turned[pl.ds(channel, group_size, stride=group_size), :] = both[0:group_size] + both[group_size:]

        grad_ref[pl.ds(pl.multiple_of(group * group_size * group_size, 128), group_size * group_size), :] = turned[...].astype(grad_ref.dtype)


def kernel_weight_grad(rows, low, seg_col, group, width):
    length, channels = rows.shape
    flops = 2 * (length + 128) * channels * group * (width + 4)
    shapes = scratch_of(length, channels, group, width)
    count = width // PH + 1
    names = ["main_seq", "side_seq", "main_in", "side_in", "main_in", "side_in"]
    out = pl.pallas_call(
        conv_weight_grad_kernel,
        out_shape=jax.ShapeDtypeStruct((channels * group, width), jnp.bfloat16),
        in_specs=[WHOLE] * 3,
        out_specs=WHOLE,
        scratch_shapes=[shapes[n] for n in names]
        + [
            pltpu.VMEM((PH * group * count + 128, 128), jnp.float32),
            pltpu.VMEM((group * group, width), jnp.float32),
        ],
        compiler_params=PARAMS,
        cost_estimate=pl.CostEstimate(flops=flops, bytes_accessed=channels * group * width * 2, transcendentals=0),
    )(rows, low, seg_col)
    return out.reshape(channels, group, width)


def tap_rows(kernel):
    channels, group, width = kernel.shape
    groups = channels // group
    return kernel.reshape(groups, group, group, width).transpose(0, 3, 2, 1).reshape(groups, width * group, group)


WP = 8


def pack_wide(main_ref, side_ref, channels_each, store):
    tiles = main_ref.shape[0]
    pad = side_ref.shape[2] // 3
    rows = (main_ref.shape[1] - 2 * pad) // WP
    ends = pad // WP
    per = 128 // channels_each
    lane = lax.broadcasted_iota(jnp.int32, (rows + 2 * ends, 128), 1) // channels_each
    for tile in range(tiles):
        for group in range(WP // per):
            loads = []
            for at in range(per):
                phase = per * group + at
                loads.append(
                    jnp.concatenate(
                        [main_ref.at[tile][pl.ds(pad + phase, rows, stride=WP), :]]
                        + [side_ref.at[end, tile][pl.ds(pad + phase, ends, stride=WP), :] for end in range(2)],
                        axis=0,
                    )
                )
            for part in range(per):
                value = loads[0] if part == 0 else pltpu.roll(loads[0], (128 - channels_each * part) % 128, 1)
                for at in range(1, per):
                    turn = (channels_each * (at - part)) % 128
                    moved = loads[at] if turn == 0 else pltpu.roll(loads[at], turn, 1)
                    value = jnp.where(lane == at, moved, value)
                store(per * tile + part, group, value.astype(jnp.bfloat16))


def norm_back_kernel(
    ranks, model_width, me_ref, unit_ref, scale_ref, gain_ref, slope_ref, seg_ref, *refs
):
    blocks, seconds = refs[:ranks], refs[ranks : 2 * ranks]
    first_ref, low_ref, parts_ref, sums_ref, main_seq, side_seq = refs[2 * ranks :]
    length, channels = slope_ref.shape
    me = me_ref[0]
    frames = length // ranks
    for at, piece in enumerate(seconds):
        block = (me + at) % ranks
        first_ref[pl.ds(pl.multiple_of(block * frames, frames), frames), :] = piece[...].astype(jnp.float32)
    total = blocks[0][...].astype(jnp.float32)
    for block in blocks[1:]:
        total = total + block[...].astype(jnp.float32)
    grad, tail = total[:length], total[length:]
    spans = length // channels
    rows = [
        jnp.concatenate([tail[spans * at + span : spans * at + span + 1] for span in range(spans)], axis=1)
        for at in range(2)
    ]
    columns = jnp.concatenate(rows + [jnp.zeros((6, length), jnp.float32)], axis=0).T * (1.0 / model_width)
    unit = unit_ref[me].astype(jnp.float32)
    scaled = grad * gain_ref[me]
    first = first_ref.near[...] + (scaled - columns[:, 0:1] - unit * columns[:, 1:2]) * scale_ref[...]
    first_ref[...] = first
    low = (first.astype(jnp.bfloat16).astype(jnp.float32) * slope_ref[...]).astype(jnp.bfloat16)
    low_ref[...] = low
    first_ref.start()
    low_ref.start()
    sums_ref[0:1] = jnp.sum(low.astype(jnp.float32), axis=0, keepdims=True)
    sums_ref[1:2] = jnp.sum(grad * unit, axis=0, keepdims=True)
    sums_ref[2:3] = jnp.sum(grad, axis=0, keepdims=True)
    if parts_ref is None:
        return
    split_segments(low_ref.near, seg_ref, main_seq, side_seq)

    def store(part, tile, value):
        parts_ref[part, :, 128 * tile : 128 * tile + 128] = value

    pack_wide(main_seq, side_seq, parts_ref.shape[2] // WP, store)


def norm_back(me, unit, scale, gain, slope, seg_col, blocks, seconds, width, group, parts):
    length, channels = slope.shape
    ranks = len(blocks)
    shapes = scratch_of(length, channels, group, width)
    outs = [
        jax.ShapeDtypeStruct((length, channels), jnp.float32),
        jax.ShapeDtypeStruct((length, channels), jnp.bfloat16),
        jax.ShapeDtypeStruct((3, channels), jnp.float32),
    ]
    scratch = []
    body = functools.partial(norm_back_kernel, ranks, channels * ranks)
    if parts:
        outs.insert(2, jax.ShapeDtypeStruct((parts, (length + width) // WP, WP * (channels // parts)), jnp.bfloat16))
        scratch = [shapes["main_seq"], shapes["side_seq"]]
        kernel = body
    else:

        def kernel(*refs):
            body(*refs[:-1], None, refs[-1], None, None)

    result = held_call(
        kernel,
        outs,
        (me[None], unit, scale, gain, slope, seg_col, *blocks, *seconds),
        scratch,
        FEW,
        pl.CostEstimate(flops=30 * length * channels, bytes_accessed=16 * length * channels, transcendentals=0),
        scalars=1,
        far=False,
    )
    return result if parts else (result[0], result[1], None, result[2])


def attention_kernel(
    ranks, me_ref, gain_ref, shift_ref, weight_ref, bias_ref, seg_col_ref, seg_row_ref, *refs
):
    pieces = refs[:ranks]
    mixed_ref, qkv_ref, probs_ref, normed_ref, unit_ref, scale_ref, here_ref = refs[ranks : ranks + 7]
    parts, held = refs[ranks + 7 : -1], refs[-1]
    length, width = mixed_ref.shape
    frames = here_ref.shape[0]
    me = me_ref[0]
    step = min(64, length)
    for at, piece in enumerate(pieces):
        held[(me + (ranks - at)) % ranks] = piece[...]
    for at in range(ranks):
        here_ref[:, width * at : width * (at + 1)] = held[at, pl.ds(pl.multiple_of(me * frames, frames), frames), :]

    gain, shift = gain_ref[...], shift_ref[...]

    @pl.loop(0, length // step)
    def _(chunk):
        rows = pl.ds(pl.multiple_of(chunk * step, step), step)
        values = jnp.concatenate([held[at, rows, :] for at in range(ranks)], axis=1).astype(jnp.float32)
        center = values - jnp.mean(values, axis=1, keepdims=True)
        scale = lax.rsqrt(jnp.mean(center * center, axis=1, keepdims=True) + EPS)
        unit = center * scale
        scale_ref[rows, :] = scale
        normed_ref[rows, :] = (unit * gain + shift).astype(jnp.bfloat16)
        unit = unit.astype(jnp.bfloat16)
        for at in range(ranks):
            unit_ref.near[at, rows, :] = unit[:, width * at : width * (at + 1)]

    here_ref.start()
    unit_ref.start()
    normed_ref.start()
    normed = normed_ref.near[...]
    for at in range(3):
        value = jnp.dot(normed, weight_ref[at], preferred_element_type=jnp.float32)
        if at != 1:
            value = value + bias_ref[at // 2 : at // 2 + 1]
        qkv_ref[at] = value.astype(jnp.bfloat16)
    qkv_ref.start()
    qkv_ref = qkv_ref.near
    rows = min(256, length)
    for at in range(0, length, rows):
        same = seg_col_ref[at : at + rows] == seg_row_ref[...]
        result = []
        for head in range(width // HD):
            lanes = slice(HD * head, HD * (head + 1))
            scores = lax.dot_general(
                qkv_ref[0, at : at + rows, lanes], qkv_ref[1, :, lanes], (((1,), (1,)), ((), ())), preferred_element_type=jnp.float32
            )
            scores = jnp.where(same, scores * HD**-0.5, NEG)
            weights = jnp.exp(scores - jnp.max(scores, axis=1, keepdims=True))
            probs = (weights * (1.0 / jnp.sum(weights, axis=1, keepdims=True))).astype(jnp.bfloat16)
            probs_ref[head, at : at + rows, :] = probs
            result.append(jnp.dot(probs, qkv_ref[2, :, lanes], preferred_element_type=jnp.float32))
        mixed_ref[at : at + rows, :] = jnp.concatenate(result, axis=1).astype(jnp.bfloat16)
    for at, part in enumerate(parts):
        block = (me + (ranks - at)) % ranks
        part[...] = mixed_ref.near[pl.ds(pl.multiple_of(block * frames, frames), frames), :]
        part.start()


def attention(me, gain, shift, weight, bias, seg_col, seg_row, pieces, frames):
    ranks = len(pieces)
    length, width = pieces[0].shape
    heads = width // HD
    model = ranks * width
    flops = 2 * length * (3 * model * width + 2 * length * width)
    return held_call(
        functools.partial(attention_kernel, ranks),
        (
            jax.ShapeDtypeStruct((length, width), jnp.bfloat16),
            jax.ShapeDtypeStruct((3, length, width), jnp.bfloat16),
            jax.ShapeDtypeStruct((heads, length, length), jnp.bfloat16),
            jax.ShapeDtypeStruct((length, model), jnp.bfloat16),
            jax.ShapeDtypeStruct((ranks, length, width), jnp.bfloat16),
            jax.ShapeDtypeStruct((length, 1), jnp.float32),
            jax.ShapeDtypeStruct((frames, model), jnp.bfloat16),
        )
        + tuple(jax.ShapeDtypeStruct((frames, width), jnp.bfloat16) for _ in range(ranks)),
        (me[None], gain, shift, weight, bias, seg_col, seg_row, *pieces),
        [pltpu.VMEM((ranks, length, width), jnp.bfloat16)],
        PARAMS,
        pl.CostEstimate(flops=flops, bytes_accessed=8 * length * model, transcendentals=heads * length * length),
        scalars=1,
    )


def attention_back_kernel(
    ranks, me_ref, qkv_ref, probs_ref, unit_ref, gain_ref, weight_ref, *refs
):
    pieces, (joined_ref, bias_ref) = refs[:ranks], refs[ranks : ranks + 2]
    outs, (cot_ref, key_sum, value_sum) = refs[ranks + 2 : 2 * ranks + 2], refs[2 * ranks + 2 :]
    length, width = cot_ref.shape
    me = me_ref[0]
    frames = length // ranks
    for at, piece in enumerate(pieces):
        block = (me + at) % ranks
        cot_ref[pl.ds(pl.multiple_of(block * frames, frames), frames), :] = piece[...]
    rows = min(256, length)
    for at in range(0, length, rows):
        queries = []
        for head in range(width // HD):
            lanes = slice(HD * head, HD * (head + 1))
            cot = cot_ref[at : at + rows, lanes]
            probs = probs_ref[head, at : at + rows, :]
            probs_wide = probs.astype(jnp.float32)
            grad = lax.dot_general(cot, qkv_ref[2, :, lanes], (((1,), (1,)), ((), ())), preferred_element_type=jnp.float32)
            delta = jnp.sum(probs_wide * grad, axis=1, keepdims=True)
            score = (probs_wide * (grad - delta)).astype(jnp.bfloat16)
            queries.append(jnp.dot(score, qkv_ref[1, :, lanes], preferred_element_type=jnp.float32))
            keys = contract_first(score, qkv_ref[0, at : at + rows, lanes])
            values = contract_first(probs, cot)
            if at:
                key_sum[head] += keys
                value_sum[head] += values
            else:
                key_sum[head] = keys
                value_sum[head] = values
        joined_ref[at : at + rows, 0:width] = (jnp.concatenate(queries, axis=1) * HD**-0.5).astype(jnp.bfloat16)
    heads = width // HD
    joined_ref[:, width : 2 * width] = (
        jnp.concatenate([key_sum[head] for head in range(heads)], axis=1) * HD**-0.5
    ).astype(jnp.bfloat16)
    joined_ref[:, 2 * width :] = jnp.concatenate([value_sum[head] for head in range(heads)], axis=1).astype(jnp.bfloat16)
    joined_ref.start()
    joined_ref = joined_ref.near
    bias_ref[0:1] = jnp.sum(joined_ref[:, 0:width].astype(jnp.float32), axis=0, keepdims=True)
    bias_ref[1:2] = jnp.sum(joined_ref[:, 2 * width :].astype(jnp.float32), axis=0, keepdims=True)
    plain = jnp.zeros((length, width), jnp.float32)
    along = jnp.zeros((length, width), jnp.float32)
    for at, out in enumerate(outs):
        block = (me + (ranks - at)) % ranks
        span = pl.ds(pl.multiple_of(block * width, width), width)
        part = jnp.zeros((length, width), jnp.float32)
        for which in range(3):
            part += contract_last(joined_ref[:, width * which : width * (which + 1)], weight_ref[which, span, :])
        out[0:length, :] = part.astype(jnp.bfloat16)
        scaled = part * gain_ref[block]
        plain += scaled
        along += scaled * unit_ref[block].astype(jnp.float32)
    ones = jnp.ones((8, width), jnp.bfloat16)
    sums = [contract_last(ones, value.astype(jnp.bfloat16))[0:1] for value in (plain, along)]
    spans = length // width
    tail = [value[:, width * span : width * (span + 1)] for value in sums for span in range(spans)]
    tail = jnp.concatenate(tail + [jnp.zeros((16 - 2 * spans, width), jnp.float32)] * (2 * spans < 16), axis=0)
    for out in outs:
        out[length:, :] = tail.astype(jnp.bfloat16)


def attention_back(me, qkv, probs, unit, gain, weight, pieces):
    ranks, length, width = unit.shape
    heads = width // HD
    flops = 2 * length * (3 * ranks * width * width + 5 * length * width)
    return held_call(
        functools.partial(attention_back_kernel, ranks),
        (
            jax.ShapeDtypeStruct((length, 3 * width), jnp.bfloat16),
            jax.ShapeDtypeStruct((2, width), jnp.float32),
        )
        + tuple(jax.ShapeDtypeStruct((length + 16, width), jnp.bfloat16) for _ in range(ranks)),
        (me[None], qkv, probs, unit, gain, weight, *pieces),
        [pltpu.VMEM((length, width), jnp.bfloat16)] + [pltpu.VMEM((heads, length, HD), jnp.float32)] * 2,
        PARAMS,
        pl.CostEstimate(flops=flops, bytes_accessed=8 * length * ranks * width, transcendentals=0),
        scalars=1,
    )


def split_weight_grad_kernel(
    rows_ref, low_ref, grad_ref, seq, side_seq, main_in, side_in, low_seq, low_all, even, odd, turned, final,
):
    batch, packed, wide = rows_ref.shape
    low_width = low_ref.shape[2]
    each = low_width // WP
    group = wide // WP
    count = side_in.shape[1] // RB
    ends = (count - 1) // 2
    main_rows = packed - 2 * ends
    blocks = main_rows // RB
    taps = WP * (count - 1)

    rows_ref, low_ref = rows_ref.ready(), low_ref.ready()

    @pl.loop(0, batch)
    def _(row):
        for tile in range(wide // 128):
            lanes = slice(128 * tile, 128 * tile + 128)
            values = rows_ref[row, :, lanes].astype(jnp.float32)
            blank = jnp.zeros((ends, 128), jnp.float32)
            seq[tile] = jnp.concatenate([blank, values[:main_rows], blank], axis=0)
            for end in range(2):
                side_seq[tile, end] = jnp.concatenate(
                    [blank, values[main_rows + ends * end : main_rows + ends * (end + 1)], blank], axis=0
                )
            for block in range(blocks + count - 1):
                main_in[row, RB * block : RB * block + RB, lanes] = seq.at[tile][pl.ds(block, RB, stride=blocks), :].astype(jnp.bfloat16)
            for d in range(count):
                side_in[row, RB * d : RB * d + RB, lanes] = jnp.concatenate(
                    [side_seq[tile, 0, d : d + ends, :], side_seq[tile, 1, d : d + ends, :]], axis=0
                ).astype(jnp.bfloat16)
        for tile in range(low_width // 128):
            lanes = slice(128 * tile, 128 * tile + 128)
            low_seq[tile] = low_ref[row, :, lanes].astype(jnp.float32)
            for block in range(blocks):
                low_all[row, RB * block : RB * block + RB, lanes] = low_seq.at[tile][pl.ds(block, RB, stride=blocks), :].astype(jnp.bfloat16)
            low_all[row, main_rows:packed, lanes] = low_ref[row, main_rows:packed, lanes]

    left = jnp.concatenate([low_all[row] for row in range(batch)], axis=0).T
    even[...] = jnp.zeros(even.shape, jnp.float32)
    odd[...] = jnp.zeros(odd.shape, jnp.float32)

    @pl.loop(0, count)
    def _(d):
        at = pl.multiple_of(RB * d, RB)
        right = jnp.concatenate(
            [
                part
                for row in range(batch)
                for part in (main_in[row, pl.ds(at, main_rows), :], side_in[row, pl.ds(at, RB), :])
            ],
            axis=0,
        )
        part = jnp.dot(left, right, preferred_element_type=jnp.float32)
        for phase in range(WP):
            held = even if phase % 2 == 0 else odd
            lanes = pl.ds(pl.multiple_of(wide * d + wide - group * (phase - phase % 2), 128), wide)
            held[:, lanes] += part[each * phase : each * (phase + 1), :]

    left_lanes = lax.broadcasted_iota(jnp.int32, (each, 128), 1) < group
    for tile in range(taps * group // 128):
        at = wide + 128 * tile
        near, far = odd[:, at : at + 128], odd[:, at + 128 : at + 256]
        value = even[:, at : at + 128] + jnp.where(left_lanes, pltpu.roll(near, group, 1), pltpu.roll(far, group, 1))
        turned[128 * tile : 128 * tile + 128, 0:each] = value.T

    @pl.loop(0, group // 8)
    def _(chunk):
        for at in range(8):
            channel = 8 * chunk + at
            final[pl.ds(channel, each, stride=group), :] = turned[pl.ds(channel, taps, stride=group), :].T[0:each, :]

    grad_ref[...] = final[...].astype(grad_ref.dtype)


def split_weight_grad(rows, low, group, width):
    batch, packed, wide = rows.shape
    each = low.shape[2] // WP
    count = width // WP + 1
    ends = (count - 1) // 2
    main_rows = packed - 2 * ends
    blocks = main_rows // RB
    flops = 2 * batch * packed * low.shape[2] * wide * count
    (out,) = held_call(
        split_weight_grad_kernel,
        (jax.ShapeDtypeStruct((each * group, width), jnp.bfloat16),),
        (rows, low),
        [
            pltpu.VMEM((wide // 128, main_rows + 2 * ends, 128), jnp.float32),
            pltpu.VMEM((wide // 128, 2, 3 * ends, 128), jnp.float32),
            pltpu.VMEM((batch, RB * (blocks + count - 1), wide), jnp.bfloat16),
            pltpu.VMEM((batch, RB * count, wide), jnp.bfloat16),
            pltpu.VMEM((low.shape[2] // 128, packed, 128), jnp.float32),
            pltpu.VMEM((batch, packed, low.shape[2]), jnp.bfloat16),
            pltpu.VMEM((each, wide * (count + 1)), jnp.float32),
            pltpu.VMEM((each, wide * (count + 1)), jnp.float32),
            pltpu.VMEM((width * group, 128), jnp.float32),
            pltpu.VMEM((each * group, width), jnp.float32),
        ],
        SOME,
        pl.CostEstimate(flops=flops, bytes_accessed=2 * (rows.size + low.size), transcendentals=0),
        far=False,
    )
    return out


def centered(values):
    center = values - jnp.mean(values, axis=1, keepdims=True)
    scale = lax.rsqrt(jnp.mean(center * center, axis=1, keepdims=True) + EPS)
    return center * scale, scale


def norm_pull(grad, unit, scale, gain):
    scaled = grad * gain
    inner = scaled - jnp.mean(scaled, axis=1, keepdims=True) - unit * jnp.mean(scaled * unit, axis=1, keepdims=True)
    return inner * scale, jnp.sum(grad * unit, axis=0, keepdims=True), jnp.sum(grad, axis=0, keepdims=True)


def attention_sum_kernel(ranks, me_ref, weight_ref, here_ref, bias_ref, gain_ref, shift_ref, *refs):
    pieces, (sum_ref, normed_ref, unit_ref, scale_ref) = refs[:ranks], refs[ranks:]
    width = pieces[0].shape[1]
    total = here_ref[...].astype(jnp.float32) + bias_ref[...]
    for at, piece in enumerate(pieces):
        block = (me_ref[0] + at) % ranks
        rows = weight_ref[pl.ds(pl.multiple_of(block * width, width), width), :]
        total = total + jnp.dot(piece[...], rows, preferred_element_type=jnp.float32)
    unit, scale = centered(total)
    sum_ref[...] = total
    normed_ref[...] = (unit * gain_ref[...] + shift_ref[...]).astype(jnp.bfloat16)
    unit_ref[...] = unit
    scale_ref[...] = scale


def attention_sum(me, weight, here, bias, gain, shift, pieces):
    frames, model = here.shape
    ranks = len(pieces)
    return held_call(
        functools.partial(attention_sum_kernel, ranks),
        (
            jax.ShapeDtypeStruct((frames, model), jnp.float32),
            jax.ShapeDtypeStruct((frames, model), jnp.bfloat16),
            jax.ShapeDtypeStruct((frames, model), jnp.float32),
            jax.ShapeDtypeStruct((frames, 1), jnp.float32),
        ),
        (me[None], weight, here, bias, gain, shift, *pieces),
        [],
        FEW,
        pl.CostEstimate(flops=2 * frames * model * model, bytes_accessed=2 * model * model, transcendentals=0),
        scalars=1,
        far=False,
    )


def head_kernel(
    ranks, second_ref, bias_ref, gain_ref, shift_ref, weight_ref, letter_ref, cot_ref, *refs
):
    pieces = refs[:ranks]
    logits_ref, third_ref, low_ref, weight_grad_ref, letter_grad_ref, norm_ref = refs[ranks:]
    total = second_ref[...] + bias_ref[...]
    for piece in pieces:
        total = total + piece[...].astype(jnp.float32)
    unit, scale = centered(total)
    final = (unit * gain_ref[...] + shift_ref[...]).astype(jnp.bfloat16)
    cot = cot_ref[...]
    logits_ref[...] = jnp.dot(final, weight_ref[...], preferred_element_type=jnp.float32) + letter_ref[...]
    weight_grad_ref[...] = contract_first(cot, final)
    letter_grad_ref[...] = jnp.sum(cot.astype(jnp.float32), axis=0, keepdims=True)
    third, norm_ref[0:1], norm_ref[1:2] = norm_pull(contract_last(cot, weight_ref[...]), unit, scale, gain_ref[...])
    third_ref[...] = third
    low_ref[...] = third.astype(jnp.bfloat16)


def head(second, bias, gain, shift, weight, letter_bias, cotangent, pieces):
    frames, model = second.shape
    letters = weight.shape[1]
    return held_call(
        functools.partial(head_kernel, len(pieces)),
        (
            jax.ShapeDtypeStruct((frames, letters), jnp.float32),
            jax.ShapeDtypeStruct((frames, model), jnp.float32),
            jax.ShapeDtypeStruct((frames, model), jnp.bfloat16),
            jax.ShapeDtypeStruct((letters, model), jnp.float32),
            jax.ShapeDtypeStruct((1, letters), jnp.float32),
            jax.ShapeDtypeStruct((2, model), jnp.float32),
        ),
        (second, bias, gain, shift, weight, letter_bias, cotangent, *pieces),
        [],
        FEW,
        pl.CostEstimate(flops=6 * frames * model * letters, bytes_accessed=16 * frames * model, transcendentals=0),
        far=False,
    )


def second_back_kernel(ranks, me_ref, weight_ref, third_ref, unit_ref, scale_ref, gain_ref, *refs):
    pieces, (low_ref, norm_ref) = refs[:ranks], refs[ranks : ranks + 2]
    mixed, seconds, held = refs[ranks + 2 : 2 * ranks + 2], refs[2 * ranks + 2 : 3 * ranks + 2], refs[-1]
    width = mixed[0].shape[1]
    total = pieces[0][...].astype(jnp.float32)
    for piece in pieces[1:]:
        total = total + piece[...].astype(jnp.float32)
    grad, norm_ref[0:1], norm_ref[1:2] = norm_pull(total, unit_ref[...], scale_ref[...], gain_ref[...])
    low = (third_ref[...] + grad).astype(jnp.bfloat16)
    low_ref[...] = low
    for block in range(ranks):
        held[block] = low[:, width * block : width * (block + 1)]
    for at in range(ranks):
        block = (me_ref[0] + (ranks - at)) % ranks
        rows = weight_ref[pl.ds(pl.multiple_of(block * width, width), width), :]
        mixed[at][...] = contract_last(low, rows).astype(jnp.bfloat16)
        mixed[at].start()
        seconds[at][...] = held[block]


def second_back(me, weight, third, unit, scale, gain, pieces):
    frames, model = third.shape
    ranks = len(pieces)
    blocks = tuple(jax.ShapeDtypeStruct((frames, model // ranks), jnp.bfloat16) for _ in range(2 * ranks))
    result = held_call(
        functools.partial(second_back_kernel, ranks),
        (
            jax.ShapeDtypeStruct((frames, model), jnp.bfloat16),
            jax.ShapeDtypeStruct((2, model), jnp.float32),
        )
        + blocks,
        (me[None], weight, third, unit, scale, gain, *pieces),
        [pltpu.VMEM((ranks, frames, model // ranks), jnp.bfloat16)],
        PARAMS,
        pl.CostEstimate(flops=2 * frames * model * model, bytes_accessed=2 * model * model, transcendentals=0),
        scalars=1,
    )
    return result[0], result[1], result[2 : 2 + ranks], result[2 + ranks :]


def unite_kernel(turn_ref, *refs):
    blocks, out_ref = refs[:-1], refs[-1]
    for at, block in enumerate(blocks):

        @pl.when(pl.program_id(0) == at)
        def _():
            out_ref[...] = block[...].astype(jnp.float32)


def unite_blocks(blocks, me):
    rows, columns = blocks[0].shape
    return pl.pallas_call(
        unite_kernel,
        out_shape=jax.ShapeDtypeStruct((len(blocks) * rows, columns), jnp.float32),
        grid_spec=pltpu.PrefetchScalarGridSpec(
            num_scalar_prefetch=1,
            grid=(len(blocks),),
            in_specs=[pl.BlockSpec((rows, columns), lambda at, turn: (0, 0)) for _ in blocks],
            out_specs=pl.BlockSpec((rows, columns), lambda at, turn: (at ^ turn[0], 0)),
        ),
        compiler_params=PARAMS,
    )(me[None], *blocks)


def paired(block, step):
    return lax.ppermute(block, "dp", [(at, at ^ step) for at in range(lax.axis_size("dp"))])


def gather_eight(block):
    half = block.shape[0] // 2
    two, four = paired(block, 2), paired(block, 4)
    one = paired(block, 1)
    six = jnp.concatenate([paired(four[:half], 2), paired(two[half:], 4)])
    return [block, one, two, paired(two, 1), four, paired(four, 1), six, paired(six, 1)]


def low(values):
    return values.astype(jnp.bfloat16)


def wide(values):
    return values.astype(jnp.float32)


def shifted(block, step):
    count = lax.axis_size("sp")
    return lax.ppermute(block, "sp", [(at, (at + step) % count) for at in range(count)])


def gather_pieces(block):
    return [block] + [shifted(block, step) for step in range(1, lax.axis_size("sp"))]


def return_pieces(pieces):
    return [pieces[0]] + [shifted(pieces[step], -step) for step in range(1, lax.axis_size("sp"))]


def sum_pieces(pieces):
    total = wide(pieces[0])
    for step in range(1, lax.axis_size("sp")):
        total = total + wide(shifted(low(pieces[step]), -step))
    return total


def weight_grad_kernel(left_ref, right_ref, out_ref):
    width = out_ref.shape[2]
    left = left_ref[...]
    for at in range(out_ref.shape[0]):
        out_ref[at] = contract_first(left, right_ref[:, width * at : width * (at + 1)]).astype(out_ref.dtype)


def weight_grad(left, right, parts):
    width = right.shape[1] // parts
    return held_call(
        weight_grad_kernel,
        (jax.ShapeDtypeStruct((parts, left.shape[1], width), jnp.bfloat16),),
        (left, right),
        [],
        SOME,
        pl.CostEstimate(flops=2 * left.size * right.shape[1], bytes_accessed=2 * left.size, transcendentals=0),
    )[0]


def after(values, *others):
    return lax.optimization_barrier((values, others))[0]


def shards(
    features,
    logit_grad,
    segment_ids,
    conv_weight,
    conv_bias,
    w_qkv,
    qv_bias,
    w_out,
    w_up,
    ffn_bias,
    w_down,
    out_biases,
    gains,
    shifts,
    ctc_weight,
    ctc_bias,
):
    ranks = lax.axis_size("sp")
    me = lax.axis_index("sp")
    signal = features[0]
    frames, model_width = signal.shape
    segments = segment_ids[0]
    length = segments.shape[0]
    local_width = model_width // ranks
    kernel_width = conv_weight.shape[2]
    group_size = conv_weight.shape[1]
    seg_col, seg_row = segments[:, None], segments[None, :]
    rows_count = lax.axis_size("dp")
    row = lax.axis_index("dp")
    part_width = local_width // rows_count
    split_rows = rows_count == 8 and part_width % 16 == 0 and group_size % part_width == 0
    owners = [(me - step) % ranks for step in range(ranks)]
    taps = tap_rows(conv_weight)
    w_three = w_qkv.transpose(1, 0, 2)
    gain_blocks = gains[0].reshape(ranks, 1, local_width)
    out_share = w_out.shape[0] // rows_count
    w_out_full = lax.all_gather(
        lax.dynamic_slice_in_dim(w_out, row * out_share, out_share), ("sp", "dp"), axis=0, tiled=True
    )

    grouped = lax.all_to_all(signal, "sp", split_axis=1, concat_axis=0, tiled=True)
    first_low, conv_slope, wide_rows = conv_forward(
        grouped, seg_col, taps, conv_bias[None], group_size, kernel_width, rows_count if split_rows else local_width // group_size
    )
    first_pieces = gather_pieces(first_low)
    mixed_heads, qkv, probs_low, normed_full, unit_one, scale_one, first_here, *mixed_parts = attention(
        me, gains[0:1], shifts[0:1], w_three, qv_bias, seg_col, seg_row, first_pieces, frames
    )
    mixed_parts = return_pieces(mixed_parts)
    if split_rows:
        wide_all = lax.all_to_all(after(wide_rows, mixed_heads), "dp", 0, 0)
        mixed_parts = after(mixed_parts, wide_all)
    second_sum, normed_two, unit_two, scale_two = attention_sum(
        me, w_out_full, first_here, out_biases[0:1], gains[1:2], shifts[1:2], mixed_parts
    )
    ffn_pieces = gather_pieces(normed_two)
    active_pieces, gelu_slopes, down_parts = [], [], []
    for piece in ffn_pieces:
        if down_parts:
            piece = after(piece, down_parts[-1])
        hidden = jnp.dot(piece, w_up, preferred_element_type=jnp.float32) + ffn_bias
        share = 0.5 * (1.0 + lax.erf(hidden * (0.5**0.5)))
        gelu_slopes.append(share + hidden * jnp.exp(-0.5 * hidden * hidden) * 0.3989422804014327)
        active_pieces.append(low(hidden * share))
        down_parts.append(low(jnp.dot(active_pieces[-1], w_down, preferred_element_type=jnp.float32)))
    logits, third_grad, down_cot, ctc_weight_grad, ctc_bias_grad, final_norm_grads = head(
        second_sum, out_biases[1:2], gains[2:3], shifts[2:3], ctc_weight, ctc_bias[None], logit_grad[0], return_pieces(down_parts)
    )
    down_pieces = gather_pieces(down_cot)
    hidden_pieces, up_parts = [], []
    for piece, slope in zip(down_pieces, gelu_slopes):
        if up_parts:
            piece = after(piece, up_parts[-1])
        hidden_pieces.append(low(contract_last(piece, w_down) * slope))
        up_parts.append(low(contract_last(hidden_pieces[-1], w_up)))
    up_back = return_pieces(up_parts)
    down_full, hidden_full, _ = lax.optimization_barrier(
        (jnp.concatenate(down_pieces), jnp.concatenate(hidden_pieces), up_back[1])
    )
    down_grad = contract_first(jnp.concatenate(active_pieces), down_full)
    up_grad = contract_first(jnp.concatenate(ffn_pieces), hidden_full)
    ffn_bias_grad = jnp.sum(wide(hidden_full), axis=0)
    down_bias_grad = jnp.sum(wide(down_full), axis=0)
    up_low, down_low = low(up_grad), low(down_grad)
    up_back[2], up_low, down_low = lax.optimization_barrier((up_back[2], up_low, down_low))
    up_sum, down_sum = lax.psum((up_low, down_low), "dp")

    out_cot, second_norm_grads, mixed_back, second_blocks = second_back(
        me, w_out_full, third_grad, unit_two, scale_two, gains[1:2], up_back
    )
    mixed_pieces = return_pieces(mixed_back)
    second_groups = return_pieces(after(second_blocks, mixed_pieces))
    joined_grad, qv_bias_grad, *norm_blocks = attention_back(
        me, qkv, probs_low, unit_one, gain_blocks, w_three, mixed_pieces
    )
    norm_blocks = return_pieces(norm_blocks)
    qkv_low = weight_grad(normed_full, joined_grad, 3)
    norm_blocks[2], qkv_low = lax.optimization_barrier((norm_blocks[2], qkv_low))
    first_grad, conv_low, low_parts, channel_sums = norm_back(
        me, unit_one, scale_one, gain_blocks, conv_slope, seg_col, norm_blocks, second_groups,
        kernel_width, group_size, rows_count if split_rows else 0,
    )
    signal_groups = conv_input_grad(conv_low, seg_col, taps, first_grad, group_size, kernel_width)
    out_pieces = gather_pieces(after(out_cot, first_grad))
    out_full = jnp.zeros((ranks, frames, model_width), jnp.bfloat16)
    for owner, piece in zip(owners, out_pieces):
        out_full = lax.dynamic_update_index_in_dim(out_full, piece, owner, 0)
    out_full = out_full.reshape(length, model_width)
    out_low = low(contract_first(mixed_heads, out_full))
    out_bias_grad = jnp.sum(wide(out_full), axis=0)
    norm_parts = jnp.stack([second_norm_grads[0], final_norm_grads[0], second_norm_grads[1], final_norm_grads[1]])
    letters = ctc_weight.shape[1]
    few = letters // ranks
    rank_rows = jnp.concatenate(
        [
            norm_parts.reshape(4, ranks, local_width).transpose(1, 0, 2).reshape(ranks, -1),
            ctc_weight_grad.reshape(letters, ranks, local_width).transpose(1, 0, 2).reshape(ranks, -1),
            ctc_bias_grad.reshape(ranks, few),
        ],
        axis=1,
    )
    rank_rows = after(rank_rows, first_grad)
    rank_sum = sum_pieces([lax.dynamic_index_in_dim(rank_rows, owner, 0, keepdims=False) for owner in owners])
    small = jnp.concatenate(
        [rank_sum, channel_sums.reshape(-1), qv_bias_grad.reshape(-1), ffn_bias_grad, out_bias_grad, down_bias_grad]
    )
    small = low(jnp.pad(small, (0, -small.shape[0] % (16 * model_width))).reshape(-1, model_width))
    out_low = jnp.concatenate([out_low, small])
    qkv_low, out_low = after((qkv_low, out_low), up_sum, down_sum)
    qkv_sum, out_sum = lax.psum((qkv_low, out_low), "dp")
    if split_rows:
        low_rows = after(lax.all_to_all(low_parts, "dp", 0, 0), signal_groups, up_sum, down_sum, out_low)
        conv_part = split_weight_grad(wide_all, low_rows, group_size, kernel_width)
        conv_sum = unite_blocks(gather_eight(conv_part), row)
        conv_sum = conv_sum.reshape(local_width, group_size, kernel_width)
        signal_groups = after(signal_groups, conv_part)
        qkv_sum, out_sum = after((qkv_sum, out_sum), conv_sum)
    else:
        conv_weight_grad = kernel_weight_grad(grouped, conv_low, seg_col, group_size, kernel_width)
        conv_sum = wide(lax.psum(conv_weight_grad, "dp"))
    feature_grad = wide(lax.all_to_all(signal_groups, "sp", split_axis=0, concat_axis=1, tiled=True))

    small = wide(out_sum[local_width:]).reshape(-1)
    out_sum = out_sum[:local_width]
    cuts, at = [], 0
    for size in (
        4 * local_width, local_width * letters, few, 3 * local_width, 2 * local_width, ffn_bias.shape[0], model_width, model_width,
    ):
        cuts.append(small[at : at + size])
        at += size
    norm_sums = cuts[0].reshape(4, local_width)
    channel_sums = cuts[3].reshape(3, local_width)
    return (
        logits[None],
        feature_grad[None],
        conv_sum,
        channel_sums[0],
        wide(qkv_sum.transpose(1, 0, 2)),
        cuts[4].reshape(2, local_width),
        wide(out_sum),
        wide(up_sum),
        cuts[5],
        wide(down_sum),
        jnp.stack([cuts[6], cuts[7]]),
        jnp.stack([channel_sums[1], norm_sums[0], norm_sums[1]]),
        jnp.stack([channel_sums[2], norm_sums[2], norm_sums[3]]),
        cuts[1].reshape(letters, local_width).T,
        cuts[2],
    )


def solution(mesh):
    in_specs = (
        P("dp", "sp", None),
        P("dp", "sp", None),
        P("dp", None),
        P("sp", None, None),
        P("sp"),
        P(None, None, "sp"),
        P(None, "sp"),
        P("sp", None),
        P(None, "sp"),
        P("sp"),
        P("sp", None),
        P(),
        P(),
        P(),
        P(),
        P(),
    )
    out_specs = (
        P("dp", "sp", None),
        P("dp", "sp", None),
        P("sp", None, None),
        P("sp"),
        P(None, None, "sp"),
        P(None, "sp"),
        P("sp", None),
        P(None, "sp"),
        P("sp"),
        P("sp", None),
        P(),
        P(None, "sp"),
        P(None, "sp"),
        P("sp", None),
        P("sp"),
    )
    return jax.shard_map(shards, mesh=mesh, in_specs=in_specs, out_specs=out_specs, check_vma=False)
```

```python
import functools

import jax
import jax.numpy as jnp
from jax import lax
from jax.experimental import pallas as pl
from jax.experimental.pallas import tpu as pltpu
from jax.sharding import PartitionSpec as P

HD = 64


EPS = 1e-05
NEG = -1e30


def norm_rows(values, gain, shift):
    center = values - jnp.mean(values, axis=-1, keepdims=True)
    spread = jnp.mean(center * center, axis=-1, keepdims=True)
    return center * lax.rsqrt(spread + EPS) * gain + shift


def gelu_exact(values):
    return jax.nn.gelu(values, approximate=False)


def contract_first(left_rows, right_rows):
    return lax.dot_general(
        left_rows, right_rows, (((0,), (0,)), ((), ())), preferred_element_type=jnp.float32
    )


def contract_last(left_rows, right_rows):
    return lax.dot_general(
        left_rows, right_rows, (((1,), (1,)), ((), ())), preferred_element_type=jnp.float32
    )


PH = 4
RB = 16


def cost(microseconds):
    return pl.CostEstimate(flops=int(microseconds * 1.15e9), bytes_accessed=0, transcendentals=0)


class Held:
    def __init__(self, far, near, semaphore, outward):
        self.near, self.waited, self.outward = near, False, outward
        self.copy = pltpu.make_async_copy(near, far, semaphore) if outward else pltpu.make_async_copy(far, near, semaphore)
        self.started = False

    def start(self):
        if not self.started:
            self.copy.start()
            self.started = True

    def ready(self):
        if not self.outward and not self.waited:
            self.copy.wait()
            self.waited = True
        return self.near

    def finish(self):
        self.start()
        if not self.waited:
            self.copy.wait()
            self.waited = True

    def __getitem__(self, index):
        return self.ready()[index]

    def __setitem__(self, index, value):
        self.near[index] = value

    @property
    def shape(self):
        return self.near.shape

    @property
    def dtype(self):
        return self.near.dtype

    @property
    def at(self):
        return self.ready().at


def add_pairs(pairs, outs):
    for (one, two), out_ref in zip(pairs, outs):
        one, two = one.ready(), two.ready()
        step = 64

        @pl.loop(0, out_ref.shape[0] // step)
        def _(chunk):
            rows = pl.ds(pl.multiple_of(chunk * step, step), step)
            out_ref[rows, :] = (one[rows, :].astype(jnp.float32) + two[rows, :].astype(jnp.float32)).astype(jnp.bfloat16)

        out_ref.start()


class Near:
    def __init__(self, ref):
        self.near, self.shape, self.dtype = ref, ref.shape, ref.dtype

    def start(self):
        pass

    def ready(self):
        return self.near

    def __getitem__(self, index):
        return self.near[index]

    def __setitem__(self, index, value):
        self.near[index] = value

    @property
    def at(self):
        return self.near.at


class HeldParts:
    def __init__(self, far, near, semaphores):
        self.near = near
        self.copies = lambda at: pltpu.make_async_copy(far.at[at], near.at[at], semaphores.at[at])
        for at in range(near.shape[0]):
            self.copies(at).start()

    def ready(self, at):
        self.copies(at).wait()
        return self.near

    @property
    def shape(self):
        return self.near.shape


def held_call(body, outs, arrays, scratch, params, cost, scalars=0, parts=(), far=True, early=()):
    kinds = []
    for at, array in enumerate(arrays):
        kinds.append("scalar" if at < scalars else "parts" if at in parts else "far" if far else "near")
    out_kinds = ["far" if far else "near" for _ in outs]
    specs = {
        "scalar": pl.BlockSpec(memory_space=pltpu.SMEM),
        "parts": pl.BlockSpec(memory_space=pltpu.HBM),
        "far": pl.BlockSpec(memory_space=pltpu.HBM),
        "near": pl.BlockSpec(memory_space=pltpu.VMEM),
    }
    shapes = list(arrays) + list(outs)
    moved = [at for at, kind in enumerate(kinds + out_kinds) if kind in ("far", "parts")]
    buffers = [pltpu.VMEM(shapes[at].shape, shapes[at].dtype) for at in moved]
    semaphores = [
        pltpu.SemaphoreType.DMA((shapes[at].shape[0],)) if at in parts else pltpu.SemaphoreType.DMA for at in moved
    ]
    count = len(shapes)

    def kernel(*refs):
        given, rest = list(refs[:count]), refs[count:]
        near, sems, own = rest[: len(moved)], rest[len(moved) : 2 * len(moved)], rest[2 * len(moved) :]
        held = []
        given = [Near(ref) if kind == "near" else ref for ref, kind in zip(given, kinds + out_kinds)]
        pending = sorted(zip(moved, near, sems), key=lambda item: item[0] not in early)
        for at, buffer, semaphore in pending:
            if at in parts:
                given[at] = HeldParts(given[at], buffer, semaphore)
                continue
            given[at] = Held(given[at], buffer, semaphore, at >= len(arrays))
            held.append(given[at])
            if not given[at].outward:
                given[at].start()
        body(*given, *own)
        for item in held:
            item.finish()

    return pl.pallas_call(
        kernel,
        out_shape=tuple(outs),
        in_specs=[specs[kind] for kind in kinds],
        out_specs=tuple(specs[kind] for kind in out_kinds),
        scratch_shapes=buffers + semaphores + list(scratch),
        compiler_params=params,
        cost_estimate=cost,
    )(*arrays)


def swap_halves(even, odd):
    half = even.shape[1] // 2
    left = lax.broadcasted_iota(jnp.int32, even.shape, 1) < half
    return (
        jnp.where(left, even, pltpu.roll(odd, half, 1)),
        jnp.where(left, pltpu.roll(even, half, 1), odd),
    )


def split_segments(rows, seg_ref, main_ref, side_ref):
    rows = rows.astype(jnp.float32)
    length, channels = rows.shape
    pad = side_ref.shape[2] // 3
    seg = seg_ref[...]
    middle = jnp.where(seg == 1, rows, 0.0)
    first = jnp.where(seg[:pad] == 0, rows[:pad], 0.0)
    last = jnp.where(seg[length - pad :] == 2, rows[length - pad :], 0.0)
    blank = jnp.zeros((pad, 128), jnp.float32)
    for tile in range(channels // 128):
        lanes = slice(128 * tile, 128 * tile + 128)
        main_ref[tile, 0:pad, :] = blank
        main_ref[tile, pad : pad + length, :] = middle[:, lanes]
        main_ref[tile, pad + length :, :] = blank
        for at, part in ((0, first), (1, last)):
            side_ref[at, tile, 0:pad, :] = blank
            side_ref[at, tile, pad : 2 * pad, :] = part[:, lanes]
            side_ref[at, tile, 2 * pad :, :] = blank


def phase_layout(main_ref, side_ref, main_out, side_out):
    tiles = main_ref.shape[0]
    pad = side_ref.shape[2] // 3
    stride = (main_ref.shape[1] - 2 * pad) // RB
    main_blocks = main_out.shape[1] // RB
    side_blocks = side_out.shape[1] // (2 * RB)

    def pack(load, store):
        for pair in range(PH // 2):
            for tile in range(tiles):
                both = swap_halves(load(tile, 2 * pair), load(tile, 2 * pair + 1))
                for at in range(2):
                    store(2 * tile + at, pair, both[at].astype(jnp.bfloat16))

    for block in range(main_blocks):

        def load(tile, phase):
            return main_ref.at[tile][pl.ds(PH * block + phase, RB, stride=stride), :]

        def store(group, pair, value):
            main_out[group, RB * block : RB * block + RB, 128 * pair : 128 * pair + 128] = value

        pack(load, store)

    for block in range(side_blocks):
        for end in range(2):

            def load(tile, phase):
                return side_ref.at[end, tile][pl.ds(PH * block + phase, RB, stride=PH), :]

            def store(group, pair, value):
                at = 2 * RB * block + RB * end
                side_out[group, at : at + RB, 128 * pair : 128 * pair + 128] = value

            pack(load, store)


def frame_layout(sums_ref, main_ref, side_ref):
    tiles = main_ref.shape[0]
    length = main_ref.shape[1]
    blocks = length // (PH * RB)
    stride = length // RB
    for tile in range(tiles):
        for pair in range(PH // 2):
            lanes = slice(128 * pair, 128 * pair + 128)
            for block in range(blocks + 2):
                rows = slice(RB * block, RB * block + RB)
                both = swap_halves(sums_ref[2 * tile, rows, lanes], sums_ref[2 * tile + 1, rows, lanes])
                for at in range(2):
                    phase = 2 * pair + at
                    if block < blocks:
                        main_ref.at[tile][pl.ds(PH * block + phase, RB, stride=stride), :] = both[at]
                    else:
                        side_ref.at[block - blocks, tile][pl.ds(phase, RB, stride=PH), :] = both[at]


def join_segments(main_ref, side_ref, seg_ref):
    length = main_ref.shape[1]
    pad = side_ref.shape[2]
    seg = seg_ref[...]
    pieces = []
    for tile in range(main_ref.shape[0]):
        main = main_ref[tile]
        top = jnp.where(seg[:pad] == 0, side_ref[0, tile], main[:pad])
        low = jnp.where(seg[length - pad :] == 2, side_ref[1, tile], main[length - pad :])
        pieces.append(jnp.concatenate([top, main[pad : length - pad], low], axis=0))
    return jnp.concatenate(pieces, axis=1)


def tap_chunks(count):
    step = 11 if count % 11 == 0 else 1
    return [(at, step) for at in range(0, count, step)]


def fill_taps(rows_ref, group, taps_ref):
    count, size = rows_ref.shape[1:]
    step = min(1024, count)
    taps_ref[0:128, :] = jnp.zeros((128, 128), taps_ref.dtype)
    for at in range(0, count, step):
        now = rows_ref[group, at : at + step, :]
        if at:
            before = rows_ref[group, at - size : at - size + step, :]
        else:
            before = jnp.concatenate([jnp.zeros((size, size), now.dtype), rows_ref[group, 0 : step - size, :]], axis=0)
        taps_ref[128 + at : 128 + at + step, :] = jnp.concatenate([now, before], axis=1)
    last = rows_ref[group, count - size : count, :]
    taps_ref[128 + count : 128 + count + size, :] = jnp.concatenate([jnp.zeros_like(last), last], axis=1)
    taps_ref[128 + count + size :, :] = jnp.zeros((taps_ref.shape[0] - 128 - count - size, 128), taps_ref.dtype)


def phase_dot(main_in, side_in, rows_ref, taps_ref, sums_ref, turned):
    rows = sums_ref.shape[1] - 2 * RB
    width = main_in.shape[2]
    count = side_in.shape[1] // (2 * RB)

    @pl.loop(0, sums_ref.shape[0])
    def _(group):
        fill_taps(rows_ref.ready(group), group, taps_ref)
        total = jnp.zeros(sums_ref.shape[1:], jnp.float32)
        for first, step in tap_chunks(count):
            if turned:
                for d in range(first, first + step):
                    back = count - 1 - d
                    left = jnp.concatenate(
                        [main_in[group, RB * back : RB * back + rows, :], side_in[group, 2 * RB * back : 2 * RB * back + 2 * RB, :]], axis=0
                    )
                    right = jnp.concatenate(
                        [taps_ref[width * d + 128 : width * d + 128 + width, :], taps_ref[width * d : width * d + width, :]], axis=1
                    )
                    total += lax.dot_general(left, right, (((1,), (1,)), ((), ())), preferred_element_type=jnp.float32)
            else:
                left = jnp.concatenate(
                    [
                        jnp.concatenate(
                            [main_in[group, RB * d : RB * d + rows, :], side_in[group, 2 * RB * d : 2 * RB * d + 2 * RB, :]], axis=0
                        )
                        for d in range(first, first + step)
                    ],
                    axis=1,
                )
                low, high = width * first, width * (first + step)
                right = jnp.concatenate([taps_ref[low + 128 : high + 128, :], taps_ref[low:high, :]], axis=1)
                total += jnp.dot(left, right, preferred_element_type=jnp.float32)
        sums_ref[group] = total


def gelu_parts(values):
    share = 0.5 * (1.0 + lax.erf(values * (0.5**0.5)))
    slope = jnp.exp(-0.5 * values * values) * 0.3989422804014327
    return values * share, share + values * slope


def conv_forward_kernel(
    frames, given_ref, seg_ref, taps_ref, bias_ref, sum_ref, slope_ref, parts_ref,
    main_seq, side_seq, main_in, side_in, sums, taps_in, main_out, side_out,
):
    given = given_ref.ready()
    rows = jnp.concatenate([given[block, 0:frames, :] for block in range(given.shape[0])], axis=0)
    split_segments(rows, seg_ref, main_seq, side_seq)
    copies = parts_ref.shape[0] * parts_ref.shape[2] // (WP * rows.shape[1])

    def store(part, tile, value):
        for copy in range(copies):
            parts_ref[copies * part + copy, :, 128 * tile : 128 * tile + 128] = value

    phase_layout(main_seq, side_seq, main_in, side_in)
    pack_wide(main_seq, side_seq, parts_ref.shape[2] // WP, store)
    parts_ref.start()
    phase_dot(main_in, side_in, taps_ref, taps_in, sums, False)
    frame_layout(sums, main_out, side_out)
    conv_sum = join_segments(main_out, side_out, seg_ref) + bias_ref[...]
    value, slope = gelu_parts(conv_sum)
    branch = value.astype(jnp.bfloat16).astype(jnp.float32)
    sum_ref[...] = (rows.astype(jnp.float32) + branch).astype(sum_ref.dtype)
    slope_ref[...] = slope.astype(slope_ref.dtype)


def conv_input_grad_kernel(
    extra, rows_ref, seg_ref, taps_ref, first_ref, *refs
):
    pairs = [refs[2 * at : 2 * at + 2] for at in range(extra)]
    grad_ref, *sums_out = refs[2 * extra : 3 * extra + 1]
    main_seq, side_seq, main_in, side_in, sums, taps_in, main_out, side_out = refs[3 * extra + 1 :]
    split_segments(rows_ref[...], seg_ref, main_seq, side_seq)
    phase_layout(main_seq, side_seq, main_in, side_in)
    add_pairs(pairs, sums_out)
    phase_dot(main_in, side_in, taps_ref, taps_in, sums, True)
    frame_layout(sums, main_out, side_out)
    grad_ref[...] = (first_ref[...] + join_segments(main_out, side_out, seg_ref)).astype(grad_ref.dtype)
    grad_ref.start()


def scratch_of(length, channels, group, taps):
    pad = taps // 2
    groups = channels // group
    tiles = channels // 128
    count = taps // PH + 1
    main_rows = RB * (length // (PH * RB) + count - 1)
    return dict(
        main_seq=pltpu.VMEM((tiles, length + 2 * pad, 128), jnp.float32),
        side_seq=pltpu.VMEM((2, tiles, 3 * pad, 128), jnp.float32),
        main_in=pltpu.VMEM((groups, main_rows, PH * group), jnp.bfloat16),
        side_in=pltpu.VMEM((groups, 2 * RB * count, PH * group), jnp.bfloat16),
        sums=pltpu.VMEM((groups, length // PH + 2 * RB, PH * group), jnp.float32),
        taps=pltpu.VMEM((PH * group * (count + 1), 128), jnp.bfloat16),
        main_out=pltpu.VMEM((tiles, length, 128), jnp.float32),
        side_out=pltpu.VMEM((2, tiles, pad, 128), jnp.float32),
    )


PARAMS = pltpu.CompilerParams(vmem_limit_bytes=60 * 1024 * 1024)
SOME = pltpu.CompilerParams(vmem_limit_bytes=28 * 1024 * 1024)
FEW = pltpu.CompilerParams(vmem_limit_bytes=14 * 1024 * 1024)
WHOLE = pl.BlockSpec(memory_space=pltpu.VMEM)


def conv_forward(given, frames, seg_col, taps, bias, group, width, parts):
    length, channels = given.shape[0] * frames, given.shape[2]
    flops = 2 * (length + 128) * channels * group * (width + 4)
    return held_call(
        functools.partial(conv_forward_kernel, frames),
        (
            jax.ShapeDtypeStruct((length, channels), jnp.bfloat16),
            jax.ShapeDtypeStruct((length, channels), jnp.float32),
            jax.ShapeDtypeStruct((parts, (length + width) // WP, WP * group), jnp.bfloat16),
        ),
        (given, seg_col, taps, bias),
        scratch_of(length, channels, group, width).values(),
        PARAMS,
        cost(12),
        parts=(2,),
    )


def conv_input_grad(rows, seg_col, taps, first, group, width, pairs=()):
    length, channels = rows.shape
    return held_call(
        functools.partial(conv_input_grad_kernel, len(pairs)),
        (jax.ShapeDtypeStruct((length, channels), jnp.bfloat16),)
        + tuple(jax.ShapeDtypeStruct(one.shape, one.dtype) for one, _ in pairs),
        (rows, seg_col, taps, first, *(values for pair in pairs for values in pair)),
        scratch_of(length, channels, group, width).values(),
        PARAMS,
        cost(13.5),
        parts=(2,),
    )


def conv_weight_grad_kernel(
    rows_ref, low_ref, seg_ref, grad_ref,
    main_seq, side_seq, main_in, side_in, main_low, side_low, folded, turned,
):
    groups, _, width = main_in.shape
    count = side_in.shape[1] // (2 * RB)
    low_rows = low_ref.shape[0] // PH
    middle = (count - 1) // 2
    group_size = width // PH
    taps = PH * (count - 1)
    split_segments(low_ref[...], seg_ref, main_seq, side_seq)
    phase_layout(main_seq, side_seq, main_low, side_low)
    split_segments(rows_ref[...], seg_ref, main_seq, side_seq)
    phase_layout(main_seq, side_seq, main_in, side_in)
    left_lanes = lax.broadcasted_iota(jnp.int32, (taps, 128), 1) < group_size

    @pl.loop(0, groups)
    def _(group):
        right = jnp.concatenate(
            [
                main_low[group, RB * middle : RB * middle + low_rows, :],
                side_low[group, 2 * RB * middle : 2 * RB * middle + 2 * RB, :],
            ],
            axis=0,
        )
        folded[0:128, :] = jnp.zeros((128, 128), jnp.float32)
        for d in range(count):
            left = jnp.concatenate(
                [main_in[group, RB * d : RB * d + low_rows, :], side_in[group, 2 * RB * d : 2 * RB * d + 2 * RB, :]], axis=0
            )
            part = lax.dot_general(left, right, (((0,), (0,)), ((), ())), preferred_element_type=jnp.float32)
            folded[width * d + 128 : width * d + 128 + width, :] = part[:, 0:128]
            folded[width * d : width * d + width, :] += part[:, 128:256]

        @pl.loop(0, group_size // 8)
        def _(chunk):
            for at in range(8):
                channel = 8 * chunk + at
                now = folded[pl.ds(128 + channel, taps, stride=group_size), :]
                later = folded[pl.ds(128 + group_size + channel, taps, stride=group_size), :]
                both = jnp.where(left_lanes, now, later).T
                turned[pl.ds(channel, group_size, stride=group_size), :] = both[0:group_size] + both[group_size:]

        grad_ref[pl.ds(pl.multiple_of(group * group_size * group_size, 128), group_size * group_size), :] = turned[...].astype(grad_ref.dtype)


def kernel_weight_grad(rows, low, seg_col, group, width):
    length, channels = rows.shape
    flops = 2 * (length + 128) * channels * group * (width + 4)
    shapes = scratch_of(length, channels, group, width)
    count = width // PH + 1
    names = ["main_seq", "side_seq", "main_in", "side_in", "main_in", "side_in"]
    out = pl.pallas_call(
        conv_weight_grad_kernel,
        out_shape=jax.ShapeDtypeStruct((channels * group, width), jnp.bfloat16),
        in_specs=[WHOLE] * 3,
        out_specs=WHOLE,
        scratch_shapes=[shapes[n] for n in names]
        + [
            pltpu.VMEM((PH * group * count + 128, 128), jnp.float32),
            pltpu.VMEM((group * group, width), jnp.float32),
        ],
        compiler_params=PARAMS,
        cost_estimate=pl.CostEstimate(flops=flops, bytes_accessed=channels * group * width * 2, transcendentals=0),
    )(rows, low, seg_col)
    return out.reshape(channels, group, width)


def tap_rows(kernel):
    channels, group, width = kernel.shape
    groups = channels // group
    return kernel.reshape(groups, group, group, width).transpose(0, 3, 2, 1).reshape(groups, width * group, group)


WP = 8


def pack_wide(main_ref, side_ref, channels_each, store):
    tiles = main_ref.shape[0]
    pad = side_ref.shape[2] // 3
    rows = (main_ref.shape[1] - 2 * pad) // WP
    ends = pad // WP
    per = 128 // channels_each
    lane = lax.broadcasted_iota(jnp.int32, (rows + 2 * ends, 128), 1) // channels_each
    for tile in range(tiles):
        for group in range(WP // per):
            loads = []
            for at in range(per):
                phase = per * group + at
                loads.append(
                    jnp.concatenate(
                        [main_ref.at[tile][pl.ds(pad + phase, rows, stride=WP), :]]
                        + [side_ref.at[end, tile][pl.ds(pad + phase, ends, stride=WP), :] for end in range(2)],
                        axis=0,
                    )
                )
            for part in range(per):
                value = loads[0] if part == 0 else pltpu.roll(loads[0], (128 - channels_each * part) % 128, 1)
                for at in range(1, per):
                    turn = (channels_each * (at - part)) % 128
                    moved = loads[at] if turn == 0 else pltpu.roll(loads[at], turn, 1)
                    value = jnp.where(lane == at, moved, value)
                store(per * tile + part, group, value.astype(jnp.bfloat16))


def norm_back_kernel(
    ranks, model_width, me_ref, unit_ref, scale_ref, gain_ref, slope_ref, seg_ref, *refs
):
    blocks, second_ref = refs[:ranks], refs[ranks]
    first_ref, low_ref, rank_ref, parts_ref, sums_ref, main_seq, side_seq = refs[ranks + 1 :]
    length, channels = slope_ref.shape
    me = me_ref[0]
    frames = length // ranks
    for block in range(ranks):
        first_ref[frames * block : frames * (block + 1), :] = second_ref[block, 0:frames, :].astype(jnp.float32)
    rank_ref[...] = sum(second_ref[block, frames:, :].astype(jnp.float32) for block in range(ranks))
    total = blocks[0][...].astype(jnp.float32)
    for block in blocks[1:]:
        total = total + block[...].astype(jnp.float32)
    grad, tail = total[:length], total[length:]
    spans = length // channels
    rows = [
        jnp.concatenate([tail[spans * at + span : spans * at + span + 1] for span in range(spans)], axis=1)
        for at in range(2)
    ]
    columns = jnp.concatenate(rows + [jnp.zeros((6, length), jnp.float32)], axis=0).T * (1.0 / model_width)
    unit = unit_ref[me].astype(jnp.float32)
    scaled = grad * gain_ref[me]
    first = first_ref.near[...] + (scaled - columns[:, 0:1] - unit * columns[:, 1:2]) * scale_ref[...]
    first_ref[...] = first
    low = (first.astype(jnp.bfloat16).astype(jnp.float32) * slope_ref[...]).astype(jnp.bfloat16)
    low_ref[...] = low
    first_ref.start()
    low_ref.start()
    sums_ref[0:1] = jnp.sum(low.astype(jnp.float32), axis=0, keepdims=True)
    sums_ref[1:2] = jnp.sum(grad * unit, axis=0, keepdims=True)
    sums_ref[2:3] = jnp.sum(grad, axis=0, keepdims=True)
    if parts_ref is None:
        return
    split_segments(low, seg_ref, main_seq, side_seq)

    def store(part, tile, value):
        parts_ref[part, :, 128 * tile : 128 * tile + 128] = value

    pack_wide(main_seq, side_seq, parts_ref.shape[2] // WP, store)


def norm_back(me, unit, scale, gain, slope, seg_col, blocks, seconds, width, group, parts):
    length, channels = slope.shape
    ranks = len(blocks)
    shapes = scratch_of(length, channels, group, width)
    outs = [
        jax.ShapeDtypeStruct((length, channels), jnp.float32),
        jax.ShapeDtypeStruct((length, channels), jnp.bfloat16),
        jax.ShapeDtypeStruct((seconds.shape[1] - length // ranks, channels), jnp.float32),
        jax.ShapeDtypeStruct((3, channels), jnp.float32),
    ]
    scratch = []
    body = functools.partial(norm_back_kernel, ranks, channels * ranks)
    if parts:
        outs.insert(3, jax.ShapeDtypeStruct((parts, (length + width) // WP, WP * (channels // parts)), jnp.bfloat16))
        scratch = [shapes["main_seq"], shapes["side_seq"]]
        kernel = body
    else:

        def kernel(*refs):
            body(*refs[:-1], None, refs[-1], None, None)

    result = held_call(
        kernel,
        outs,
        (me[None], unit, scale, gain, slope, seg_col, *blocks, seconds),
        scratch,
        FEW,
        cost(1.8),
        scalars=1,
        far=False,
    )
    return result if parts else (*result[:3], None, result[3])


def attention_kernel(
    ranks, me_ref, gain_ref, shift_ref, weight_ref, bias_ref, seg_col_ref, seg_row_ref, *refs
):
    pieces = refs[:ranks]
    mixed_ref, qkv_ref, probs_ref, normed_ref, unit_ref, scale_ref, here_ref = refs[ranks : ranks + 7]
    parts, held = refs[ranks + 7 : -1], refs[-1]
    length, width = mixed_ref.shape
    frames = here_ref.shape[0]
    me = me_ref[0]
    step = min(64, length)
    for at, piece in enumerate(pieces):
        held[(me + (ranks - at)) % ranks] = piece[...]
    for at in range(ranks):
        here_ref[:, width * at : width * (at + 1)] = held[at, pl.ds(pl.multiple_of(me * frames, frames), frames), :]

    gain, shift = gain_ref[...], shift_ref[...]

    @pl.loop(0, length // step)
    def _(chunk):
        rows = pl.ds(pl.multiple_of(chunk * step, step), step)
        values = jnp.concatenate([held[at, rows, :] for at in range(ranks)], axis=1).astype(jnp.float32)
        center = values - jnp.mean(values, axis=1, keepdims=True)
        scale = lax.rsqrt(jnp.mean(center * center, axis=1, keepdims=True) + EPS)
        unit = center * scale
        scale_ref[rows, :] = scale
        normed_ref[rows, :] = (unit * gain + shift).astype(jnp.bfloat16)
        unit = unit.astype(jnp.bfloat16)
        for at in range(ranks):
            unit_ref.near[at, rows, :] = unit[:, width * at : width * (at + 1)]

    here_ref.start()
    unit_ref.start()
    normed_ref.start()
    normed = normed_ref.near[...]
    for at in range(3):
        value = jnp.dot(normed, weight_ref[at], preferred_element_type=jnp.float32)
        if at != 1:
            value = value + bias_ref[at // 2 : at // 2 + 1]
        qkv_ref[at] = value.astype(jnp.bfloat16)
    qkv_ref.start()
    qkv_ref = qkv_ref.near
    rows = min(256, length)
    for at in range(0, length, rows):
        same = seg_col_ref[at : at + rows] == seg_row_ref[...]
        result = []
        for head in range(width // HD):
            lanes = slice(HD * head, HD * (head + 1))
            scores = lax.dot_general(
                qkv_ref[0, at : at + rows, lanes], qkv_ref[1, :, lanes], (((1,), (1,)), ((), ())), preferred_element_type=jnp.float32
            )
            scores = jnp.where(same, scores * HD**-0.5, NEG)
            weights = jnp.exp(scores - jnp.max(scores, axis=1, keepdims=True))
            probs = (weights * (1.0 / jnp.sum(weights, axis=1, keepdims=True))).astype(jnp.bfloat16)
            probs_ref[head, at : at + rows, :] = probs
            result.append(jnp.dot(probs, qkv_ref[2, :, lanes], preferred_element_type=jnp.float32))
        mixed_ref[at : at + rows, :] = jnp.concatenate(result, axis=1).astype(jnp.bfloat16)
    for at, part in enumerate(parts):
        block = (me + (ranks - at)) % ranks
        part[...] = mixed_ref.near[pl.ds(pl.multiple_of(block * frames, frames), frames), :]
        part.start()


def attention(me, gain, shift, weight, bias, seg_col, seg_row, pieces, frames):
    ranks = len(pieces)
    length, width = pieces[0].shape
    heads = width // HD
    model = ranks * width
    flops = 2 * length * (3 * model * width + 2 * length * width)
    return held_call(
        functools.partial(attention_kernel, ranks),
        (
            jax.ShapeDtypeStruct((length, width), jnp.bfloat16),
            jax.ShapeDtypeStruct((3, length, width), jnp.bfloat16),
            jax.ShapeDtypeStruct((heads, length, length), jnp.bfloat16),
            jax.ShapeDtypeStruct((length, model), jnp.bfloat16),
            jax.ShapeDtypeStruct((ranks, length, width), jnp.bfloat16),
            jax.ShapeDtypeStruct((length, 1), jnp.float32),
            jax.ShapeDtypeStruct((frames, model), jnp.bfloat16),
        )
        + tuple(jax.ShapeDtypeStruct((frames, width), jnp.bfloat16) for _ in range(ranks)),
        (me[None], gain, shift, weight, bias, seg_col, seg_row, *pieces),
        [pltpu.VMEM((ranks, length, width), jnp.bfloat16)],
        PARAMS,
        cost(11.5),
        scalars=1,
        early=range(7, 7 + ranks),
    )


def attention_back_kernel(
    ranks, extra, me_ref, qkv_ref, probs_ref, unit_ref, gain_ref, weight_ref, *refs
):
    pieces, refs = refs[:ranks], refs[ranks:]
    pairs, refs = [refs[2 * at : 2 * at + 2] for at in range(extra)], refs[2 * extra :]
    (joined_ref, bias_ref), outs, refs = refs[:2], refs[2 : ranks + 2], refs[ranks + 2 :]
    sums_out, (cot_ref, key_sum, value_sum) = refs[:extra], refs[extra:]
    length, width = cot_ref.shape
    me = me_ref[0]
    frames = length // ranks
    for at, piece in enumerate(pieces):
        block = (me + at) % ranks
        cot_ref[pl.ds(pl.multiple_of(block * frames, frames), frames), :] = piece[...]
    rows = min(256, length)
    for at in range(0, length, rows):
        queries = []
        for head in range(width // HD):
            lanes = slice(HD * head, HD * (head + 1))
            cot = cot_ref[at : at + rows, lanes]
            probs = (probs_ref.near if at else probs_ref.ready(head))[head, at : at + rows, :]
            probs_wide = probs.astype(jnp.float32)
            grad = lax.dot_general(cot, qkv_ref[2, :, lanes], (((1,), (1,)), ((), ())), preferred_element_type=jnp.float32)
            delta = jnp.sum(probs_wide * grad, axis=1, keepdims=True)
            score = (probs_wide * (grad - delta)).astype(jnp.bfloat16)
            queries.append(jnp.dot(score, qkv_ref[1, :, lanes], preferred_element_type=jnp.float32))
            keys = contract_first(score, qkv_ref[0, at : at + rows, lanes])
            values = contract_first(probs, cot)
            if at:
                key_sum[head] += keys
                value_sum[head] += values
            else:
                key_sum[head] = keys
                value_sum[head] = values
        joined_ref[at : at + rows, 0:width] = (jnp.concatenate(queries, axis=1) * HD**-0.5).astype(jnp.bfloat16)
    heads = width // HD
    joined_ref[:, width : 2 * width] = (
        jnp.concatenate([key_sum[head] for head in range(heads)], axis=1) * HD**-0.5
    ).astype(jnp.bfloat16)
    joined_ref[:, 2 * width :] = jnp.concatenate([value_sum[head] for head in range(heads)], axis=1).astype(jnp.bfloat16)
    joined_ref.start()
    joined_ref = joined_ref.near
    bias_ref[0:1] = jnp.sum(joined_ref[:, 0:width].astype(jnp.float32), axis=0, keepdims=True)
    bias_ref[1:2] = jnp.sum(joined_ref[:, 2 * width :].astype(jnp.float32), axis=0, keepdims=True)
    plain = jnp.zeros((length, width), jnp.float32)
    along = jnp.zeros((length, width), jnp.float32)
    for at, out in enumerate(outs):
        block = (me + (ranks - at)) % ranks
        span = pl.ds(pl.multiple_of(block * width, width), width)
        part = jnp.zeros((length, width), jnp.float32)
        for which in range(3):
            part += contract_last(joined_ref[:, width * which : width * (which + 1)], weight_ref[which, span, :])
        out[0:length, :] = part.astype(jnp.bfloat16)
        scaled = part * gain_ref[block]
        plain += scaled
        along += scaled * unit_ref[block].astype(jnp.float32)
    ones = jnp.ones((8, width), jnp.bfloat16)
    sums = [contract_last(ones, value.astype(jnp.bfloat16))[0:1] for value in (plain, along)]
    spans = length // width
    tail = [value[:, width * span : width * (span + 1)] for value in sums for span in range(spans)]
    tail = jnp.concatenate(tail + [jnp.zeros((16 - 2 * spans, width), jnp.float32)] * (2 * spans < 16), axis=0)
    for out in outs:
        out[length:, :] = tail.astype(jnp.bfloat16)
        out.start()
    add_pairs(pairs, sums_out)


def attention_back(me, qkv, probs, unit, gain, weight, pieces, pairs=()):
    ranks, length, width = unit.shape
    heads = width // HD
    flops = 2 * length * (3 * ranks * width * width + 5 * length * width)
    return held_call(
        functools.partial(attention_back_kernel, ranks, len(pairs)),
        (
            jax.ShapeDtypeStruct((length, 3 * width), jnp.bfloat16),
            jax.ShapeDtypeStruct((2, width), jnp.float32),
        )
        + tuple(jax.ShapeDtypeStruct((length + 16, width), jnp.bfloat16) for _ in range(ranks))
        + tuple(jax.ShapeDtypeStruct(one.shape, one.dtype) for one, _ in pairs),
        (me[None], qkv, probs, unit, gain, weight, *pieces, *(values for pair in pairs for values in pair)),
        [pltpu.VMEM((length, width), jnp.bfloat16)] + [pltpu.VMEM((heads, length, HD), jnp.float32)] * 2,
        PARAMS,
        cost(12),
        scalars=1,
        parts=(2,),
        early=(1, *range(6, 6 + ranks)),
    )


def split_weight_grad_kernel(
    rows_ref, low_ref, grad_ref, seq, side_seq, main_in, side_in, low_seq, low_all, even, odd, turned, final,
):
    batch, packed, wide = rows_ref.shape
    low_width = low_ref.shape[2]
    each = low_width // WP
    group = wide // WP
    count = side_in.shape[1] // RB
    ends = (count - 1) // 2
    main_rows = packed - 2 * ends
    blocks = main_rows // RB
    taps = WP * (count - 1)

    rows_ref, low_ref = rows_ref.ready(), low_ref.ready()

    @pl.loop(0, batch)
    def _(row):
        for tile in range(wide // 128):
            lanes = slice(128 * tile, 128 * tile + 128)
            values = rows_ref[row, :, lanes].astype(jnp.float32)
            blank = jnp.zeros((ends, 128), jnp.float32)
            seq[tile] = jnp.concatenate([blank, values[:main_rows], blank], axis=0)
            for end in range(2):
                side_seq[tile, end] = jnp.concatenate(
                    [blank, values[main_rows + ends * end : main_rows + ends * (end + 1)], blank], axis=0
                )
            for block in range(blocks + count - 1):
                main_in[row, RB * block : RB * block + RB, lanes] = seq.at[tile][pl.ds(block, RB, stride=blocks), :].astype(jnp.bfloat16)
            for d in range(count):
                side_in[row, RB * d : RB * d + RB, lanes] = jnp.concatenate(
                    [side_seq[tile, 0, d : d + ends, :], side_seq[tile, 1, d : d + ends, :]], axis=0
                ).astype(jnp.bfloat16)
        for tile in range(low_width // 128):
            lanes = slice(128 * tile, 128 * tile + 128)
            low_seq[tile] = low_ref[row, :, lanes].astype(jnp.float32)
            for block in range(blocks):
                low_all[row, RB * block : RB * block + RB, lanes] = low_seq.at[tile][pl.ds(block, RB, stride=blocks), :].astype(jnp.bfloat16)
            low_all[row, main_rows:packed, lanes] = low_ref[row, main_rows:packed, lanes]

    left = jnp.concatenate([low_all[row] for row in range(batch)], axis=0).T
    even[...] = jnp.zeros(even.shape, jnp.float32)
    odd[...] = jnp.zeros(odd.shape, jnp.float32)

    for d in range(count):
        at = RB * d
        right = jnp.concatenate(
            [
                part
                for row in range(batch)
                for part in (main_in[row, pl.ds(at, main_rows), :], side_in[row, pl.ds(at, RB), :])
            ],
            axis=0,
        )
        part = jnp.dot(left, right, preferred_element_type=jnp.float32)
        for phase in range(WP):
            held = even if phase % 2 == 0 else odd
            lanes = pl.ds(wide * d + wide - group * (phase - phase % 2), wide)
            held[:, lanes] += part[each * phase : each * (phase + 1), :]

    left_lanes = lax.broadcasted_iota(jnp.int32, (each, 128), 1) < group
    for tile in range(taps * group // 128):
        at = wide + 128 * tile
        near, far = odd[:, at : at + 128], odd[:, at + 128 : at + 256]
        value = even[:, at : at + 128] + jnp.where(left_lanes, pltpu.roll(near, group, 1), pltpu.roll(far, group, 1))
        turned[128 * tile : 128 * tile + 128, 0:each] = value.T

    for channel in range(group):
        final[pl.ds(channel, each, stride=group), :] = turned[pl.ds(channel, taps, stride=group), :].T[0:each, :]

    grad_ref[...] = final[...].astype(grad_ref.dtype)


def split_weight_grad(rows, low, group, width):
    batch, packed, wide = rows.shape
    each = low.shape[2] // WP
    count = width // WP + 1
    ends = (count - 1) // 2
    main_rows = packed - 2 * ends
    blocks = main_rows // RB
    flops = 2 * batch * packed * low.shape[2] * wide * count
    (out,) = held_call(
        split_weight_grad_kernel,
        (jax.ShapeDtypeStruct((each * group, width), jnp.bfloat16),),
        (rows, low),
        [
            pltpu.VMEM((wide // 128, main_rows + 2 * ends, 128), jnp.float32),
            pltpu.VMEM((wide // 128, 2, 3 * ends, 128), jnp.float32),
            pltpu.VMEM((batch, RB * (blocks + count - 1), wide), jnp.bfloat16),
            pltpu.VMEM((batch, RB * count, wide), jnp.bfloat16),
            pltpu.VMEM((low.shape[2] // 128, packed, 128), jnp.float32),
            pltpu.VMEM((batch, packed, low.shape[2]), jnp.bfloat16),
            pltpu.VMEM((each, wide * (count + 1)), jnp.float32),
            pltpu.VMEM((each, wide * (count + 1)), jnp.float32),
            pltpu.VMEM((width * group, 128), jnp.float32),
            pltpu.VMEM((each * group, width), jnp.float32),
        ],
        SOME,
        cost(8),
        far=False,
    )
    return out


def centered(values):
    center = values - jnp.mean(values, axis=1, keepdims=True)
    scale = lax.rsqrt(jnp.mean(center * center, axis=1, keepdims=True) + EPS)
    return center * scale, scale


def norm_pull(grad, unit, scale, gain):
    scaled = grad * gain
    inner = scaled - jnp.mean(scaled, axis=1, keepdims=True) - unit * jnp.mean(scaled * unit, axis=1, keepdims=True)
    return inner * scale, jnp.sum(grad * unit, axis=0, keepdims=True), jnp.sum(grad, axis=0, keepdims=True)


def weight_rows(weight_ref, turn, block, width):
    down = width // weight_ref.shape[2]
    across = weight_ref.shape[0] // down
    return jnp.concatenate(
        [
            jnp.concatenate([weight_ref[(down * column + at) ^ turn, block] for at in range(down)], axis=0)
            for column in range(across)
        ],
        axis=1,
    )


def attention_sum_kernel(ranks, me_ref, weight_ref, here_ref, bias_ref, gain_ref, shift_ref, *refs):
    pieces, (sum_ref, normed_ref, unit_ref, scale_ref) = refs[:ranks], refs[ranks:]
    width = pieces[0].shape[1]
    total = here_ref[...].astype(jnp.float32) + bias_ref[...]
    for at, piece in enumerate(pieces):
        block = (me_ref[0] + at) % ranks
        rows = weight_rows(weight_ref, me_ref[1], block, width)
        total = total + jnp.dot(piece[...], rows, preferred_element_type=jnp.float32)
    unit, scale = centered(total)
    sum_ref[...] = total
    normed_ref[...] = (unit * gain_ref[...] + shift_ref[...]).astype(jnp.bfloat16)
    unit_ref[...] = unit
    scale_ref[...] = scale


def attention_sum(me, weight, here, bias, gain, shift, pieces):
    frames, model = here.shape
    ranks = len(pieces)
    return held_call(
        functools.partial(attention_sum_kernel, ranks),
        (
            jax.ShapeDtypeStruct((frames, model), jnp.float32),
            jax.ShapeDtypeStruct((frames, model), jnp.bfloat16),
            jax.ShapeDtypeStruct((frames, model), jnp.float32),
            jax.ShapeDtypeStruct((frames, 1), jnp.float32),
        ),
        (me, weight, here, bias, gain, shift, *pieces),
        [],
        FEW,
        cost(1.3),
        scalars=1,
        far=False,
    )


def head_kernel(
    ranks, second_ref, bias_ref, gain_ref, shift_ref, weight_ref, letter_ref, cot_ref, *refs
):
    pieces = refs[:ranks]
    logits_ref, third_ref, low_ref, weight_grad_ref, letter_grad_ref, norm_ref = refs[ranks:]
    total = second_ref[...] + bias_ref[...]
    for piece in pieces:
        total = total + piece[...].astype(jnp.float32)
    unit, scale = centered(total)
    final = (unit * gain_ref[...] + shift_ref[...]).astype(jnp.bfloat16)
    cot = cot_ref[...]
    logits_ref[...] = jnp.dot(final, weight_ref[...], preferred_element_type=jnp.float32) + letter_ref[...]
    weight_grad_ref[...] = contract_first(cot, final)
    letter_grad_ref[...] = jnp.sum(cot.astype(jnp.float32), axis=0, keepdims=True)
    third, norm_ref[0:1], norm_ref[1:2] = norm_pull(contract_last(cot, weight_ref[...]), unit, scale, gain_ref[...])
    third_ref[...] = third
    low_ref[...] = third.astype(jnp.bfloat16)


def head(second, bias, gain, shift, weight, letter_bias, cotangent, pieces):
    frames, model = second.shape
    letters = weight.shape[1]
    return held_call(
        functools.partial(head_kernel, len(pieces)),
        (
            jax.ShapeDtypeStruct((frames, letters), jnp.float32),
            jax.ShapeDtypeStruct((frames, model), jnp.float32),
            jax.ShapeDtypeStruct((frames, model), jnp.bfloat16),
            jax.ShapeDtypeStruct((letters, model), jnp.float32),
            jax.ShapeDtypeStruct((1, letters), jnp.float32),
            jax.ShapeDtypeStruct((2, model), jnp.float32),
        ),
        (second, bias, gain, shift, weight, letter_bias, cotangent, *pieces),
        [],
        FEW,
        cost(1.9),
        far=False,
    )


def second_back_kernel(
    ranks, me_ref, weight_ref, third_ref, unit_ref, scale_ref, gain_ref, letters_ref, bias_ref, final_ref, *refs
):
    pieces, (low_ref,) = refs[:ranks], refs[ranks : ranks + 1]
    mixed, seconds = refs[ranks + 1 : 2 * ranks + 1], refs[2 * ranks + 1]
    frames, width = mixed[0].shape
    total = pieces[0][...].astype(jnp.float32)
    for piece in pieces[1:]:
        total = total + piece[...].astype(jnp.float32)
    grad, gain_grad, shift_grad = norm_pull(total, unit_ref[...], scale_ref[...], gain_ref[...])
    low = (third_ref[...] + grad).astype(jnp.bfloat16)
    low_ref[...] = low
    low_ref.start()
    letters = letters_ref.shape[0]
    spare = seconds.shape[1] - frames - letters - 5
    small = jnp.concatenate([letters_ref[...], gain_grad, shift_grad, final_ref[...]], axis=0)
    last = jnp.concatenate([bias_ref[...], jnp.zeros((1, width - letters), jnp.float32)], axis=1)
    for block in range(ranks):
        lanes = slice(width * block, width * (block + 1))
        rows = [small[:, lanes], last, jnp.zeros((spare, width), jnp.float32)]
        seconds[block, 0:frames, :] = low[:, lanes]
        seconds[block, frames:, :] = jnp.concatenate(rows, axis=0).astype(jnp.bfloat16)
    for at in range(ranks):
        block = (me_ref[0] + (ranks - at)) % ranks
        mixed[at][...] = contract_last(low, weight_rows(weight_ref, me_ref[1], block, width)).astype(jnp.bfloat16)
        mixed[at].start()


def second_back(me, weight, third, unit, scale, gain, letters_grad, bias_grad, final_grads, pieces):
    frames, model = third.shape
    ranks = len(pieces)
    rows = frames + (letters_grad.shape[0] + 5 + 15) // 16 * 16
    result = held_call(
        functools.partial(second_back_kernel, ranks),
        (jax.ShapeDtypeStruct((frames, model), jnp.bfloat16),)
        + tuple(jax.ShapeDtypeStruct((frames, model // ranks), jnp.bfloat16) for _ in range(ranks))
        + (jax.ShapeDtypeStruct((ranks, rows, model // ranks), jnp.bfloat16),),
        (me, weight, third, unit, scale, gain, letters_grad, bias_grad, final_grads, *pieces),
        [],
        PARAMS,
        cost(8),
        scalars=1,
        early=range(10, 10 + ranks),
    )
    return result[0], result[1 : 1 + ranks], result[1 + ranks]


def ffn_grad_kernel(count, me_ref, *refs):
    groups = [refs[count * at : count * (at + 1)] for at in range(4)]
    keep_refs, give_refs, sums = refs[4 * count : 4 * count + 2], refs[4 * count + 2 : 4 * count + 4], refs[4 * count + 4 :]
    core = me_ref[0] % 2
    for which in range(2):
        left = jnp.concatenate([ref[...] for ref in groups[2 * which]], axis=0)
        right = jnp.concatenate([ref[...] for ref in groups[2 * which + 1]], axis=0)
        sums[which][...] = jnp.sum(right.astype(jnp.float32), axis=0, keepdims=True)
        rows = 256
        for at in range(0, left.shape[1], rows):
            block = contract_first(left[:, at : at + rows], right).astype(jnp.bfloat16)
            part, down = divmod(at, keep_refs[0].shape[0])

            @pl.when(core == which)
            def _():
                keep_refs[part][down : down + rows, :] = block

            @pl.when(core != which)
            def _():
                give_refs[part][down : down + rows, :] = block


def ffn_grads(row, lefts, rights):
    count = len(lefts[0])
    rows, columns = lefts[0][0].shape[1], rights[0][0].shape[1]
    frames = lefts[0][0].shape[0]
    return held_call(
        functools.partial(ffn_grad_kernel, count),
        tuple(jax.ShapeDtypeStruct((rows // 2, columns), jnp.bfloat16) for _ in range(4))
        + tuple(jax.ShapeDtypeStruct((1, columns), jnp.float32) for _ in range(2)),
        (row[None], *lefts[0], *rights[0], *lefts[1], *rights[1]),
        [],
        PARAMS,
        cost(9.8),
        scalars=1,
    )


def out_grad_kernel(ranks, me_ref, mixed_ref, *refs):
    pieces, (out_ref, sum_ref) = refs[:ranks], refs[ranks:]
    width = mixed_ref.shape[1]
    frames = pieces[0].shape[0]
    mixed_ref = mixed_ref.ready()
    left, right = [], []
    for at, piece in enumerate(pieces):
        block = (me_ref[0] + (ranks - at)) % ranks
        left.append(mixed_ref[pl.ds(pl.multiple_of(block * frames, frames), frames), :])
        right.append(piece[...])
    left, right = jnp.concatenate(left, axis=0), jnp.concatenate(right, axis=0)
    sum_ref[...] = jnp.sum(right.astype(jnp.float32), axis=0, keepdims=True)
    for block in range(ranks):
        lanes = slice(width * block, width * (block + 1))
        out_ref[block] = contract_first(left, right[:, lanes]).astype(out_ref.dtype)


def out_grads(me, mixed, pieces):
    length, width = mixed.shape
    model = pieces[0].shape[1]
    return held_call(
        functools.partial(out_grad_kernel, len(pieces)),
        (
            jax.ShapeDtypeStruct((model // width, width, width), jnp.bfloat16),
            jax.ShapeDtypeStruct((1, model), jnp.float32),
        ),
        (me[None], mixed, *pieces),
        [],
        PARAMS,
        cost(3.1),
        scalars=1,
    )


def unite_blocks(blocks, me, outs, emit):
    count = len(blocks)
    rows, columns = blocks[0].shape

    def kernel(turn_ref, *refs):
        given, rest = refs[:count], refs[count:]
        out_refs, (held, semaphores) = rest[: len(outs)], rest[len(outs) :]
        step = pl.program_id(0)
        copies = [pltpu.make_async_copy(given[at], held.at[at], semaphores.at[at]) for at in range(count)]

        @pl.when(step == 0)
        def _():
            for copy in copies:
                copy.start()

        for at in range(count):

            @pl.when((step ^ turn_ref[0]) == at)
            def _():
                copies[at].wait()

        emit(step, held[step ^ turn_ref[0]].astype(jnp.float32), out_refs)

    return pl.pallas_call(
        kernel,
        out_shape=tuple(shape for shape, _, _ in outs),
        grid_spec=pltpu.PrefetchScalarGridSpec(
            num_scalar_prefetch=1,
            grid=(count,),
            in_specs=[pl.BlockSpec(memory_space=pltpu.HBM)] * count,
            out_specs=tuple(pl.BlockSpec(block, index) for _, block, index in outs),
            scratch_shapes=[pltpu.VMEM((count, rows, columns), blocks[0].dtype), pltpu.SemaphoreType.DMA((count,))],
        ),
        compiler_params=SOME,
        cost_estimate=cost(5),
    )(me[None], *blocks)


def unite_one(blocks, me):
    rows, columns = blocks[0].shape

    def emit(step, value, outs):
        outs[0][...] = value

    shape = jax.ShapeDtypeStruct((len(blocks) * rows, columns), jnp.float32)
    return unite_blocks(blocks, me, [(shape, (rows, columns), lambda at, turn: (at, 0))], emit)[0]


def paired(block, step):
    return lax.ppermute(block, "dp", [(at, at ^ step) for at in range(lax.axis_size("dp"))])


def add_low(mine, other):
    return low(wide(mine) + wide(other))


def cross_first(values):
    half = values.shape[0] // 32 * 16
    return add_low(values[:half], paired(values[:half], 2)), add_low(values[half:], paired(values[half:], 4))


def cross_second(upper, lower):
    return jnp.concatenate([add_low(upper, paired(upper, 4)), add_low(lower, paired(lower, 2))])


def core_halves(values, row):
    half = values.shape[0] // 2
    core = row % 2
    return tuple(lax.dynamic_slice_in_dim(values, side * half, half) for side in (core, 1 - core))


def core_join(values, row):
    other = paired(values, 1)
    return jnp.where(row % 2 == 0, values, other), jnp.where(row % 2 == 0, other, values)


def gather_eight(block, meanwhile=()):
    half = block.shape[0] // 32 * 16
    (two, four), meanwhile = lax.optimization_barrier(((paired(block, 2), paired(block, 4)), meanwhile))
    six = jnp.concatenate([paired(four[:half], 2), paired(two[half:], 4)])
    one = paired(after(block, two), 1)
    return [block, one, two, paired(two, 1), four, paired(four, 1), six, paired(six, 1)], meanwhile


def low(values):
    return values.astype(jnp.bfloat16)


def wide(values):
    return values.astype(jnp.float32)


def shifted(block, step):
    count = lax.axis_size("sp")
    return lax.ppermute(block, "sp", [(at, (at + step) % count) for at in range(count)])


def gather_pieces(block):
    return [block] + [shifted(block, step) for step in range(1, lax.axis_size("sp"))]


def return_pieces(pieces):
    return [pieces[0]] + [shifted(pieces[step], -step) for step in range(1, lax.axis_size("sp"))]


def sum_pieces(pieces):
    total = wide(pieces[0])
    for step in range(1, lax.axis_size("sp")):
        total = total + wide(shifted(low(pieces[step]), -step))
    return total


def weight_grad_kernel(me_ref, left_ref, right_ref, keep_ref, give_ref):
    count, rows, width = keep_ref.shape
    core = me_ref[0] % 2
    left_ref, right_ref = left_ref.ready(), right_ref.ready()
    for out_ref, side in ((give_ref, 1 - core), (keep_ref, core)):
        left = left_ref[:, pl.ds(pl.multiple_of(rows * side, rows), rows)]
        for at in range(count):
            out_ref[at] = contract_first(left, right_ref[:, width * at : width * (at + 1)]).astype(out_ref.dtype)
        out_ref.start()


def weight_grad(row, left, right, parts):
    width = right.shape[1] // parts
    return held_call(
        weight_grad_kernel,
        tuple(jax.ShapeDtypeStruct((parts, left.shape[1] // 2, width), jnp.bfloat16) for _ in range(2)),
        (row[None], left, right),
        [],
        PARAMS,
        cost(3),
        scalars=1,
    )


def after(values, *others):
    return lax.optimization_barrier((values, others))[0]


def shards(
    features,
    logit_grad,
    segment_ids,
    conv_weight,
    conv_bias,
    w_qkv,
    qv_bias,
    w_out,
    w_up,
    ffn_bias,
    w_down,
    out_biases,
    gains,
    shifts,
    ctc_weight,
    ctc_bias,
):
    ranks = lax.axis_size("sp")
    me = lax.axis_index("sp")
    signal = features[0]
    frames, model_width = signal.shape
    segments = segment_ids[0]
    length = segments.shape[0]
    local_width = model_width // ranks
    kernel_width = conv_weight.shape[2]
    group_size = conv_weight.shape[1]
    seg_col, seg_row = segments[:, None], segments[None, :]
    rows_count = lax.axis_size("dp")
    row = lax.axis_index("dp")
    part_width = local_width // rows_count
    split_rows = rows_count == 8 and part_width % 16 == 0 and group_size % part_width == 0
    owners = [(me - step) % ranks for step in range(ranks)]
    taps = tap_rows(conv_weight)
    w_three = w_qkv.transpose(1, 0, 2)
    gain_blocks = gains[0].reshape(ranks, 1, local_width)
    down = local_width // frames
    slices = split_rows and local_width % frames == 0 and down * ranks == rows_count
    signal_blocks = signal.reshape(frames, ranks, local_width).transpose(1, 0, 2)
    if slices:
        share = lax.dynamic_slice(
            w_out, ((row % down) * frames, (row // down) * local_width), (frames, local_width)
        )
        share = jnp.broadcast_to(share[None], signal_blocks.shape)
        signal_blocks = jnp.concatenate([signal_blocks, share], axis=1)
    given = lax.all_to_all(signal_blocks, "sp", 0, 0)
    turn = row if slices else jnp.zeros_like(row)
    places = jnp.stack([me, turn])
    first_low, conv_slope, wide_rows = conv_forward(
        given, frames, seg_col, taps, conv_bias[None], group_size, kernel_width, rows_count if split_rows else local_width // group_size
    )
    first_pieces = gather_pieces(first_low)
    if slices:
        w_parts = jnp.stack(gather_eight(after(given[:, frames:].reshape(-1, local_width), first_low))[0])
        w_parts = w_parts.reshape(rows_count, ranks, frames, local_width)
        first_pieces[2] = after(first_pieces[2], w_parts)
    else:
        w_parts = lax.all_gather(w_out, "sp", axis=0)[None]
    mixed_heads, qkv, probs_low, normed_full, unit_one, scale_one, first_here, *mixed_parts = attention(
        me, gains[0:1], shifts[0:1], w_three, qv_bias, seg_col, seg_row, first_pieces, frames
    )
    mixed_parts = return_pieces(mixed_parts)
    second_sum, normed_two, unit_two, scale_two = attention_sum(
        places, w_parts, first_here, out_biases[0:1], gains[1:2], shifts[1:2], mixed_parts
    )
    ffn_pieces = gather_pieces(normed_two)
    if split_rows:
        wide_all = lax.all_to_all(after(wide_rows, normed_two), "dp", 0, 0)
        ffn_pieces[2] = after(ffn_pieces[2], wide_all)
    active_pieces, gelu_slopes, down_parts = [], [], []
    for piece in ffn_pieces:
        if down_parts:
            piece = after(piece, down_parts[-1])
        hidden = jnp.dot(piece, w_up, preferred_element_type=jnp.float32) + ffn_bias
        share = 0.5 * (1.0 + lax.erf(hidden * (0.5**0.5)))
        gelu_slopes.append(share + hidden * jnp.exp(-0.5 * hidden * hidden) * 0.3989422804014327)
        active_pieces.append(low(hidden * share))
        down_parts.append(low(jnp.dot(active_pieces[-1], w_down, preferred_element_type=jnp.float32)))
    logits, third_grad, down_cot, ctc_weight_grad, ctc_bias_grad, final_norm_grads = head(
        second_sum, out_biases[1:2], gains[2:3], shifts[2:3], ctc_weight, ctc_bias[None], logit_grad[0], return_pieces(down_parts)
    )
    down_pieces = gather_pieces(down_cot)
    hidden_pieces, up_parts = [], []
    for piece, slope in zip(down_pieces, gelu_slopes):
        if up_parts:
            piece = after(piece, up_parts[-1])
        hidden_pieces.append(low(contract_last(piece, w_down) * slope))
        up_parts.append(low(contract_last(hidden_pieces[-1], w_up)))
    up_back = return_pieces(up_parts)
    if slices:
        active_pieces, ffn_pieces, down_pieces, hidden_pieces = after(
            (active_pieces, ffn_pieces, down_pieces, hidden_pieces), up_back[1]
        )
        *ffn_halves, down_bias_grad, ffn_bias_grad = ffn_grads(
            row, (active_pieces, ffn_pieces), (down_pieces, hidden_pieces)
        )
        up_back[2] = after(up_back[2], ffn_halves[0])
        ffn_pairs = [(keep, paired(give, 1)) for keep, give in zip(ffn_halves[:2], ffn_halves[2:])]
    else:
        down_full, hidden_full = jnp.concatenate(down_pieces), jnp.concatenate(hidden_pieces)
        down_grad = contract_first(jnp.concatenate(active_pieces), down_full)
        up_grad = contract_first(jnp.concatenate(ffn_pieces), hidden_full)
        ffn_bias_grad = jnp.sum(wide(hidden_full), axis=0)
        down_bias_grad = jnp.sum(wide(down_full), axis=0)
        up_sum, down_sum = (wide(total) for total in lax.psum((low(up_grad), low(down_grad)), "dp"))

    out_cot, mixed_back, second_blocks = second_back(
        places, w_parts, third_grad, unit_two, scale_two, gains[1:2], ctc_weight_grad, ctc_bias_grad, final_norm_grads, up_back
    )
    mixed_pieces = return_pieces(mixed_back)
    joined_grad, qv_bias_grad, *norm_blocks = attention_back(
        me, qkv, probs_low, unit_one, gain_blocks, w_three, mixed_pieces, ffn_pairs if slices else ()
    )
    norm_blocks, ffn_halves = norm_blocks[:ranks], norm_blocks[ranks:]
    norm_blocks = return_pieces(norm_blocks)
    second_groups = lax.all_to_all(after(second_blocks, norm_blocks[1]), "sp", 0, 0)
    if slices:
        ffn_halves = [add_low(half, paired(half, step)) for half, step in zip(ffn_halves, (2, 4))]
        norm_blocks[1] = after(norm_blocks[1], ffn_halves)
    first_grad, conv_low, rank_sums, low_parts, channel_sums = norm_back(
        me, unit_one, scale_one, gain_blocks, conv_slope, seg_col, norm_blocks, second_groups,
        kernel_width, group_size, rows_count if split_rows else 0,
    )
    signal_groups, *_ = conv_input_grad(conv_low, seg_col, taps, first_grad, group_size, kernel_width)
    out_pieces = gather_pieces(after(out_cot, first_grad))
    if slices:
        joined_grad = after(joined_grad, first_grad)
        qkv_keep, qkv_give = (half.reshape(-1, local_width) for half in weight_grad(row, normed_full, joined_grad, 3))
        qkv_half = add_low(qkv_keep, paired(qkv_give, 1))
        ffn_half = cross_second(*ffn_halves)
        low_rows = after(lax.all_to_all(low_parts, "dp", 0, 0), signal_groups, qkv_half, ffn_half, out_pieces)
        qkv_cross = cross_first(qkv_half)
        conv_part = split_weight_grad(wide_all, low_rows, group_size, kernel_width)
        conv_blocks, qkv_cross = gather_eight(conv_part, qkv_cross)
        out_pieces = after(out_pieces, conv_part)
    else:
        grouped = given[:, :frames].reshape(length, local_width)
        conv_weight_grad = kernel_weight_grad(grouped, conv_low, seg_col, group_size, kernel_width)
    out_low, out_bias_grad = out_grads(me, mixed_heads, out_pieces)
    small_parts = [rank_sums, channel_sums, qv_bias_grad]
    small_parts += [values.reshape(-1, local_width) for values in (ffn_bias_grad, out_bias_grad, down_bias_grad)]
    small = jnp.concatenate(small_parts)
    few = -(-small.shape[0] // 64) * 64
    small = low(jnp.pad(small, ((0, few - small.shape[0]), (0, 0))))
    if slices:
        out_rows = jnp.concatenate([out_low.reshape(-1, local_width), small])
        out_rows = after(out_rows, conv_blocks[2])
        out_half = add_low(*(lambda keep, give: (keep, paired(give, 1)))(*core_halves(out_rows, row)))
        qkv_half = cross_second(*qkv_cross)
        out_half = cross_second(*cross_first(out_half))
        conv_sum = unite_one(conv_blocks, row).reshape(local_width, group_size, kernel_width)
        down_sum, up_sum = (wide(total) for total in core_join(ffn_half, row))
        qkv_sum = [half.reshape(3, 1, -1, local_width) for half in core_join(qkv_half, row)]
        qkv_sum = wide(jnp.concatenate(qkv_sum, axis=1)).reshape(3, model_width, local_width)
        out_rows = wide(jnp.concatenate(core_join(out_half, row)))
        out_sum = out_rows[:model_width].reshape(ranks, local_width, local_width)
        small = out_rows[model_width:]
        signal_groups = after(signal_groups, conv_part)
    else:
        qkv_low = contract_first(normed_full, joined_grad).reshape(model_width, 3, local_width).transpose(1, 0, 2)
        conv_sum, qkv_sum, out_sum, small = (
            wide(total) for total in lax.psum((conv_weight_grad, low(qkv_low), out_low, small), "dp")
        )
    out_sum = out_sum.transpose(1, 0, 2).reshape(local_width, model_width)
    feature_grad = wide(lax.all_to_all(signal_groups, "sp", split_axis=0, concat_axis=1, tiled=True))

    cuts, at = [], 0
    for part in small_parts:
        cuts.append(small[at : at + part.shape[0]])
        at += part.shape[0]
    letters = ctc_weight.shape[1]
    few_letters = letters // ranks
    rank_sums, channel_sums, qv_sum, ffn_bias_sum, out_bias_sum, down_bias_sum = cuts
    norm_sums = rank_sums[letters : letters + 4]
    return (
        logits[None],
        feature_grad[None],
        conv_sum,
        channel_sums[0],
        qkv_sum.transpose(1, 0, 2),
        qv_sum,
        out_sum,
        up_sum,
        ffn_bias_sum.reshape(-1),
        down_sum,
        jnp.stack([out_bias_sum.reshape(-1), down_bias_sum.reshape(-1)]),
        jnp.stack([channel_sums[1], norm_sums[0], norm_sums[2]]),
        jnp.stack([channel_sums[2], norm_sums[1], norm_sums[3]]),
        rank_sums[:letters].T,
        lax.dynamic_slice_in_dim(rank_sums[letters + 4, :letters], me * few_letters, few_letters),
    )


def solution(mesh):
    in_specs = (
        P("dp", "sp", None),
        P("dp", "sp", None),
        P("dp", None),
        P("sp", None, None),
        P("sp"),
        P(None, None, "sp"),
        P(None, "sp"),
        P("sp", None),
        P(None, "sp"),
        P("sp"),
        P("sp", None),
        P(),
        P(),
        P(),
        P(),
        P(),
    )
    out_specs = (
        P("dp", "sp", None),
        P("dp", "sp", None),
        P("sp", None, None),
        P("sp"),
        P(None, None, "sp"),
        P(None, "sp"),
        P("sp", None),
        P(None, "sp"),
        P("sp"),
        P("sp", None),
        P(),
        P(None, "sp"),
        P(None, "sp"),
        P("sp", None),
        P("sp"),
    )
    return jax.shard_map(shards, mesh=mesh, in_specs=in_specs, out_specs=out_specs, check_vma=False)
```

```python
import functools

import jax
import jax.numpy as jnp
from jax import lax
from jax.experimental import pallas as pl
from jax.experimental.pallas import tpu as pltpu
from jax.sharding import PartitionSpec as P

HD = 64


EPS = 1e-05
NEG = -1e30


def norm_rows(values, gain, shift):
    center = values - jnp.mean(values, axis=-1, keepdims=True)
    spread = jnp.mean(center * center, axis=-1, keepdims=True)
    return center * lax.rsqrt(spread + EPS) * gain + shift


def gelu_exact(values):
    return jax.nn.gelu(values, approximate=False)


def contract_first(left_rows, right_rows):
    return lax.dot_general(
        left_rows, right_rows, (((0,), (0,)), ((), ())), preferred_element_type=jnp.float32
    )


def contract_last(left_rows, right_rows):
    return lax.dot_general(
        left_rows, right_rows, (((1,), (1,)), ((), ())), preferred_element_type=jnp.float32
    )


PH = 4
RB = 16


def cost(microseconds):
    return pl.CostEstimate(flops=int(microseconds * 1.15e9), bytes_accessed=0, transcendentals=0)


class Held:
    def __init__(self, far, near, semaphore, outward):
        self.near, self.waited, self.outward = near, False, outward
        self.copy = pltpu.make_async_copy(near, far, semaphore) if outward else pltpu.make_async_copy(far, near, semaphore)
        self.started = False

    def start(self):
        if not self.started:
            self.copy.start()
            self.started = True

    def ready(self):
        if not self.outward and not self.waited:
            self.copy.wait()
            self.waited = True
        return self.near

    def finish(self):
        self.start()
        if not self.waited:
            self.copy.wait()
            self.waited = True

    def __getitem__(self, index):
        return self.ready()[index]

    def __setitem__(self, index, value):
        self.near[index] = value

    @property
    def shape(self):
        return self.near.shape

    @property
    def dtype(self):
        return self.near.dtype

    @property
    def at(self):
        return self.ready().at


def add_pairs(pairs, outs):
    for (one, two), out_ref in zip(pairs, outs):
        one, two = one.ready(), two.ready()
        step = 64

        @pl.loop(0, out_ref.shape[0] // step)
        def _(chunk):
            rows = pl.ds(pl.multiple_of(chunk * step, step), step)
            out_ref[rows, :] = (one[rows, :].astype(jnp.float32) + two[rows, :].astype(jnp.float32)).astype(jnp.bfloat16)

        out_ref.start()


class Near:
    def __init__(self, ref):
        self.near, self.shape, self.dtype = ref, ref.shape, ref.dtype

    def start(self):
        pass

    def ready(self):
        return self.near

    def __getitem__(self, index):
        return self.near[index]

    def __setitem__(self, index, value):
        self.near[index] = value

    @property
    def at(self):
        return self.near.at


class HeldParts:
    def __init__(self, far, near, semaphores):
        self.near = near
        self.copies = lambda at: pltpu.make_async_copy(far.at[at], near.at[at], semaphores.at[at])
        for at in range(near.shape[0]):
            self.copies(at).start()

    def ready(self, at):
        self.copies(at).wait()
        return self.near

    @property
    def shape(self):
        return self.near.shape


def held_call(body, outs, arrays, scratch, params, cost, scalars=0, parts=(), far=True, early=()):
    kinds = []
    for at, array in enumerate(arrays):
        kinds.append("scalar" if at < scalars else "parts" if at in parts else "far" if far else "near")
    out_kinds = ["far" if far else "near" for _ in outs]
    specs = {
        "scalar": pl.BlockSpec(memory_space=pltpu.SMEM),
        "parts": pl.BlockSpec(memory_space=pltpu.HBM),
        "far": pl.BlockSpec(memory_space=pltpu.HBM),
        "near": pl.BlockSpec(memory_space=pltpu.VMEM),
    }
    shapes = list(arrays) + list(outs)
    moved = [at for at, kind in enumerate(kinds + out_kinds) if kind in ("far", "parts")]
    buffers = [pltpu.VMEM(shapes[at].shape, shapes[at].dtype) for at in moved]
    semaphores = [
        pltpu.SemaphoreType.DMA((shapes[at].shape[0],)) if at in parts else pltpu.SemaphoreType.DMA for at in moved
    ]
    count = len(shapes)

    def kernel(*refs):
        given, rest = list(refs[:count]), refs[count:]
        near, sems, own = rest[: len(moved)], rest[len(moved) : 2 * len(moved)], rest[2 * len(moved) :]
        held = []
        given = [Near(ref) if kind == "near" else ref for ref, kind in zip(given, kinds + out_kinds)]
        pending = sorted(zip(moved, near, sems), key=lambda item: item[0] not in early)
        for at, buffer, semaphore in pending:
            if at in parts:
                given[at] = HeldParts(given[at], buffer, semaphore)
                continue
            given[at] = Held(given[at], buffer, semaphore, at >= len(arrays))
            held.append(given[at])
            if not given[at].outward:
                given[at].start()
        body(*given, *own)
        for item in held:
            item.finish()

    return pl.pallas_call(
        kernel,
        out_shape=tuple(outs),
        in_specs=[specs[kind] for kind in kinds],
        out_specs=tuple(specs[kind] for kind in out_kinds),
        scratch_shapes=buffers + semaphores + list(scratch),
        compiler_params=params,
        cost_estimate=cost,
    )(*arrays)


def swap_halves(even, odd):
    half = even.shape[1] // 2
    left = lax.broadcasted_iota(jnp.int32, even.shape, 1) < half
    return (
        jnp.where(left, even, pltpu.roll(odd, half, 1)),
        jnp.where(left, pltpu.roll(even, half, 1), odd),
    )


def split_segments(rows, seg_ref, main_ref, side_ref):
    rows = rows.astype(jnp.float32)
    length, channels = rows.shape
    pad = side_ref.shape[2] // 3
    seg = seg_ref[...]
    middle = jnp.where(seg == 1, rows, 0.0)
    first = jnp.where(seg[:pad] == 0, rows[:pad], 0.0)
    last = jnp.where(seg[length - pad :] == 2, rows[length - pad :], 0.0)
    blank = jnp.zeros((pad, 128), jnp.float32)
    for tile in range(channels // 128):
        lanes = slice(128 * tile, 128 * tile + 128)
        main_ref[tile, 0:pad, :] = blank
        main_ref[tile, pad : pad + length, :] = middle[:, lanes]
        main_ref[tile, pad + length :, :] = blank
        for at, part in ((0, first), (1, last)):
            side_ref[at, tile, 0:pad, :] = blank
            side_ref[at, tile, pad : 2 * pad, :] = part[:, lanes]
            side_ref[at, tile, 2 * pad :, :] = blank


def phase_layout(main_ref, side_ref, main_out, side_out):
    tiles = main_ref.shape[0]
    pad = side_ref.shape[2] // 3
    stride = (main_ref.shape[1] - 2 * pad) // RB
    main_blocks = main_out.shape[1] // RB
    side_blocks = side_out.shape[1] // (2 * RB)

    def pack(load, store):
        for pair in range(PH // 2):
            for tile in range(tiles):
                both = swap_halves(load(tile, 2 * pair), load(tile, 2 * pair + 1))
                for at in range(2):
                    store(2 * tile + at, pair, both[at].astype(jnp.bfloat16))

    for block in range(main_blocks):

        def load(tile, phase):
            return main_ref.at[tile][pl.ds(PH * block + phase, RB, stride=stride), :]

        def store(group, pair, value):
            main_out[group, RB * block : RB * block + RB, 128 * pair : 128 * pair + 128] = value

        pack(load, store)

    for block in range(side_blocks):
        for end in range(2):

            def load(tile, phase):
                return side_ref.at[end, tile][pl.ds(PH * block + phase, RB, stride=PH), :]

            def store(group, pair, value):
                at = 2 * RB * block + RB * end
                side_out[group, at : at + RB, 128 * pair : 128 * pair + 128] = value

            pack(load, store)


def frame_layout(sums_ref, main_ref, side_ref):
    tiles = main_ref.shape[0]
    length = main_ref.shape[1]
    blocks = length // (PH * RB)
    stride = length // RB
    for tile in range(tiles):
        for pair in range(PH // 2):
            lanes = slice(128 * pair, 128 * pair + 128)
            for block in range(blocks + 2):
                rows = slice(RB * block, RB * block + RB)
                both = swap_halves(sums_ref[2 * tile, rows, lanes], sums_ref[2 * tile + 1, rows, lanes])
                for at in range(2):
                    phase = 2 * pair + at
                    if block < blocks:
                        main_ref.at[tile][pl.ds(PH * block + phase, RB, stride=stride), :] = both[at]
                    else:
                        side_ref.at[block - blocks, tile][pl.ds(phase, RB, stride=PH), :] = both[at]


def join_segments(main_ref, side_ref, seg_ref):
    length = main_ref.shape[1]
    pad = side_ref.shape[2]
    seg = seg_ref[...]
    pieces = []
    for tile in range(main_ref.shape[0]):
        main = main_ref[tile]
        top = jnp.where(seg[:pad] == 0, side_ref[0, tile], main[:pad])
        low = jnp.where(seg[length - pad :] == 2, side_ref[1, tile], main[length - pad :])
        pieces.append(jnp.concatenate([top, main[pad : length - pad], low], axis=0))
    return jnp.concatenate(pieces, axis=1)


def tap_chunks(count):
    step = 11 if count % 11 == 0 else 1
    return [(at, step) for at in range(0, count, step)]


def fill_taps(rows_ref, group, taps_ref):
    count, size = rows_ref.shape[1:]
    step = min(1024, count)
    taps_ref[0:128, :] = jnp.zeros((128, 128), taps_ref.dtype)
    for at in range(0, count, step):
        now = rows_ref[group, at : at + step, :]
        if at:
            before = rows_ref[group, at - size : at - size + step, :]
        else:
            before = jnp.concatenate([jnp.zeros((size, size), now.dtype), rows_ref[group, 0 : step - size, :]], axis=0)
        taps_ref[128 + at : 128 + at + step, :] = jnp.concatenate([now, before], axis=1)
    last = rows_ref[group, count - size : count, :]
    taps_ref[128 + count : 128 + count + size, :] = jnp.concatenate([jnp.zeros_like(last), last], axis=1)
    taps_ref[128 + count + size :, :] = jnp.zeros((taps_ref.shape[0] - 128 - count - size, 128), taps_ref.dtype)


def phase_dot(main_in, side_in, rows_ref, taps_ref, sums_ref, turned):
    rows = sums_ref.shape[1] - 2 * RB
    width = main_in.shape[2]
    count = side_in.shape[1] // (2 * RB)

    @pl.loop(0, sums_ref.shape[0])
    def _(group):
        fill_taps(rows_ref.ready(group), group, taps_ref)
        total = jnp.zeros(sums_ref.shape[1:], jnp.float32)
        for first, step in tap_chunks(count):
            if turned:
                for d in range(first, first + step):
                    back = count - 1 - d
                    left = jnp.concatenate(
                        [main_in[group, RB * back : RB * back + rows, :], side_in[group, 2 * RB * back : 2 * RB * back + 2 * RB, :]], axis=0
                    )
                    right = jnp.concatenate(
                        [taps_ref[width * d + 128 : width * d + 128 + width, :], taps_ref[width * d : width * d + width, :]], axis=1
                    )
                    total += lax.dot_general(left, right, (((1,), (1,)), ((), ())), preferred_element_type=jnp.float32)
            else:
                left = jnp.concatenate(
                    [
                        jnp.concatenate(
                            [main_in[group, RB * d : RB * d + rows, :], side_in[group, 2 * RB * d : 2 * RB * d + 2 * RB, :]], axis=0
                        )
                        for d in range(first, first + step)
                    ],
                    axis=1,
                )
                low, high = width * first, width * (first + step)
                right = jnp.concatenate([taps_ref[low + 128 : high + 128, :], taps_ref[low:high, :]], axis=1)
                total += jnp.dot(left, right, preferred_element_type=jnp.float32)
        sums_ref[group] = total


def gelu_parts(values):
    share = 0.5 * (1.0 + lax.erf(values * (0.5**0.5)))
    slope = jnp.exp(-0.5 * values * values) * 0.3989422804014327
    return values * share, share + values * slope


def conv_forward_kernel(
    frames, given_ref, seg_ref, taps_ref, bias_ref, sum_ref, slope_ref, parts_ref,
    main_seq, side_seq, main_in, side_in, sums, taps_in, main_out, side_out,
):
    given = given_ref.ready()
    rows = jnp.concatenate([given[block, 0:frames, :] for block in range(given.shape[0])], axis=0)
    split_segments(rows, seg_ref, main_seq, side_seq)
    copies = parts_ref.shape[0] * parts_ref.shape[2] // (WP * rows.shape[1])

    def store(part, tile, value):
        for copy in range(copies):
            parts_ref[copies * part + copy, :, 128 * tile : 128 * tile + 128] = value

    phase_layout(main_seq, side_seq, main_in, side_in)
    pack_wide(main_seq, side_seq, parts_ref.shape[2] // WP, store)
    parts_ref.start()
    phase_dot(main_in, side_in, taps_ref, taps_in, sums, False)
    frame_layout(sums, main_out, side_out)
    conv_sum = join_segments(main_out, side_out, seg_ref) + bias_ref[...]
    value, slope = gelu_parts(conv_sum)
    branch = value.astype(jnp.bfloat16).astype(jnp.float32)
    sum_ref[...] = (rows.astype(jnp.float32) + branch).astype(sum_ref.dtype)
    slope_ref[...] = slope.astype(slope_ref.dtype)


def conv_input_grad_kernel(
    extra, rows_ref, seg_ref, taps_ref, first_ref, *refs
):
    pairs = [refs[2 * at : 2 * at + 2] for at in range(extra)]
    grad_ref, *sums_out = refs[2 * extra : 3 * extra + 1]
    main_seq, side_seq, main_in, side_in, sums, taps_in, main_out, side_out = refs[3 * extra + 1 :]
    split_segments(rows_ref[...], seg_ref, main_seq, side_seq)
    phase_layout(main_seq, side_seq, main_in, side_in)
    add_pairs(pairs, sums_out)
    phase_dot(main_in, side_in, taps_ref, taps_in, sums, True)
    frame_layout(sums, main_out, side_out)
    grad_ref[...] = (first_ref[...] + join_segments(main_out, side_out, seg_ref)).astype(grad_ref.dtype)
    grad_ref.start()


def scratch_of(length, channels, group, taps):
    pad = taps // 2
    groups = channels // group
    tiles = channels // 128
    count = taps // PH + 1
    main_rows = RB * (length // (PH * RB) + count - 1)
    return dict(
        main_seq=pltpu.VMEM((tiles, length + 2 * pad, 128), jnp.float32),
        side_seq=pltpu.VMEM((2, tiles, 3 * pad, 128), jnp.float32),
        main_in=pltpu.VMEM((groups, main_rows, PH * group), jnp.bfloat16),
        side_in=pltpu.VMEM((groups, 2 * RB * count, PH * group), jnp.bfloat16),
        sums=pltpu.VMEM((groups, length // PH + 2 * RB, PH * group), jnp.float32),
        taps=pltpu.VMEM((PH * group * (count + 1), 128), jnp.bfloat16),
        main_out=pltpu.VMEM((tiles, length, 128), jnp.float32),
        side_out=pltpu.VMEM((2, tiles, pad, 128), jnp.float32),
    )


PARAMS = pltpu.CompilerParams(vmem_limit_bytes=60 * 1024 * 1024)
SOME = pltpu.CompilerParams(vmem_limit_bytes=28 * 1024 * 1024)
FEW = pltpu.CompilerParams(vmem_limit_bytes=14 * 1024 * 1024)
WHOLE = pl.BlockSpec(memory_space=pltpu.VMEM)


def conv_forward(given, frames, seg_col, taps, bias, group, width, parts):
    length, channels = given.shape[0] * frames, given.shape[2]
    flops = 2 * (length + 128) * channels * group * (width + 4)
    return held_call(
        functools.partial(conv_forward_kernel, frames),
        (
            jax.ShapeDtypeStruct((length, channels), jnp.bfloat16),
            jax.ShapeDtypeStruct((length, channels), jnp.float32),
            jax.ShapeDtypeStruct((parts, (length + width) // WP, WP * group), jnp.bfloat16),
        ),
        (given, seg_col, taps, bias),
        scratch_of(length, channels, group, width).values(),
        PARAMS,
        cost(12),
        parts=(2,),
    )


def conv_input_grad(rows, seg_col, taps, first, group, width, pairs=()):
    length, channels = rows.shape
    return held_call(
        functools.partial(conv_input_grad_kernel, len(pairs)),
        (jax.ShapeDtypeStruct((length, channels), jnp.bfloat16),)
        + tuple(jax.ShapeDtypeStruct(one.shape, one.dtype) for one, _ in pairs),
        (rows, seg_col, taps, first, *(values for pair in pairs for values in pair)),
        scratch_of(length, channels, group, width).values(),
        PARAMS,
        cost(13.5),
        parts=(2,),
    )


def conv_weight_grad_kernel(
    rows_ref, low_ref, seg_ref, grad_ref,
    main_seq, side_seq, main_in, side_in, main_low, side_low, folded, turned,
):
    groups, _, width = main_in.shape
    count = side_in.shape[1] // (2 * RB)
    low_rows = low_ref.shape[0] // PH
    middle = (count - 1) // 2
    group_size = width // PH
    taps = PH * (count - 1)
    split_segments(low_ref[...], seg_ref, main_seq, side_seq)
    phase_layout(main_seq, side_seq, main_low, side_low)
    split_segments(rows_ref[...], seg_ref, main_seq, side_seq)
    phase_layout(main_seq, side_seq, main_in, side_in)
    left_lanes = lax.broadcasted_iota(jnp.int32, (taps, 128), 1) < group_size

    @pl.loop(0, groups)
    def _(group):
        right = jnp.concatenate(
            [
                main_low[group, RB * middle : RB * middle + low_rows, :],
                side_low[group, 2 * RB * middle : 2 * RB * middle + 2 * RB, :],
            ],
            axis=0,
        )
        folded[0:128, :] = jnp.zeros((128, 128), jnp.float32)
        for d in range(count):
            left = jnp.concatenate(
                [main_in[group, RB * d : RB * d + low_rows, :], side_in[group, 2 * RB * d : 2 * RB * d + 2 * RB, :]], axis=0
            )
            part = lax.dot_general(left, right, (((0,), (0,)), ((), ())), preferred_element_type=jnp.float32)
            folded[width * d + 128 : width * d + 128 + width, :] = part[:, 0:128]
            folded[width * d : width * d + width, :] += part[:, 128:256]

        @pl.loop(0, group_size // 8)
        def _(chunk):
            for at in range(8):
                channel = 8 * chunk + at
                now = folded[pl.ds(128 + channel, taps, stride=group_size), :]
                later = folded[pl.ds(128 + group_size + channel, taps, stride=group_size), :]
                both = jnp.where(left_lanes, now, later).T
                turned[pl.ds(channel, group_size, stride=group_size), :] = both[0:group_size] + both[group_size:]

        grad_ref[pl.ds(pl.multiple_of(group * group_size * group_size, 128), group_size * group_size), :] = turned[...].astype(grad_ref.dtype)


def kernel_weight_grad(rows, low, seg_col, group, width):
    length, channels = rows.shape
    flops = 2 * (length + 128) * channels * group * (width + 4)
    shapes = scratch_of(length, channels, group, width)
    count = width // PH + 1
    names = ["main_seq", "side_seq", "main_in", "side_in", "main_in", "side_in"]
    out = pl.pallas_call(
        conv_weight_grad_kernel,
        out_shape=jax.ShapeDtypeStruct((channels * group, width), jnp.bfloat16),
        in_specs=[WHOLE] * 3,
        out_specs=WHOLE,
        scratch_shapes=[shapes[n] for n in names]
        + [
            pltpu.VMEM((PH * group * count + 128, 128), jnp.float32),
            pltpu.VMEM((group * group, width), jnp.float32),
        ],
        compiler_params=PARAMS,
        cost_estimate=pl.CostEstimate(flops=flops, bytes_accessed=channels * group * width * 2, transcendentals=0),
    )(rows, low, seg_col)
    return out.reshape(channels, group, width)


def tap_rows(kernel):
    channels, group, width = kernel.shape
    groups = channels // group
    return kernel.reshape(groups, group, group, width).transpose(0, 3, 2, 1).reshape(groups, width * group, group)


WP = 8


def pack_wide(main_ref, side_ref, channels_each, store):
    tiles = main_ref.shape[0]
    pad = side_ref.shape[2] // 3
    rows = (main_ref.shape[1] - 2 * pad) // WP
    ends = pad // WP
    per = 128 // channels_each
    lane = lax.broadcasted_iota(jnp.int32, (rows + 2 * ends, 128), 1) // channels_each
    for tile in range(tiles):
        for group in range(WP // per):
            loads = []
            for at in range(per):
                phase = per * group + at
                loads.append(
                    jnp.concatenate(
                        [main_ref.at[tile][pl.ds(pad + phase, rows, stride=WP), :]]
                        + [side_ref.at[end, tile][pl.ds(pad + phase, ends, stride=WP), :] for end in range(2)],
                        axis=0,
                    )
                )
            for part in range(per):
                value = loads[0] if part == 0 else pltpu.roll(loads[0], (128 - channels_each * part) % 128, 1)
                for at in range(1, per):
                    turn = (channels_each * (at - part)) % 128
                    moved = loads[at] if turn == 0 else pltpu.roll(loads[at], turn, 1)
                    value = jnp.where(lane == at, moved, value)
                store(per * tile + part, group, value.astype(jnp.bfloat16))


def norm_back_kernel(
    ranks, model_width, me_ref, unit_ref, scale_ref, gain_ref, slope_ref, seg_ref, *refs
):
    blocks, second_ref = refs[:ranks], refs[ranks]
    first_ref, low_ref, rank_ref, parts_ref, sums_ref, main_seq, side_seq = refs[ranks + 1 :]
    length, channels = slope_ref.shape
    me = me_ref[0]
    frames = length // ranks
    for block in range(ranks):
        first_ref[frames * block : frames * (block + 1), :] = second_ref[block, 0:frames, :].astype(jnp.float32)
    rank_ref[...] = sum(second_ref[block, frames:, :].astype(jnp.float32) for block in range(ranks))
    total = blocks[0][...].astype(jnp.float32)
    for block in blocks[1:]:
        total = total + block[...].astype(jnp.float32)
    grad, tail = total[:length], total[length:]
    spans = length // channels
    rows = [
        jnp.concatenate([tail[spans * at + span : spans * at + span + 1] for span in range(spans)], axis=1)
        for at in range(2)
    ]
    columns = jnp.concatenate(rows + [jnp.zeros((6, length), jnp.float32)], axis=0).T * (1.0 / model_width)
    unit = unit_ref[me].astype(jnp.float32)
    scaled = grad * gain_ref[me]
    first = first_ref.near[...] + (scaled - columns[:, 0:1] - unit * columns[:, 1:2]) * scale_ref[...]
    first_ref[...] = first
    low = (first.astype(jnp.bfloat16).astype(jnp.float32) * slope_ref[...]).astype(jnp.bfloat16)
    low_ref[...] = low
    first_ref.start()
    low_ref.start()
    sums_ref[0:1] = jnp.sum(low.astype(jnp.float32), axis=0, keepdims=True)
    sums_ref[1:2] = jnp.sum(grad * unit, axis=0, keepdims=True)
    sums_ref[2:3] = jnp.sum(grad, axis=0, keepdims=True)
    if parts_ref is None:
        return
    split_segments(low, seg_ref, main_seq, side_seq)

    def store(part, tile, value):
        parts_ref[part, :, 128 * tile : 128 * tile + 128] = value

    pack_wide(main_seq, side_seq, parts_ref.shape[2] // WP, store)


def norm_back(me, unit, scale, gain, slope, seg_col, blocks, seconds, width, group, parts):
    length, channels = slope.shape
    ranks = len(blocks)
    shapes = scratch_of(length, channels, group, width)
    outs = [
        jax.ShapeDtypeStruct((length, channels), jnp.float32),
        jax.ShapeDtypeStruct((length, channels), jnp.bfloat16),
        jax.ShapeDtypeStruct((seconds.shape[1] - length // ranks, channels), jnp.float32),
        jax.ShapeDtypeStruct((3, channels), jnp.float32),
    ]
    scratch = []
    body = functools.partial(norm_back_kernel, ranks, channels * ranks)
    if parts:
        outs.insert(3, jax.ShapeDtypeStruct((parts, (length + width) // WP, WP * (channels // parts)), jnp.bfloat16))
        scratch = [shapes["main_seq"], shapes["side_seq"]]
        kernel = body
    else:

        def kernel(*refs):
            body(*refs[:-1], None, refs[-1], None, None)

    result = held_call(
        kernel,
        outs,
        (me[None], unit, scale, gain, slope, seg_col, *blocks, seconds),
        scratch,
        FEW,
        cost(1.8),
        scalars=1,
        far=False,
    )
    return result if parts else (*result[:3], None, result[3])


def attention_kernel(
    ranks, me_ref, gain_ref, shift_ref, weight_ref, bias_ref, seg_col_ref, seg_row_ref, *refs
):
    pieces = refs[:ranks]
    mixed_ref, qkv_ref, probs_ref, normed_ref, unit_ref, scale_ref, here_ref = refs[ranks : ranks + 7]
    parts, held = refs[ranks + 7 : -1], refs[-1]
    length, width = mixed_ref.shape
    frames = here_ref.shape[0]
    me = me_ref[0]
    step = min(64, length)
    for at, piece in enumerate(pieces):
        held[(me + (ranks - at)) % ranks] = piece[...]
    for at in range(ranks):
        here_ref[:, width * at : width * (at + 1)] = held[at, pl.ds(pl.multiple_of(me * frames, frames), frames), :]

    gain, shift = gain_ref[...], shift_ref[...]

    @pl.loop(0, length // step)
    def _(chunk):
        rows = pl.ds(pl.multiple_of(chunk * step, step), step)
        values = jnp.concatenate([held[at, rows, :] for at in range(ranks)], axis=1).astype(jnp.float32)
        center = values - jnp.mean(values, axis=1, keepdims=True)
        scale = lax.rsqrt(jnp.mean(center * center, axis=1, keepdims=True) + EPS)
        unit = center * scale
        scale_ref[rows, :] = scale
        normed_ref[rows, :] = (unit * gain + shift).astype(jnp.bfloat16)
        unit = unit.astype(jnp.bfloat16)
        for at in range(ranks):
            unit_ref.near[at, rows, :] = unit[:, width * at : width * (at + 1)]

    here_ref.start()
    unit_ref.start()
    normed_ref.start()
    normed = normed_ref.near[...]
    for at in range(3):
        value = jnp.dot(normed, weight_ref[at], preferred_element_type=jnp.float32)
        if at != 1:
            value = value + bias_ref[at // 2 : at // 2 + 1]
        qkv_ref[at] = value.astype(jnp.bfloat16)
    qkv_ref.start()
    qkv_ref = qkv_ref.near
    rows = min(256, length)
    for at in range(0, length, rows):
        same = seg_col_ref[at : at + rows] == seg_row_ref[...]
        result = []
        for head in range(width // HD):
            lanes = slice(HD * head, HD * (head + 1))
            scores = lax.dot_general(
                qkv_ref[0, at : at + rows, lanes], qkv_ref[1, :, lanes], (((1,), (1,)), ((), ())), preferred_element_type=jnp.float32
            )
            scores = jnp.where(same, scores * HD**-0.5, NEG)
            weights = jnp.exp(scores - jnp.max(scores, axis=1, keepdims=True))
            probs = (weights * (1.0 / jnp.sum(weights, axis=1, keepdims=True))).astype(jnp.bfloat16)
            probs_ref[head, at : at + rows, :] = probs
            result.append(jnp.dot(probs, qkv_ref[2, :, lanes], preferred_element_type=jnp.float32))
        mixed_ref[at : at + rows, :] = jnp.concatenate(result, axis=1).astype(jnp.bfloat16)
    for at, part in enumerate(parts):
        block = (me + (ranks - at)) % ranks
        part[...] = mixed_ref.near[pl.ds(pl.multiple_of(block * frames, frames), frames), :]
        part.start()


def attention(me, gain, shift, weight, bias, seg_col, seg_row, pieces, frames):
    ranks = len(pieces)
    length, width = pieces[0].shape
    heads = width // HD
    model = ranks * width
    flops = 2 * length * (3 * model * width + 2 * length * width)
    return held_call(
        functools.partial(attention_kernel, ranks),
        (
            jax.ShapeDtypeStruct((length, width), jnp.bfloat16),
            jax.ShapeDtypeStruct((3, length, width), jnp.bfloat16),
            jax.ShapeDtypeStruct((heads, length, length), jnp.bfloat16),
            jax.ShapeDtypeStruct((length, model), jnp.bfloat16),
            jax.ShapeDtypeStruct((ranks, length, width), jnp.bfloat16),
            jax.ShapeDtypeStruct((length, 1), jnp.float32),
            jax.ShapeDtypeStruct((frames, model), jnp.bfloat16),
        )
        + tuple(jax.ShapeDtypeStruct((frames, width), jnp.bfloat16) for _ in range(ranks)),
        (me[None], gain, shift, weight, bias, seg_col, seg_row, *pieces),
        [pltpu.VMEM((ranks, length, width), jnp.bfloat16)],
        PARAMS,
        cost(11.5),
        scalars=1,
        early=range(7, 7 + ranks),
    )


def attention_back_kernel(
    ranks, extra, me_ref, qkv_ref, probs_ref, unit_ref, gain_ref, weight_ref, *refs
):
    pieces, refs = refs[:ranks], refs[ranks:]
    pairs, refs = [refs[2 * at : 2 * at + 2] for at in range(extra)], refs[2 * extra :]
    (joined_ref, bias_ref), outs, refs = refs[:2], refs[2 : ranks + 2], refs[ranks + 2 :]
    sums_out, (cot_ref, key_sum, value_sum) = refs[:extra], refs[extra:]
    length, width = cot_ref.shape
    me = me_ref[0]
    frames = length // ranks
    for at, piece in enumerate(pieces):
        block = (me + at) % ranks
        cot_ref[pl.ds(pl.multiple_of(block * frames, frames), frames), :] = piece[...]
    rows = min(256, length)
    for at in range(0, length, rows):
        queries = []
        for head in range(width // HD):
            lanes = slice(HD * head, HD * (head + 1))
            cot = cot_ref[at : at + rows, lanes]
            probs = (probs_ref.near if at else probs_ref.ready(head))[head, at : at + rows, :]
            probs_wide = probs.astype(jnp.float32)
            grad = lax.dot_general(cot, qkv_ref[2, :, lanes], (((1,), (1,)), ((), ())), preferred_element_type=jnp.float32)
            delta = jnp.sum(probs_wide * grad, axis=1, keepdims=True)
            score = (probs_wide * (grad - delta)).astype(jnp.bfloat16)
            queries.append(jnp.dot(score, qkv_ref[1, :, lanes], preferred_element_type=jnp.float32))
            keys = contract_first(score, qkv_ref[0, at : at + rows, lanes])
            values = contract_first(probs, cot)
            if at:
                key_sum[head] += keys
                value_sum[head] += values
            else:
                key_sum[head] = keys
                value_sum[head] = values
        joined_ref[at : at + rows, 0:width] = (jnp.concatenate(queries, axis=1) * HD**-0.5).astype(jnp.bfloat16)
    heads = width // HD
    joined_ref[:, width : 2 * width] = (
        jnp.concatenate([key_sum[head] for head in range(heads)], axis=1) * HD**-0.5
    ).astype(jnp.bfloat16)
    joined_ref[:, 2 * width :] = jnp.concatenate([value_sum[head] for head in range(heads)], axis=1).astype(jnp.bfloat16)
    joined_ref.start()
    joined_ref = joined_ref.near
    bias_ref[0:1] = jnp.sum(joined_ref[:, 0:width].astype(jnp.float32), axis=0, keepdims=True)
    bias_ref[1:2] = jnp.sum(joined_ref[:, 2 * width :].astype(jnp.float32), axis=0, keepdims=True)
    plain = jnp.zeros((length, width), jnp.float32)
    along = jnp.zeros((length, width), jnp.float32)
    for at, out in enumerate(outs):
        block = (me + (ranks - at)) % ranks
        span = pl.ds(pl.multiple_of(block * width, width), width)
        part = jnp.zeros((length, width), jnp.float32)
        for which in range(3):
            part += contract_last(joined_ref[:, width * which : width * (which + 1)], weight_ref[which, span, :])
        out[0:length, :] = part.astype(jnp.bfloat16)
        scaled = part * gain_ref[block]
        plain += scaled
        along += scaled * unit_ref[block].astype(jnp.float32)
    ones = jnp.ones((8, width), jnp.bfloat16)
    sums = [contract_last(ones, value.astype(jnp.bfloat16))[0:1] for value in (plain, along)]
    spans = length // width
    tail = [value[:, width * span : width * (span + 1)] for value in sums for span in range(spans)]
    tail = jnp.concatenate(tail + [jnp.zeros((16 - 2 * spans, width), jnp.float32)] * (2 * spans < 16), axis=0)
    for out in outs:
        out[length:, :] = tail.astype(jnp.bfloat16)
        out.start()
    add_pairs(pairs, sums_out)


def attention_back(me, qkv, probs, unit, gain, weight, pieces, pairs=()):
    ranks, length, width = unit.shape
    heads = width // HD
    flops = 2 * length * (3 * ranks * width * width + 5 * length * width)
    return held_call(
        functools.partial(attention_back_kernel, ranks, len(pairs)),
        (
            jax.ShapeDtypeStruct((length, 3 * width), jnp.bfloat16),
            jax.ShapeDtypeStruct((2, width), jnp.float32),
        )
        + tuple(jax.ShapeDtypeStruct((length + 16, width), jnp.bfloat16) for _ in range(ranks))
        + tuple(jax.ShapeDtypeStruct(one.shape, one.dtype) for one, _ in pairs),
        (me[None], qkv, probs, unit, gain, weight, *pieces, *(values for pair in pairs for values in pair)),
        [pltpu.VMEM((length, width), jnp.bfloat16)] + [pltpu.VMEM((heads, length, HD), jnp.float32)] * 2,
        PARAMS,
        cost(12),
        scalars=1,
        parts=(2,),
        early=(1, *range(6, 6 + ranks)),
    )


def split_weight_grad_kernel(
    rows_ref, low_ref, grad_ref, seq, side_seq, main_in, side_in, low_seq, low_all, even, odd, turned, final,
):
    batch, packed, wide = rows_ref.shape
    low_width = low_ref.shape[2]
    each = low_width // WP
    group = wide // WP
    count = side_in.shape[1] // RB
    ends = (count - 1) // 2
    main_rows = packed - 2 * ends
    blocks = main_rows // RB
    taps = WP * (count - 1)

    rows_ref, low_ref = rows_ref.ready(), low_ref.ready()

    @pl.loop(0, batch)
    def _(row):
        for tile in range(wide // 128):
            lanes = slice(128 * tile, 128 * tile + 128)
            values = rows_ref[row, :, lanes].astype(jnp.float32)
            blank = jnp.zeros((ends, 128), jnp.float32)
            seq[tile] = jnp.concatenate([blank, values[:main_rows], blank], axis=0)
            for end in range(2):
                side_seq[tile, end] = jnp.concatenate(
                    [blank, values[main_rows + ends * end : main_rows + ends * (end + 1)], blank], axis=0
                )
            for block in range(blocks + count - 1):
                main_in[row, RB * block : RB * block + RB, lanes] = seq.at[tile][pl.ds(block, RB, stride=blocks), :].astype(jnp.bfloat16)
            for d in range(count):
                side_in[row, RB * d : RB * d + RB, lanes] = jnp.concatenate(
                    [side_seq[tile, 0, d : d + ends, :], side_seq[tile, 1, d : d + ends, :]], axis=0
                ).astype(jnp.bfloat16)
        for tile in range(low_width // 128):
            lanes = slice(128 * tile, 128 * tile + 128)
            low_seq[tile] = low_ref[row, :, lanes].astype(jnp.float32)
            for block in range(blocks):
                low_all[row, RB * block : RB * block + RB, lanes] = low_seq.at[tile][pl.ds(block, RB, stride=blocks), :].astype(jnp.bfloat16)
            low_all[row, main_rows:packed, lanes] = low_ref[row, main_rows:packed, lanes]

    left = jnp.concatenate([low_all[row] for row in range(batch)], axis=0).T
    even[...] = jnp.zeros(even.shape, jnp.float32)
    odd[...] = jnp.zeros(odd.shape, jnp.float32)

    for d in range(count):
        at = RB * d
        right = jnp.concatenate(
            [
                part
                for row in range(batch)
                for part in (main_in[row, pl.ds(at, main_rows), :], side_in[row, pl.ds(at, RB), :])
            ],
            axis=0,
        )
        part = jnp.dot(left, right, preferred_element_type=jnp.float32)
        for phase in range(WP):
            held = even if phase % 2 == 0 else odd
            lanes = pl.ds(wide * d + wide - group * (phase - phase % 2), wide)
            held[:, lanes] += part[each * phase : each * (phase + 1), :]

    left_lanes = lax.broadcasted_iota(jnp.int32, (each, 128), 1) < group
    for tile in range(taps * group // 128):
        at = wide + 128 * tile
        near, far = odd[:, at : at + 128], odd[:, at + 128 : at + 256]
        value = even[:, at : at + 128] + jnp.where(left_lanes, pltpu.roll(near, group, 1), pltpu.roll(far, group, 1))
        turned[128 * tile : 128 * tile + 128, 0:each] = value.T

    for channel in range(group):
        final[pl.ds(channel, each, stride=group), :] = turned[pl.ds(channel, taps, stride=group), :].T[0:each, :]

    grad_ref[...] = final[...].astype(grad_ref.dtype)


def split_weight_grad(rows, low, group, width):
    batch, packed, wide = rows.shape
    each = low.shape[2] // WP
    count = width // WP + 1
    ends = (count - 1) // 2
    main_rows = packed - 2 * ends
    blocks = main_rows // RB
    flops = 2 * batch * packed * low.shape[2] * wide * count
    (out,) = held_call(
        split_weight_grad_kernel,
        (jax.ShapeDtypeStruct((each * group, width), jnp.bfloat16),),
        (rows, low),
        [
            pltpu.VMEM((wide // 128, main_rows + 2 * ends, 128), jnp.float32),
            pltpu.VMEM((wide // 128, 2, 3 * ends, 128), jnp.float32),
            pltpu.VMEM((batch, RB * (blocks + count - 1), wide), jnp.bfloat16),
            pltpu.VMEM((batch, RB * count, wide), jnp.bfloat16),
            pltpu.VMEM((low.shape[2] // 128, packed, 128), jnp.float32),
            pltpu.VMEM((batch, packed, low.shape[2]), jnp.bfloat16),
            pltpu.VMEM((each, wide * (count + 1)), jnp.float32),
            pltpu.VMEM((each, wide * (count + 1)), jnp.float32),
            pltpu.VMEM((width * group, 128), jnp.float32),
            pltpu.VMEM((each * group, width), jnp.float32),
        ],
        SOME,
        cost(8),
        far=False,
    )
    return out


def centered(values):
    center = values - jnp.mean(values, axis=1, keepdims=True)
    scale = lax.rsqrt(jnp.mean(center * center, axis=1, keepdims=True) + EPS)
    return center * scale, scale


def norm_pull(grad, unit, scale, gain):
    scaled = grad * gain
    inner = scaled - jnp.mean(scaled, axis=1, keepdims=True) - unit * jnp.mean(scaled * unit, axis=1, keepdims=True)
    return inner * scale, jnp.sum(grad * unit, axis=0, keepdims=True), jnp.sum(grad, axis=0, keepdims=True)


def weight_rows(weight_ref, turn, block, width):
    down = width // weight_ref.shape[2]
    across = weight_ref.shape[0] // down
    return jnp.concatenate(
        [
            jnp.concatenate([weight_ref[(down * column + at) ^ turn, block] for at in range(down)], axis=0)
            for column in range(across)
        ],
        axis=1,
    )


def attention_sum_kernel(ranks, me_ref, weight_ref, here_ref, bias_ref, gain_ref, shift_ref, *refs):
    pieces, (sum_ref, normed_ref, unit_ref, scale_ref) = refs[:ranks], refs[ranks:]
    width = pieces[0].shape[1]
    total = here_ref[...].astype(jnp.float32) + bias_ref[...]
    for at, piece in enumerate(pieces):
        block = (me_ref[0] + at) % ranks
        rows = weight_rows(weight_ref, me_ref[1], block, width)
        total = total + jnp.dot(piece[...], rows, preferred_element_type=jnp.float32)
    unit, scale = centered(total)
    sum_ref[...] = total
    normed_ref[...] = (unit * gain_ref[...] + shift_ref[...]).astype(jnp.bfloat16)
    unit_ref[...] = unit
    scale_ref[...] = scale


def attention_sum(me, weight, here, bias, gain, shift, pieces):
    frames, model = here.shape
    ranks = len(pieces)
    return held_call(
        functools.partial(attention_sum_kernel, ranks),
        (
            jax.ShapeDtypeStruct((frames, model), jnp.float32),
            jax.ShapeDtypeStruct((frames, model), jnp.bfloat16),
            jax.ShapeDtypeStruct((frames, model), jnp.float32),
            jax.ShapeDtypeStruct((frames, 1), jnp.float32),
        ),
        (me, weight, here, bias, gain, shift, *pieces),
        [],
        FEW,
        cost(1.3),
        scalars=1,
        far=False,
    )


def head_kernel(
    ranks, second_ref, bias_ref, gain_ref, shift_ref, weight_ref, letter_ref, cot_ref, *refs
):
    pieces = refs[:ranks]
    logits_ref, third_ref, low_ref, weight_grad_ref, letter_grad_ref, norm_ref = refs[ranks:]
    total = second_ref[...] + bias_ref[...]
    for piece in pieces:
        total = total + piece[...].astype(jnp.float32)
    unit, scale = centered(total)
    final = (unit * gain_ref[...] + shift_ref[...]).astype(jnp.bfloat16)
    cot = cot_ref[...]
    logits_ref[...] = jnp.dot(final, weight_ref[...], preferred_element_type=jnp.float32) + letter_ref[...]
    weight_grad_ref[...] = contract_first(cot, final)
    letter_grad_ref[...] = jnp.sum(cot.astype(jnp.float32), axis=0, keepdims=True)
    third, norm_ref[0:1], norm_ref[1:2] = norm_pull(contract_last(cot, weight_ref[...]), unit, scale, gain_ref[...])
    third_ref[...] = third
    low_ref[...] = third.astype(jnp.bfloat16)


def head(second, bias, gain, shift, weight, letter_bias, cotangent, pieces):
    frames, model = second.shape
    letters = weight.shape[1]
    return held_call(
        functools.partial(head_kernel, len(pieces)),
        (
            jax.ShapeDtypeStruct((frames, letters), jnp.float32),
            jax.ShapeDtypeStruct((frames, model), jnp.float32),
            jax.ShapeDtypeStruct((frames, model), jnp.bfloat16),
            jax.ShapeDtypeStruct((letters, model), jnp.float32),
            jax.ShapeDtypeStruct((1, letters), jnp.float32),
            jax.ShapeDtypeStruct((2, model), jnp.float32),
        ),
        (second, bias, gain, shift, weight, letter_bias, cotangent, *pieces),
        [],
        FEW,
        cost(1.9),
        far=False,
    )


def second_back_kernel(
    ranks, me_ref, weight_ref, third_ref, unit_ref, scale_ref, gain_ref, letters_ref, bias_ref, final_ref, *refs
):
    pieces, (low_ref,) = refs[:ranks], refs[ranks : ranks + 1]
    mixed, seconds = refs[ranks + 1 : 2 * ranks + 1], refs[2 * ranks + 1]
    frames, width = mixed[0].shape
    total = pieces[0][...].astype(jnp.float32)
    for piece in pieces[1:]:
        total = total + piece[...].astype(jnp.float32)
    grad, gain_grad, shift_grad = norm_pull(total, unit_ref[...], scale_ref[...], gain_ref[...])
    low = (third_ref[...] + grad).astype(jnp.bfloat16)
    low_ref[...] = low
    low_ref.start()
    letters = letters_ref.shape[0]
    spare = seconds.shape[1] - frames - letters - 5
    small = jnp.concatenate([letters_ref[...], gain_grad, shift_grad, final_ref[...]], axis=0)
    last = jnp.concatenate([bias_ref[...], jnp.zeros((1, width - letters), jnp.float32)], axis=1)
    for block in range(ranks):
        lanes = slice(width * block, width * (block + 1))
        rows = [small[:, lanes], last, jnp.zeros((spare, width), jnp.float32)]
        seconds[block, 0:frames, :] = low[:, lanes]
        seconds[block, frames:, :] = jnp.concatenate(rows, axis=0).astype(jnp.bfloat16)
    for at in range(ranks):
        block = (me_ref[0] + (ranks - at)) % ranks
        mixed[at][...] = contract_last(low, weight_rows(weight_ref, me_ref[1], block, width)).astype(jnp.bfloat16)
        mixed[at].start()


def second_back(me, weight, third, unit, scale, gain, letters_grad, bias_grad, final_grads, pieces):
    frames, model = third.shape
    ranks = len(pieces)
    rows = frames + (letters_grad.shape[0] + 5 + 15) // 16 * 16
    result = held_call(
        functools.partial(second_back_kernel, ranks),
        (jax.ShapeDtypeStruct((frames, model), jnp.bfloat16),)
        + tuple(jax.ShapeDtypeStruct((frames, model // ranks), jnp.bfloat16) for _ in range(ranks))
        + (jax.ShapeDtypeStruct((ranks, rows, model // ranks), jnp.bfloat16),),
        (me, weight, third, unit, scale, gain, letters_grad, bias_grad, final_grads, *pieces),
        [],
        PARAMS,
        cost(8),
        scalars=1,
        early=range(10, 10 + ranks),
    )
    return result[0], result[1 : 1 + ranks], result[1 + ranks]


def ffn_grad_kernel(count, me_ref, *refs):
    groups = [refs[count * at : count * (at + 1)] for at in range(4)]
    keep_refs, give_refs, sums = refs[4 * count : 4 * count + 2], refs[4 * count + 2 : 4 * count + 4], refs[4 * count + 4 :]
    core = me_ref[0] % 2
    for which in range(2):
        left = jnp.concatenate([ref[...] for ref in groups[2 * which]], axis=0)
        right = jnp.concatenate([ref[...] for ref in groups[2 * which + 1]], axis=0)
        sums[which][...] = jnp.sum(right.astype(jnp.float32), axis=0, keepdims=True)
        rows = 256
        for at in range(0, left.shape[1], rows):
            block = contract_first(left[:, at : at + rows], right).astype(jnp.bfloat16)
            part, down = divmod(at, keep_refs[0].shape[0])

            @pl.when(core == which)
            def _():
                keep_refs[part][down : down + rows, :] = block

            @pl.when(core != which)
            def _():
                give_refs[part][down : down + rows, :] = block


def ffn_grads(row, lefts, rights):
    count = len(lefts[0])
    rows, columns = lefts[0][0].shape[1], rights[0][0].shape[1]
    frames = lefts[0][0].shape[0]
    return held_call(
        functools.partial(ffn_grad_kernel, count),
        tuple(jax.ShapeDtypeStruct((rows // 2, columns), jnp.bfloat16) for _ in range(4))
        + tuple(jax.ShapeDtypeStruct((1, columns), jnp.float32) for _ in range(2)),
        (row[None], *lefts[0], *rights[0], *lefts[1], *rights[1]),
        [],
        PARAMS,
        cost(9.8),
        scalars=1,
    )


def out_grad_kernel(ranks, me_ref, mixed_ref, *refs):
    pieces, (out_ref, sum_ref) = refs[:ranks], refs[ranks:]
    width = mixed_ref.shape[1]
    frames = pieces[0].shape[0]
    mixed_ref = mixed_ref.ready()
    left, right = [], []
    for at, piece in enumerate(pieces):
        block = (me_ref[0] + (ranks - at)) % ranks
        left.append(mixed_ref[pl.ds(pl.multiple_of(block * frames, frames), frames), :])
        right.append(piece[...])
    left, right = jnp.concatenate(left, axis=0), jnp.concatenate(right, axis=0)
    sum_ref[...] = jnp.sum(right.astype(jnp.float32), axis=0, keepdims=True)
    for block in range(ranks):
        lanes = slice(width * block, width * (block + 1))
        out_ref[block] = contract_first(left, right[:, lanes]).astype(out_ref.dtype)


def out_grads(me, mixed, pieces):
    length, width = mixed.shape
    model = pieces[0].shape[1]
    return held_call(
        functools.partial(out_grad_kernel, len(pieces)),
        (
            jax.ShapeDtypeStruct((model // width, width, width), jnp.bfloat16),
            jax.ShapeDtypeStruct((1, model), jnp.float32),
        ),
        (me[None], mixed, *pieces),
        [],
        PARAMS,
        cost(3.1),
        scalars=1,
    )


def unite_blocks(blocks, me, outs, emit):
    count = len(blocks)
    rows, columns = blocks[0].shape

    def kernel(turn_ref, *refs):
        given, rest = refs[:count], refs[count:]
        out_refs, (held, semaphores) = rest[: len(outs)], rest[len(outs) :]
        step = pl.program_id(0)
        copies = [pltpu.make_async_copy(given[at], held.at[at], semaphores.at[at]) for at in range(count)]

        @pl.when(step == 0)
        def _():
            for copy in copies:
                copy.start()

        for at in range(count):

            @pl.when((step ^ turn_ref[0]) == at)
            def _():
                copies[at].wait()

        emit(step, held[step ^ turn_ref[0]].astype(jnp.float32), out_refs)

    return pl.pallas_call(
        kernel,
        out_shape=tuple(shape for shape, _, _ in outs),
        grid_spec=pltpu.PrefetchScalarGridSpec(
            num_scalar_prefetch=1,
            grid=(count,),
            in_specs=[pl.BlockSpec(memory_space=pltpu.HBM)] * count,
            out_specs=tuple(pl.BlockSpec(block, index) for _, block, index in outs),
            scratch_shapes=[pltpu.VMEM((count, rows, columns), blocks[0].dtype), pltpu.SemaphoreType.DMA((count,))],
        ),
        compiler_params=SOME,
        cost_estimate=cost(5),
    )(me[None], *blocks)


def unite_one(blocks, me):
    rows, columns = blocks[0].shape

    def emit(step, value, outs):
        outs[0][...] = value

    shape = jax.ShapeDtypeStruct((len(blocks) * rows, columns), jnp.float32)
    return unite_blocks(blocks, me, [(shape, (rows, columns), lambda at, turn: (at, 0))], emit)[0]


def paired(block, step):
    return lax.ppermute(block, "dp", [(at, at ^ step) for at in range(lax.axis_size("dp"))])


def add_low(mine, other):
    return low(wide(mine) + wide(other))


def cross_first(values):
    half = values.shape[0] // 32 * 16
    return add_low(values[:half], paired(values[:half], 2)), add_low(values[half:], paired(values[half:], 4))


def cross_second(upper, lower):
    return jnp.concatenate([add_low(upper, paired(upper, 4)), add_low(lower, paired(lower, 2))])


def core_halves(values, row):
    half = values.shape[0] // 2
    core = row % 2
    return tuple(lax.dynamic_slice_in_dim(values, side * half, half) for side in (core, 1 - core))


def core_join(values, row):
    other = paired(values, 1)
    return jnp.where(row % 2 == 0, values, other), jnp.where(row % 2 == 0, other, values)


def gather_eight(block, meanwhile=()):
    half = block.shape[0] // 32 * 16
    (two, four), meanwhile = lax.optimization_barrier(((paired(block, 2), paired(block, 4)), meanwhile))
    six = jnp.concatenate([paired(four[:half], 2), paired(two[half:], 4)])
    one = paired(after(block, two), 1)
    return [block, one, two, paired(two, 1), four, paired(four, 1), six, paired(six, 1)], meanwhile


def low(values):
    return values.astype(jnp.bfloat16)


def wide(values):
    return values.astype(jnp.float32)


def shifted(block, step):
    count = lax.axis_size("sp")
    return lax.ppermute(block, "sp", [(at, (at + step) % count) for at in range(count)])


def gather_pieces(block):
    return [block] + [shifted(block, step) for step in range(1, lax.axis_size("sp"))]


def return_pieces(pieces):
    return [pieces[0]] + [shifted(pieces[step], -step) for step in range(1, lax.axis_size("sp"))]


def sum_pieces(pieces):
    total = wide(pieces[0])
    for step in range(1, lax.axis_size("sp")):
        total = total + wide(shifted(low(pieces[step]), -step))
    return total


def weight_grad_kernel(me_ref, left_ref, right_ref, keep_ref, give_ref):
    count, rows, width = keep_ref.shape
    core = me_ref[0] % 2
    left_ref, right_ref = left_ref.ready(), right_ref.ready()
    for out_ref, side in ((give_ref, 1 - core), (keep_ref, core)):
        left = left_ref[:, pl.ds(pl.multiple_of(rows * side, rows), rows)]
        for at in range(count):
            out_ref[at] = contract_first(left, right_ref[:, width * at : width * (at + 1)]).astype(out_ref.dtype)
        out_ref.start()


def weight_grad(row, left, right, parts):
    width = right.shape[1] // parts
    return held_call(
        weight_grad_kernel,
        tuple(jax.ShapeDtypeStruct((parts, left.shape[1] // 2, width), jnp.bfloat16) for _ in range(2)),
        (row[None], left, right),
        [],
        PARAMS,
        cost(3),
        scalars=1,
    )


def after(values, *others):
    return lax.optimization_barrier((values, others))[0]


def shards(
    features,
    logit_grad,
    segment_ids,
    conv_weight,
    conv_bias,
    w_qkv,
    qv_bias,
    w_out,
    w_up,
    ffn_bias,
    w_down,
    out_biases,
    gains,
    shifts,
    ctc_weight,
    ctc_bias,
):
    ranks = lax.axis_size("sp")
    me = lax.axis_index("sp")
    signal = features[0]
    frames, model_width = signal.shape
    segments = segment_ids[0]
    length = segments.shape[0]
    local_width = model_width // ranks
    kernel_width = conv_weight.shape[2]
    group_size = conv_weight.shape[1]
    seg_col, seg_row = segments[:, None], segments[None, :]
    rows_count = lax.axis_size("dp")
    row = lax.axis_index("dp")
    part_width = local_width // rows_count
    split_rows = rows_count == 8 and part_width % 16 == 0 and group_size % part_width == 0
    owners = [(me - step) % ranks for step in range(ranks)]
    taps = tap_rows(conv_weight)
    w_three = w_qkv.transpose(1, 0, 2)
    gain_blocks = gains[0].reshape(ranks, 1, local_width)
    down = local_width // frames
    slices = split_rows and local_width % frames == 0 and down * ranks == rows_count
    signal_blocks = signal.reshape(frames, ranks, local_width).transpose(1, 0, 2)
    if slices:
        share = lax.dynamic_slice(
            w_out, ((row % down) * frames, (row // down) * local_width), (frames, local_width)
        )
        share = jnp.broadcast_to(share[None], signal_blocks.shape)
        signal_blocks = jnp.concatenate([signal_blocks, share], axis=1)
    given = lax.all_to_all(signal_blocks, "sp", 0, 0)
    turn = row if slices else jnp.zeros_like(row)
    places = jnp.stack([me, turn])
    first_low, conv_slope, wide_rows = conv_forward(
        given, frames, seg_col, taps, conv_bias[None], group_size, kernel_width, rows_count if split_rows else local_width // group_size
    )
    first_pieces = gather_pieces(first_low)
    if slices:
        w_parts = jnp.stack(gather_eight(after(given[:, frames:].reshape(-1, local_width), first_low))[0])
        w_parts = w_parts.reshape(rows_count, ranks, frames, local_width)
        first_pieces[2] = after(first_pieces[2], w_parts)
    else:
        w_parts = lax.all_gather(w_out, "sp", axis=0)[None]
    mixed_heads, qkv, probs_low, normed_full, unit_one, scale_one, first_here, *mixed_parts = attention(
        me, gains[0:1], shifts[0:1], w_three, qv_bias, seg_col, seg_row, first_pieces, frames
    )
    mixed_parts = return_pieces(mixed_parts)
    second_sum, normed_two, unit_two, scale_two = attention_sum(
        places, w_parts, first_here, out_biases[0:1], gains[1:2], shifts[1:2], mixed_parts
    )
    ffn_pieces = gather_pieces(normed_two)
    if split_rows:
        wide_all = lax.all_to_all(after(wide_rows, normed_two), "dp", 0, 0)
        ffn_pieces[2] = after(ffn_pieces[2], wide_all)
    active_pieces, gelu_slopes, down_parts = [], [], []
    for piece in ffn_pieces:
        if down_parts:
            piece = after(piece, down_parts[-1])
        hidden = jnp.dot(piece, w_up, preferred_element_type=jnp.float32) + ffn_bias
        share = 0.5 * (1.0 + lax.erf(hidden * (0.5**0.5)))
        gelu_slopes.append(share + hidden * jnp.exp(-0.5 * hidden * hidden) * 0.3989422804014327)
        active_pieces.append(low(hidden * share))
        down_parts.append(low(jnp.dot(active_pieces[-1], w_down, preferred_element_type=jnp.float32)))
    logits, third_grad, down_cot, ctc_weight_grad, ctc_bias_grad, final_norm_grads = head(
        second_sum, out_biases[1:2], gains[2:3], shifts[2:3], ctc_weight, ctc_bias[None], logit_grad[0], return_pieces(down_parts)
    )
    down_pieces = gather_pieces(down_cot)
    hidden_pieces, up_parts = [], []
    for piece, slope in zip(down_pieces, gelu_slopes):
        if up_parts:
            piece = after(piece, up_parts[-1])
        hidden_pieces.append(low(contract_last(piece, w_down) * slope))
        up_parts.append(low(contract_last(hidden_pieces[-1], w_up)))
    up_back = return_pieces(up_parts)
    if slices:
        active_pieces, ffn_pieces, down_pieces, hidden_pieces = after(
            (active_pieces, ffn_pieces, down_pieces, hidden_pieces), up_back[1]
        )
        *ffn_halves, down_bias_grad, ffn_bias_grad = ffn_grads(
            row, (active_pieces, ffn_pieces), (down_pieces, hidden_pieces)
        )
        up_back[2] = after(up_back[2], ffn_halves[0])
        ffn_pairs = [(keep, paired(give, 1)) for keep, give in zip(ffn_halves[:2], ffn_halves[2:])]
    else:
        down_full, hidden_full = jnp.concatenate(down_pieces), jnp.concatenate(hidden_pieces)
        down_grad = contract_first(jnp.concatenate(active_pieces), down_full)
        up_grad = contract_first(jnp.concatenate(ffn_pieces), hidden_full)
        ffn_bias_grad = jnp.sum(wide(hidden_full), axis=0)
        down_bias_grad = jnp.sum(wide(down_full), axis=0)
        up_sum, down_sum = (wide(total) for total in lax.psum((low(up_grad), low(down_grad)), "dp"))

    out_cot, mixed_back, second_blocks = second_back(
        places, w_parts, third_grad, unit_two, scale_two, gains[1:2], ctc_weight_grad, ctc_bias_grad, final_norm_grads, up_back
    )
    mixed_pieces = return_pieces(mixed_back)
    joined_grad, qv_bias_grad, *norm_blocks = attention_back(
        me, qkv, probs_low, unit_one, gain_blocks, w_three, mixed_pieces, ffn_pairs if slices else ()
    )
    norm_blocks, ffn_halves = norm_blocks[:ranks], norm_blocks[ranks:]
    norm_blocks = return_pieces(norm_blocks)
    second_groups = lax.all_to_all(after(second_blocks, norm_blocks[1]), "sp", 0, 0)
    if slices:
        ffn_halves = [add_low(half, paired(half, step)) for half, step in zip(ffn_halves, (2, 4))]
        norm_blocks[1] = after(norm_blocks[1], ffn_halves)
    first_grad, conv_low, rank_sums, low_parts, channel_sums = norm_back(
        me, unit_one, scale_one, gain_blocks, conv_slope, seg_col, norm_blocks, second_groups,
        kernel_width, group_size, rows_count if split_rows else 0,
    )
    signal_groups, *_ = conv_input_grad(conv_low, seg_col, taps, first_grad, group_size, kernel_width)
    out_pieces = gather_pieces(after(out_cot, first_grad))
    if slices:
        joined_grad = after(joined_grad, first_grad)
        qkv_keep, qkv_give = (half.reshape(-1, local_width) for half in weight_grad(row, normed_full, joined_grad, 3))
        qkv_half = add_low(qkv_keep, paired(qkv_give, 1))
        ffn_half = cross_second(*ffn_halves)
        low_rows = after(lax.all_to_all(low_parts, "dp", 0, 0), signal_groups, qkv_half, ffn_half, out_pieces)
        qkv_cross = cross_first(qkv_half)
        conv_part = split_weight_grad(wide_all, low_rows, group_size, kernel_width)
        conv_blocks, qkv_cross = gather_eight(conv_part, qkv_cross)
        out_pieces = after(out_pieces, conv_part)
    else:
        grouped = given[:, :frames].reshape(length, local_width)
        conv_weight_grad = kernel_weight_grad(grouped, conv_low, seg_col, group_size, kernel_width)
    out_low, out_bias_grad = out_grads(me, mixed_heads, out_pieces)
    small_parts = [rank_sums, channel_sums, qv_bias_grad]
    small_parts += [values.reshape(-1, local_width) for values in (ffn_bias_grad, out_bias_grad, down_bias_grad)]
    small = jnp.concatenate(small_parts)
    few = -(-small.shape[0] // 64) * 64
    small = low(jnp.pad(small, ((0, few - small.shape[0]), (0, 0))))
    if slices:
        out_rows = jnp.concatenate([out_low.reshape(-1, local_width), small])
        down_sum, up_sum = (wide(total) for total in core_join(ffn_half, row))
        out_rows, down_sum, up_sum = after((out_rows, down_sum, up_sum), conv_blocks[2])
        out_half = add_low(*(lambda keep, give: (keep, paired(give, 1)))(*core_halves(out_rows, row)))
        out_cross = cross_first(out_half)
        conv_blocks = after(conv_blocks, out_cross)
        out_half = cross_second(*out_cross)
        conv_sum = unite_one(conv_blocks, row).reshape(local_width, group_size, kernel_width)
        qkv_half, conv_sum = lax.optimization_barrier((cross_second(*qkv_cross), conv_sum))
        qkv_sum = [half.reshape(3, 1, -1, local_width) for half in core_join(qkv_half, row)]
        qkv_sum = wide(jnp.concatenate(qkv_sum, axis=1)).reshape(3, model_width, local_width)
        out_rows = wide(jnp.concatenate(core_join(out_half, row)))
        out_sum = out_rows[:model_width].reshape(ranks, local_width, local_width)
        small = out_rows[model_width:]
        signal_groups = after(signal_groups, conv_part)
    else:
        qkv_low = contract_first(normed_full, joined_grad).reshape(model_width, 3, local_width).transpose(1, 0, 2)
        conv_sum, qkv_sum, out_sum, small = (
            wide(total) for total in lax.psum((conv_weight_grad, low(qkv_low), out_low, small), "dp")
        )
    out_sum = out_sum.transpose(1, 0, 2).reshape(local_width, model_width)
    feature_grad = wide(lax.all_to_all(signal_groups, "sp", split_axis=0, concat_axis=1, tiled=True))

    cuts, at = [], 0
    for part in small_parts:
        cuts.append(small[at : at + part.shape[0]])
        at += part.shape[0]
    letters = ctc_weight.shape[1]
    few_letters = letters // ranks
    rank_sums, channel_sums, qv_sum, ffn_bias_sum, out_bias_sum, down_bias_sum = cuts
    norm_sums = rank_sums[letters : letters + 4]
    return (
        logits[None],
        feature_grad[None],
        conv_sum,
        channel_sums[0],
        qkv_sum.transpose(1, 0, 2),
        qv_sum,
        out_sum,
        up_sum,
        ffn_bias_sum.reshape(-1),
        down_sum,
        jnp.stack([out_bias_sum.reshape(-1), down_bias_sum.reshape(-1)]),
        jnp.stack([channel_sums[1], norm_sums[0], norm_sums[2]]),
        jnp.stack([channel_sums[2], norm_sums[1], norm_sums[3]]),
        rank_sums[:letters].T,
        lax.dynamic_slice_in_dim(rank_sums[letters + 4, :letters], me * few_letters, few_letters),
    )


def solution(mesh):
    in_specs = (
        P("dp", "sp", None),
        P("dp", "sp", None),
        P("dp", None),
        P("sp", None, None),
        P("sp"),
        P(None, None, "sp"),
        P(None, "sp"),
        P("sp", None),
        P(None, "sp"),
        P("sp"),
        P("sp", None),
        P(),
        P(),
        P(),
        P(),
        P(),
    )
    out_specs = (
        P("dp", "sp", None),
        P("dp", "sp", None),
        P("sp", None, None),
        P("sp"),
        P(None, None, "sp"),
        P(None, "sp"),
        P("sp", None),
        P(None, "sp"),
        P("sp"),
        P("sp", None),
        P(),
        P(None, "sp"),
        P(None, "sp"),
        P("sp", None),
        P("sp"),
    )
    return jax.shard_map(shards, mesh=mesh, in_specs=in_specs, out_specs=out_specs, check_vma=False)
```
